32 devices in a mesh: ctx: 8 (over z, core), mp: 4 (over y, x).
Axes of the slice: x: 2, y: 2, z: 4, core: 2. Of those that a mesh axis runs over, the one named last changes fastest.
Arguments:
- grad_out: bfloat16 [4096, 4096], P('ctx', 'mp'), may hold values from -6 to 6
- proj_out: bfloat16 [4096, 4096], P('mp', 'ctx'), may hold values from -0.09375 to 0.09375
- query: bfloat16 [4096, 4096], P('ctx', 'mp'), may hold values from -6 to 6
- key_in: bfloat16 [4096, 4096], P('ctx', 'mp'), may hold values from -6 to 6
- value_in: bfloat16 [4096, 4096], P('ctx', 'mp'), may hold values from -6 to 6
- filters: float32 [4096, 4096], P(('mp', 'ctx')), may hold values from -0.09375 to 0.09375
Outputs:
- grad_query: bfloat16 [4096, 4096], P('ctx', 'mp')
- grad_key: bfloat16 [4096, 4096], P('ctx', 'mp')
- grad_value: bfloat16 [4096, 4096], P('ctx', 'mp')
- filter_grad: float32 [4096, 4096], P(('mp', 'ctx'))
The draws below stay inside these ranges and needn't reach their ends.
All inputs are finite; a program needn't handle non-finite values.
Results may differ from the reference program's by a relative error of at most 0.013.
Values may be sent and summed in bfloat16 or wider, within the bound.
No kernel may reach another device: no remote copies, remote signals or barrier semaphores. Data moves between devices by JAX's collectives and lax.ppermute only.
A program may use at most 128 MiB of HBM per device.

```python
import math
import jax
import jax.numpy as jnp
from jax import lax

D = 4096
SEQ = 4096


def block_levels(stream_key, dims, cuts, smallest, largest):
    factor_of, own = 1.0, jax.random.fold_in(stream_key, 6)
    for dim, shards_of in cuts:
        heights = jnp.exp(jax.random.uniform(jax.random.fold_in(own, dim), (shards_of,), jnp.float32, smallest / len(cuts), largest / len(cuts)))
        factor_of = factor_of * jnp.repeat(heights, dims[dim] // shards_of).reshape([-1 if axis == dim else 1 for axis in range(len(dims))])
    return factor_of


def normal_values(key, dims, deviation, most, pieces=(), kind=jnp.bfloat16):
    factor_of = block_levels(key, dims, pieces, -0.22, 0.18) if pieces else 1.0
    drawn = jax.random.normal(key, dims, jnp.float32) * deviation * factor_of
    return jnp.minimum(jnp.maximum(drawn, -most), most).astype(kind)


def setup_inputs(seed: int = 0) -> dict:
    key_list = jax.random.split(jax.random.key(seed), 7)
    return {
        "grad_out": normal_values(key_list[0], (SEQ, D), 1.0, 6.0, ((0, 8), (1, 4))),
        "proj_out": normal_values(key_list[1], (D, D), D ** -0.5, 0.09375, ((0, 4), (1, 8))),
        "query": normal_values(key_list[2], (SEQ, D), 1.0, 6.0, ((0, 8), (1, 4))),
        "key_in": normal_values(key_list[3], (SEQ, D), 1.0, 6.0, ((0, 8), (1, 4))),
        "value_in": normal_values(key_list[4], (SEQ, D), 1.0, 6.0, ((0, 8), (1, 4))),
        "filters": normal_values(key_list[5], (D, SEQ), SEQ ** -0.5, 0.09375, ((0, 32),), jnp.float32),
    }


def channel_block(blocks):
    gated, scaled, kernel = blocks
    length_all = 2 * SEQ
    gated_spec = jnp.fft.rfft(gated, n=length_all, axis=1)
    scaled_spec = jnp.fft.rfft(scaled, n=length_all, axis=1)
    kernel_spec = jnp.fft.rfft(kernel, n=length_all, axis=1)
    conv_out = jnp.fft.irfft(kernel_spec * gated_spec, n=length_all, axis=1)[:, :SEQ]
    grad_gated = jnp.fft.irfft(scaled_spec * jnp.conj(kernel_spec), n=length_all, axis=1)[:, :SEQ]
    grad_kernel = jnp.fft.irfft(scaled_spec * jnp.conj(gated_spec), n=length_all, axis=1)[:, :SEQ]
    return (conv_out, grad_gated, grad_kernel)

def reference(grad_out, proj_out, query, key_in, value_in, filters):
    grad_mix = jnp.dot(grad_out, proj_out.T, preferred_element_type=jnp.float32).astype(jnp.bfloat16)
    gated = (key_in.astype(jnp.float32) * value_in.astype(jnp.float32)).astype(jnp.bfloat16)
    scaled = (grad_mix.astype(jnp.float32) * query.astype(jnp.float32)).astype(jnp.bfloat16)
    width_block = min(256, D)

    def to_blocks(values):
        return values.astype(jnp.float32).T.reshape(D // width_block, width_block, SEQ)
    kernels = filters.astype(jnp.float32).reshape(D // width_block, width_block, SEQ)
    conv_out, grad_gated, grad_kernel = lax.map(channel_block, (to_blocks(gated), to_blocks(scaled), kernels))
    conv_out = conv_out.reshape(D, SEQ).T.astype(jnp.bfloat16)
    grad_gated = grad_gated.reshape(D, SEQ).T.astype(jnp.bfloat16)
    filter_grad = (grad_kernel.reshape(D, SEQ) / math.sqrt(SEQ)).astype(jnp.float32)
    grad_query = (grad_mix.astype(jnp.float32) * conv_out.astype(jnp.float32)).astype(jnp.bfloat16)
    grad_key = (grad_gated.astype(jnp.float32) * value_in.astype(jnp.float32)).astype(jnp.bfloat16)
    grad_value = (grad_gated.astype(jnp.float32) * key_in.astype(jnp.float32)).astype(jnp.bfloat16)
    return (grad_query, grad_key, grad_value, filter_grad)
```

```python
import functools
import math

import jax
import jax.numpy as jnp
import ml_dtypes
import numpy as np
from jax import lax
from jax.experimental import pallas as pl
from jax.experimental.pallas import tpu as pltpu
from jax.sharding import PartitionSpec as P

def phase_table(rows_n, cols_n, modulus):
    prod_idx = (
        jnp.arange(rows_n, dtype=jnp.int32)[:, None]
        * jnp.arange(cols_n, dtype=jnp.int32)[None, :]
        % modulus
    )
    angles = prod_idx.astype(jnp.float32) * (2.0 * math.pi / modulus)
    return (jnp.cos(angles), jnp.sin(angles))


def make_tables(length_all):
    size_second = min(128, length_all)
    size_first = length_all // size_second
    cos_first, sin_first = phase_table(size_first, size_first, size_first)
    twist_cos, twist_sin = phase_table(size_first, size_second, length_all)
    cos_second, sin_second = phase_table(size_second, size_second, size_second)
    return (cos_first, sin_first, twist_cos, twist_sin, cos_second, sin_second)


def contract(form, left, right):
    return jnp.einsum(form, left, right, precision=lax.Precision.HIGHEST)


def forward_real(signal, tables):
    cos_first, sin_first, twist_cos, twist_sin, cos_second, sin_second = tables
    part_re = contract("kn,cnm->ckm", cos_first, signal)
    part_im = -contract("kn,cnm->ckm", sin_first, signal)
    turned_re = part_re * twist_cos + part_im * twist_sin
    turned_im = part_im * twist_cos - part_re * twist_sin
    spec_re = contract("ckm,mj->ckj", turned_re, cos_second) + contract(
        "ckm,mj->ckj", turned_im, sin_second
    )
    spec_im = contract("ckm,mj->ckj", turned_im, cos_second) - contract(
        "ckm,mj->ckj", turned_re, sin_second
    )
    return (spec_re, spec_im)


def inverse_real(spec_re, spec_im, tables):
    cos_first, sin_first, twist_cos, twist_sin, cos_second, sin_second = tables
    back_re = contract("ckj,jm->ckm", spec_re, cos_second) - contract(
        "ckj,jm->ckm", spec_im, sin_second
    )
    back_im = contract("ckj,jm->ckm", spec_re, sin_second) + contract(
        "ckj,jm->ckm", spec_im, cos_second
    )
    twist_re = back_re * twist_cos - back_im * twist_sin
    twist_im = back_re * twist_sin + back_im * twist_cos
    return contract("nk,ckm->cnm", cos_first, twist_re) - contract(
        "nk,ckm->cnm", sin_first, twist_im
    )


def long_filter_grads(gated, scaled, kernel):
    channels, seq_len = kernel.shape
    length_all = 2 * seq_len
    tables = make_tables(length_all)
    spec_shape = (channels, tables[0].shape[0], tables[4].shape[0])

    def padded(values):
        wide = jnp.concatenate(
            [values.astype(jnp.float32), jnp.zeros((channels, seq_len), jnp.float32)], axis=1
        )
        return wide.reshape(spec_shape)

    def restore(spec_re, spec_im):
        return (
            inverse_real(spec_re, spec_im, tables).reshape(channels, length_all)[:, :seq_len]
            / length_all
        )

    gated_re, gated_im = forward_real(padded(gated), tables)
    scaled_re, scaled_im = forward_real(padded(scaled), tables)
    kernel_re, kernel_im = forward_real(padded(kernel), tables)
    conv_out = restore(
        kernel_re * gated_re - kernel_im * gated_im, kernel_re * gated_im + kernel_im * gated_re
    )
    grad_gated = restore(
        scaled_re * kernel_re + scaled_im * kernel_im, scaled_im * kernel_re - scaled_re * kernel_im
    )
    grad_kernel = restore(
        scaled_re * gated_re + scaled_im * gated_im, scaled_im * gated_re - scaled_re * gated_im
    )
    filter_grad = grad_kernel / math.sqrt(seq_len)
    return (conv_out.astype(jnp.bfloat16), grad_gated.astype(jnp.bfloat16), filter_grad)


def product(left, right):
    return (left.astype(jnp.float32) * right.astype(jnp.float32)).astype(jnp.bfloat16)


def general_body(grad_out, proj_out, query, key_in, value_in, filters):
    weight_rows = lax.all_gather(proj_out, "ctx", axis=1, tiled=True)
    grad_mix = lax.dot_general(
        lax.all_gather(grad_out, "mp", axis=1, tiled=True),
        weight_rows,
        (((1,), (1,)), ((), ())),
        preferred_element_type=jnp.float32,
    ).astype(jnp.bfloat16)
    gated = product(key_in, value_in)
    scaled = product(grad_mix, query)
    chan_gated, chan_scaled = (
        lax.all_to_all(gated.T, "ctx", split_axis=0, concat_axis=1, tiled=True),
        lax.all_to_all(scaled.T, "ctx", split_axis=0, concat_axis=1, tiled=True),
    )
    conv_out, grad_gated, filter_grad = long_filter_grads(chan_gated, chan_scaled, filters)
    back_grad, back_conv = (
        lax.all_to_all(grad_gated, "ctx", split_axis=1, concat_axis=0, tiled=True),
        lax.all_to_all(conv_out, "ctx", split_axis=1, concat_axis=0, tiled=True),
    )
    grad_query = product(grad_mix, back_conv.T)
    grad_key = product(back_grad.T, value_in)
    grad_value = product(back_grad.T, key_in)
    return (grad_query, grad_key, grad_value, filter_grad)


FAST = 32
LANES = 128
F32, BF16 = jnp.float32, jnp.bfloat16

def tables(seq):
    size = 2 * seq
    slow = size // FAST
    half = slow // 2
    b = np.arange(half)
    s = np.arange(half)
    ang = 2 * np.pi * ((s[:, None] * b[None, :]) % slow) / slow
    first = np.concatenate([np.cos(ang), -np.sin(ang)], 0)
    first[half] = 1.0 - 2.0 * (b % 2)
    weight = np.full((half,), 2.0); weight[0] = 1.0
    last = np.concatenate([np.cos(ang) * weight[:, None], -np.sin(ang) * weight[:, None]], 0)
    last[half] = 1.0 - 2.0 * (b % 2)
    last = last.T / size
    a = np.arange(FAST)
    kb = np.arange(half + 1)
    k = kb[:, None] + slow * a[None, :]
    th = 2 * np.pi * ((k[:, :, None] * a[None, None, :]) % size) / size
    c, sn = np.cos(th), np.sin(th)
    fwd = np.concatenate([np.concatenate([c, sn], 2), np.concatenate([-sn, c], 2)], 1)
    fwd[0, :, FAST:] = 0.0
    fwd[half, :, FAST:] = np.concatenate([c[half], -sn[half]], 0)
    fwd[half, :, :FAST] = 0.0
    ct, st = c.transpose(0, 2, 1), sn.transpose(0, 2, 1)
    inv = np.concatenate([np.concatenate([ct, -st], 2), np.concatenate([st, ct], 2)], 1)
    inv[0, FAST:] = 0.0
    inv[half, FAST:] = np.concatenate([ct[half], -st[half]], 1)
    inv[half, :FAST] = 0.0
    return [jnp.asarray(t.astype(ml_dtypes.bfloat16)) for t in (first, fwd, inv, last)]

def dot(l, r):
    return jnp.dot(l, r, preferred_element_type=F32)

U1, U2 = 4, 8

def loop(lo, n, unroll, fn):
    def step(i, carry):
        for u in range(unroll):
            fn(lo + i * unroll + u)
        return carry
    lax.fori_loop(0, n // unroll, step, 0)

def spread(signal, first_ref, mid_ref):
    half = first_ref.shape[1]
    def one(a):
        out = dot(first_ref[...], signal(a))
        mid_ref[pl.ds(a, half, stride=2 * FAST), :] = out[:half]
        mid_ref[pl.ds(FAST + a, half, stride=2 * FAST), :] = out[half:]
    loop(0, FAST, U1, one)

def spectrum_row(kb, half, fwd_ref, mid_ref):
    slot = lax.rem(kb, half) if not isinstance(kb, int) else kb % half
    rows = mid_ref[pl.ds(pl.multiple_of(slot * 2 * FAST, 2 * FAST), 2 * FAST), :].astype(BF16)
    return dot(fwd_ref[kb], rows)

def gather(last_ref, mid_ref, emit):
    half = last_ref.shape[0]
    def one(a):
        re = mid_ref[pl.ds(a, half, stride=2 * FAST), :]
        im = mid_ref[pl.ds(FAST + a, half, stride=2 * FAST), :]
        emit(a, dot(last_ref[...], jnp.concatenate([re, im], 0).astype(BF16)))
    loop(0, FAST, U1, one)

def put(mid_ref, slot, value):
    mid_ref[pl.ds(pl.multiple_of(slot * 2 * FAST, 2 * FAST), 2 * FAST), :] = value

def cmul(x, y):
    xr, xi, yr, yi = x[:FAST], x[FAST:], y[:FAST], y[FAST:]
    return jnp.concatenate([xr * yr - xi * yi, xr * yi + xi * yr], 0)

def cmulc(x, y):
    xr, xi, yr, yi = x[:FAST], x[FAST:], y[:FAST], y[FAST:]
    return jnp.concatenate([xr * yr + xi * yi, xi * yr - xr * yi], 0)

def filter_kernel(h_ref, first_ref, fwd_ref, spec_ref, time_ref, mid_ref):
    half = first_ref.shape[1]
    seq = h_ref.shape[1]
    def turn(i):
        cols = pl.ds(pl.multiple_of(i * LANES, LANES), LANES)
        time_ref[cols, :] = h_ref[:, cols].T
    loop(0, seq // LANES, 4, turn)
    spread(lambda a: time_ref[pl.ds(a, half, stride=FAST), :].astype(BF16), first_ref, mid_ref)
    def one(kb):
        spec_ref[kb] = spectrum_row(kb, half, fwd_ref, mid_ref)
    loop(0, half, U2, one)
    one(half)

def pair_kernel(conj, x_ref, h_ref, first_ref, fwd_ref, inv_ref, last_ref, out_ref, spec_ref, mid_ref, back_ref):
    half = first_ref.shape[1]
    n, _, per, _ = x_ref.shape
    mul = cmulc if conj else cmul
    spread(lambda a: x_ref[:, a].reshape(half, LANES), first_ref, mid_ref)
    def row(kb):
        x = spectrum_row(kb, half, fwd_ref, mid_ref)
        spec_ref[kb] = x
        return dot(inv_ref[kb], mul(x, h_ref[kb]).astype(BF16))
    put(back_ref, 0, row(0) + row(half))
    def one(kb):
        put(back_ref, kb, row(kb))
    loop(1, half - 8, U2, one)
    for kb in range(half - 7, half):
        one(kb)
    def emit(a, rows):
        out_ref[:, a] = rows.reshape(n, per, LANES).astype(out_ref.dtype)
    gather(last_ref, back_ref, emit)

def grad_kernel(scale, s_ref, g_ref, inv_ref, last_ref, out_ref, time_ref, back_ref):
    half = last_ref.shape[0]
    seq = out_ref.shape[1]
    def row(kb):
        return dot(inv_ref[kb], cmulc(s_ref[kb], g_ref[kb]).astype(BF16))
    put(back_ref, 0, row(0) + row(half))
    def one(kb):
        put(back_ref, kb, row(kb))
    loop(1, half - 8, U2, one)
    for kb in range(half - 7, half):
        one(kb)
    def emit(a, rows):
        time_ref[pl.ds(a, half, stride=FAST), :] = rows * scale
    gather(last_ref, back_ref, emit)
    def turn(i):
        cols = pl.ds(pl.multiple_of(i * LANES, LANES), LANES)
        out_ref[:, cols] = time_ref[cols, :].T
    loop(0, seq // LANES, 4, turn)

PARAMS = pltpu.CompilerParams(vmem_limit_bytes=56 * 2**20)
VM = pl.BlockSpec(memory_space=pltpu.VMEM)

def sds(shape, dt): return jax.ShapeDtypeStruct(shape, dt)

def filter_spectrum(h, tabs):
    first, fwd, inv, last = tabs
    seq = h.shape[1]; half = seq // FAST
    return pl.pallas_call(filter_kernel, out_shape=sds((half + 1, 2 * FAST, LANES), F32),
        in_specs=[VM] * 3, out_specs=VM, name="filter_spectrum",
        scratch_shapes=[pltpu.VMEM((seq, LANES), F32), pltpu.VMEM((2 * seq, LANES), F32)],
        compiler_params=PARAMS)(h, first, fwd)

def convolve(x, spec, tabs, conj):
    first, fwd, inv, last = tabs
    half = first.shape[1]; seq = half * FAST
    return pl.pallas_call(functools.partial(pair_kernel, conj),
        out_shape=(sds(x.shape, BF16), sds(spec.shape, F32)),
        in_specs=[VM] * 6, out_specs=(VM, VM), name="convolve",
        scratch_shapes=[pltpu.VMEM((2 * seq, LANES), F32), pltpu.VMEM((2 * seq, LANES), F32)],
        compiler_params=PARAMS)(x, spec, first, fwd, inv, last)

def filter_gradient(s, g, tabs, scale):
    first, fwd, inv, last = tabs
    half = first.shape[1]; seq = half * FAST
    return pl.pallas_call(functools.partial(grad_kernel, scale),
        out_shape=sds((LANES, seq), F32),
        in_specs=[VM] * 4, out_specs=VM, name="filter_gradient",
        scratch_shapes=[pltpu.VMEM((seq, LANES), F32), pltpu.VMEM((2 * seq, LANES), F32)],
        compiler_params=PARAMS)(s, g, inv, last)


def permuted(value, hold_ref, emit):
    hold_ref[...] = value
    per = value.shape[0] // FAST
    for a in range(FAST):
        emit(a, hold_ref[pl.ds(a, per, stride=FAST), :].astype(BF16))


def gate_kernel(key_ref, value_ref, out_ref, hold_ref):
    def emit(a, rows):
        out_ref[0, a] = rows

    permuted(key_ref[...].astype(F32) * value_ref[...].astype(F32), hold_ref, emit)


def gate(key_in, value_in, groups):
    rows = key_in.shape[0]
    block = pl.BlockSpec((rows, LANES), lambda j: (0, j))
    return pl.pallas_call(
        gate_kernel,
        grid=(groups,),
        out_shape=sds((groups, FAST, rows // FAST, LANES), BF16),
        in_specs=[block, block],
        out_specs=pl.BlockSpec((1, FAST, rows // FAST, LANES), lambda j: (j, 0, 0, 0)),
        scratch_shapes=[pltpu.VMEM((rows, LANES), F32)],
        compiler_params=PARAMS,
        name="gate",
    )(key_in, value_in)


WIDE = 256


def mix_kernel(x_ref, w_ref, query_ref, mix_ref, out_ref, hold_ref):
    parts, depth = w_ref.shape[0], w_ref.shape[2]
    piece = x_ref.shape[2]
    total = None
    for i in range(parts):
        col = i * depth
        left = x_ref[col // piece, :, col % piece : col % piece + depth]
        part = lax.dot_general(left, w_ref[i], (((1,), (1,)), ((), ())), preferred_element_type=F32)
        total = part if total is None else total + part
    mix = total.astype(BF16)
    mix_ref[...] = mix
    scaled = mix.astype(F32) * query_ref[...].astype(F32)
    for g in range(WIDE // LANES):
        def emit(a, rows):
            out_ref[g, a] = rows

        permuted(scaled[:, g * LANES : (g + 1) * LANES], hold_ref, emit)


def mix(x, w, query, groups):
    rows, cols = query.shape
    return pl.pallas_call(
        mix_kernel,
        grid=(cols // WIDE,),
        out_shape=(sds((rows, cols), BF16), sds((groups, FAST, rows // FAST, LANES), BF16)),
        in_specs=[
            pl.BlockSpec(x.shape, lambda j: (0, 0, 0)),
            pl.BlockSpec((w.shape[0], WIDE, w.shape[2]), lambda j: (0, j, 0)),
            pl.BlockSpec((rows, WIDE), lambda j: (0, j)),
        ],
        out_specs=(
            pl.BlockSpec((rows, WIDE), lambda j: (0, j)),
            pl.BlockSpec((WIDE // LANES, FAST, rows // FAST, LANES), lambda j: (j, 0, 0, 0)),
        ),
        scratch_shapes=[pltpu.VMEM((rows, LANES), F32)],
        compiler_params=PARAMS,
        name="mix",
    )(x, w, query)


def unpermuted(part_ref, hold_ref):
    per = part_ref.shape[2]
    for a in range(FAST):
        hold_ref[pl.ds(a, per, stride=FAST), :] = part_ref[0, a].astype(F32)
    return hold_ref[...]


def finish_kernel(conv_ref, back_ref, mix_ref, key_ref, value_ref, gq_ref, gk_ref, gv_ref, hold_ref):
    conv = unpermuted(conv_ref, hold_ref)
    gq_ref[...] = (mix_ref[...].astype(F32) * conv).astype(BF16)
    back = unpermuted(back_ref, hold_ref)
    gk_ref[...] = (back * value_ref[...].astype(F32)).astype(BF16)
    gv_ref[...] = (back * key_ref[...].astype(F32)).astype(BF16)


def finish(conv, back, grad_mix, key_in, value_in):
    groups, _, per, _ = conv.shape
    rows, cols = key_in.shape
    block = pl.BlockSpec((rows, LANES), lambda j: (0, j))
    part = pl.BlockSpec((1, FAST, per, LANES), lambda j: (j, 0, 0, 0))
    return pl.pallas_call(
        finish_kernel,
        grid=(groups,),
        out_shape=(sds((rows, cols), BF16),) * 3,
        in_specs=[part, part, block, block, block],
        out_specs=(block,) * 3,
        scratch_shapes=[pltpu.VMEM((rows, LANES), F32)],
        compiler_params=PARAMS,
        name="finish",
    )(conv, back, grad_mix, key_in, value_in)


def exchange(parts):
    return lax.all_to_all(parts, "ctx", split_axis=0, concat_axis=0, tiled=True)


def lane_body(grad_out, proj_out, query, key_in, value_in, filters):
    seq = filters.shape[1]
    groups = seq // key_in.shape[0]
    tabs = tables(seq)
    gated = exchange(gate(key_in, value_in, groups))
    spec = filter_spectrum(filters, tabs)
    conv_out, gated_spec = convolve(gated, spec, tabs, False)
    conv_back = exchange(conv_out)
    x = lax.all_gather(grad_out, "mp", axis=0)
    w = lax.all_gather(proj_out, "ctx", axis=0)
    grad_mix, scaled = mix(x, w, query, groups)
    scaled = exchange(scaled)
    grad_gated, scaled_spec = convolve(scaled, spec, tabs, True)
    grad_back = exchange(grad_gated)
    filter_grad = filter_gradient(scaled_spec, gated_spec, tabs, 1.0 / math.sqrt(seq))
    grad_query, grad_key, grad_value = finish(conv_back, grad_back, grad_mix, key_in, value_in)
    return (grad_query, grad_key, grad_value, filter_grad)


def body(grad_out, proj_out, query, key_in, value_in, filters):
    rows, cols = key_in.shape
    lanes, seq = filters.shape
    fits = (
        lanes == LANES
        and rows % (16 * FAST) == 0
        and cols % WIDE == 0
        and seq % (LANES * FAST) == 0
        and seq // FAST <= 2 * LANES
        and proj_out.shape[1] % LANES == 0
        and grad_out.shape[1] % proj_out.shape[1] == 0
    )
    args = (grad_out, proj_out, query, key_in, value_in, filters)
    return lane_body(*args) if fits else general_body(*args)


def solution(mesh):
    return jax.shard_map(
        body,
        mesh=mesh,
        in_specs=(
            P("ctx", "mp"),
            P("mp", "ctx"),
            P("ctx", "mp"),
            P("ctx", "mp"),
            P("ctx", "mp"),
            P(("mp", "ctx"), None),
        ),
        out_specs=(P("ctx", "mp"), P("ctx", "mp"), P("ctx", "mp"), P(("mp", "ctx"), None)),
        check_vma=False,
    )
```

```python
import functools
import math

import jax
import jax.numpy as jnp
import ml_dtypes
import numpy as np
from jax import lax
from jax.experimental import pallas as pl
from jax.experimental.pallas import tpu as pltpu
from jax.sharding import PartitionSpec as P


def phase_table(rows_n, cols_n, modulus):
    prod_idx = (
        jnp.arange(rows_n, dtype=jnp.int32)[:, None]
        * jnp.arange(cols_n, dtype=jnp.int32)[None, :]
        % modulus
    )
    angles = prod_idx.astype(jnp.float32) * (2.0 * math.pi / modulus)
    return (jnp.cos(angles), jnp.sin(angles))


def make_tables(length_all):
    size_second = min(128, length_all)
    size_first = length_all // size_second
    cos_first, sin_first = phase_table(size_first, size_first, size_first)
    twist_cos, twist_sin = phase_table(size_first, size_second, length_all)
    cos_second, sin_second = phase_table(size_second, size_second, size_second)
    return (cos_first, sin_first, twist_cos, twist_sin, cos_second, sin_second)


def contract(form, left, right):
    return jnp.einsum(form, left, right, precision=lax.Precision.HIGHEST)


def forward_real(signal, tables):
    cos_first, sin_first, twist_cos, twist_sin, cos_second, sin_second = tables
    part_re = contract("kn,cnm->ckm", cos_first, signal)
    part_im = -contract("kn,cnm->ckm", sin_first, signal)
    turned_re = part_re * twist_cos + part_im * twist_sin
    turned_im = part_im * twist_cos - part_re * twist_sin
    spec_re = contract("ckm,mj->ckj", turned_re, cos_second) + contract(
        "ckm,mj->ckj", turned_im, sin_second
    )
    spec_im = contract("ckm,mj->ckj", turned_im, cos_second) - contract(
        "ckm,mj->ckj", turned_re, sin_second
    )
    return (spec_re, spec_im)


def inverse_real(spec_re, spec_im, tables):
    cos_first, sin_first, twist_cos, twist_sin, cos_second, sin_second = tables
    back_re = contract("ckj,jm->ckm", spec_re, cos_second) - contract(
        "ckj,jm->ckm", spec_im, sin_second
    )
    back_im = contract("ckj,jm->ckm", spec_re, sin_second) + contract(
        "ckj,jm->ckm", spec_im, cos_second
    )
    twist_re = back_re * twist_cos - back_im * twist_sin
    twist_im = back_re * twist_sin + back_im * twist_cos
    return contract("nk,ckm->cnm", cos_first, twist_re) - contract(
        "nk,ckm->cnm", sin_first, twist_im
    )


def long_filter_grads(gated, scaled, kernel):
    channels, seq_len = kernel.shape
    length_all = 2 * seq_len
    tables = make_tables(length_all)
    spec_shape = (channels, tables[0].shape[0], tables[4].shape[0])

    def padded(values):
        wide = jnp.concatenate(
            [values.astype(jnp.float32), jnp.zeros((channels, seq_len), jnp.float32)], axis=1
        )
        return wide.reshape(spec_shape)

    def restore(spec_re, spec_im):
        return (
            inverse_real(spec_re, spec_im, tables).reshape(channels, length_all)[:, :seq_len]
            / length_all
        )

    gated_re, gated_im = forward_real(padded(gated), tables)
    scaled_re, scaled_im = forward_real(padded(scaled), tables)
    kernel_re, kernel_im = forward_real(padded(kernel), tables)
    conv_out = restore(
        kernel_re * gated_re - kernel_im * gated_im, kernel_re * gated_im + kernel_im * gated_re
    )
    grad_gated = restore(
        scaled_re * kernel_re + scaled_im * kernel_im, scaled_im * kernel_re - scaled_re * kernel_im
    )
    grad_kernel = restore(
        scaled_re * gated_re + scaled_im * gated_im, scaled_im * gated_re - scaled_re * gated_im
    )
    filter_grad = grad_kernel / math.sqrt(seq_len)
    return (conv_out.astype(jnp.bfloat16), grad_gated.astype(jnp.bfloat16), filter_grad)


def product(left, right):
    return (left.astype(jnp.float32) * right.astype(jnp.float32)).astype(jnp.bfloat16)


def general_body(grad_out, proj_out, query, key_in, value_in, filters):
    weight_rows = lax.all_gather(proj_out, "ctx", axis=1, tiled=True)
    grad_mix = lax.dot_general(
        lax.all_gather(grad_out, "mp", axis=1, tiled=True),
        weight_rows,
        (((1,), (1,)), ((), ())),
        preferred_element_type=jnp.float32,
    ).astype(jnp.bfloat16)
    gated = product(key_in, value_in)
    scaled = product(grad_mix, query)
    chan_gated, chan_scaled = (
        lax.all_to_all(gated.T, "ctx", split_axis=0, concat_axis=1, tiled=True),
        lax.all_to_all(scaled.T, "ctx", split_axis=0, concat_axis=1, tiled=True),
    )
    conv_out, grad_gated, filter_grad = long_filter_grads(chan_gated, chan_scaled, filters)
    back_grad, back_conv = (
        lax.all_to_all(grad_gated, "ctx", split_axis=1, concat_axis=0, tiled=True),
        lax.all_to_all(conv_out, "ctx", split_axis=1, concat_axis=0, tiled=True),
    )
    grad_query = product(grad_mix, back_conv.T)
    grad_key = product(back_grad.T, value_in)
    grad_value = product(back_grad.T, key_in)
    return (grad_query, grad_key, grad_value, filter_grad)


FAST = 32
SLOT = 2 * FAST
PAIR = 2 * SLOT
LANES = 128
F32, BF16 = jnp.float32, jnp.bfloat16
PARAMS = pltpu.CompilerParams(vmem_limit_bytes=60 * 2**20)
VM = pl.BlockSpec(memory_space=pltpu.VMEM)
ANY = pl.BlockSpec(memory_space=pl.ANY)
U1, U2 = 16, 16


def sds(shape, dtype):
    return jax.ShapeDtypeStruct(shape, dtype)


def cost(flops, moved):
    return pl.CostEstimate(flops=flops // 10**6, bytes_accessed=moved // 10**3, transcendentals=0)


def tables(seq):
    size = 2 * seq
    slow = size // FAST
    half = slow // 2
    s = np.arange(half)
    angle = 2 * np.pi * ((s[:, None] * s[None, :]) % slow) / slow
    first = np.concatenate([np.cos(angle), -np.sin(angle)], 0)
    first[half] = 1.0 - 2.0 * (s % 2)
    weight = np.full((2 * half, 1), 2.0)
    weight[0] = weight[half] = 1.0
    last = (first * weight).T / size
    a = np.arange(FAST)
    k = np.arange(half + 1)[:, None] + slow * a[None, :]
    turn = 2 * np.pi * ((k[:, :, None] * a[None, None, :]) % size) / size
    c, d = np.cos(turn), np.sin(turn)
    fwd = np.concatenate([np.concatenate([c, d], 2), np.concatenate([-d, c], 2)], 1)
    inv = fwd.transpose(0, 2, 1).copy()
    fwd[0, :, FAST:] = 0.0
    inv[0, FAST:] = 0.0

    def paired(blocks):
        out = np.zeros((half // 2 + 1, PAIR, PAIR))
        out[:-1, :SLOT, :SLOT] = blocks[0:half:2]
        out[:-1, SLOT:, SLOT:] = blocks[1:half:2]
        return out

    fwd, inv, edge_fwd, edge_inv = paired(fwd), paired(inv), fwd[half], inv[half]
    fwd[-1, :SLOT, FAST:SLOT] = edge_fwd[:, :FAST]
    inv[-1, FAST:SLOT, :SLOT] = edge_inv[:FAST]
    return [jnp.asarray(t.astype(ml_dtypes.bfloat16)) for t in (first, fwd, inv, last)]


def dot(left, right):
    return jnp.dot(left, right, preferred_element_type=F32)


def loop(count, unroll, step):
    def some(i, carry):
        for u in range(unroll):
            step(i * unroll + u)
        return carry

    lax.fori_loop(0, count // unroll, some, 0)


def span(start, size):
    return pl.ds(pl.multiple_of(start * size, size), size)


def spread(signal, first_ref, mid_ref):
    half = first_ref.shape[1]

    def step(a):
        out = dot(first_ref[...], signal(a))
        mid_ref[pl.ds(a, half, stride=SLOT), :] = out[:half]
        mid_ref[pl.ds(FAST + a, half, stride=SLOT), :] = out[half:]

    loop(FAST, U1, step)


def collect(last_ref, back_ref, emit):
    half = last_ref.shape[0]

    def step(a):
        re = back_ref[pl.ds(a, half, stride=SLOT), :]
        im = back_ref[pl.ds(FAST + a, half, stride=SLOT), :]
        emit(a, dot(last_ref[...], jnp.concatenate([re, im], 0).astype(BF16)))

    loop(FAST, U1, step)


def times(x, y, conjugate):
    parts = []
    for i in range(0, x.shape[0], SLOT):
        xr, xi, yr, yi = (v[i + j : i + j + FAST] for v in (x, y) for j in (0, FAST))
        if conjugate:
            parts += [xr * yr + xi * yi, xi * yr - xr * yi]
        else:
            parts += [xr * yr - xi * yi, xr * yi + xi * yr]
    return jnp.concatenate(parts, 0).astype(BF16)


def filter_kernel(h_ref, first_ref, fwd_ref, spec_ref, time_ref, mid_ref):
    half = first_ref.shape[1]
    seq = h_ref.shape[1]

    def turn(i):
        time_ref[span(i, LANES), :] = h_ref[:, span(i, LANES)].T

    loop(seq // LANES, 8, turn)
    spread(lambda a: time_ref[pl.ds(a, half, stride=FAST), :].astype(BF16), first_ref, mid_ref)

    def step(p):
        spec_ref[span(p, PAIR), :] = dot(fwd_ref[p], mid_ref[span(p, PAIR), :].astype(BF16))

    loop(half // 2, U2, step)
    spec_ref[span(half // 2, PAIR), :] = dot(fwd_ref[half // 2], mid_ref[:PAIR, :].astype(BF16))


def convolve_kernel(conjugate, x_ref, h_any, first_ref, fwd_any, inv_any, last_ref,
                    out_ref, spec_any, h_ref, fwd_ref, inv_ref, spec_ref, mid_ref, back_ref, sem):
    half = first_ref.shape[1]
    groups, _, per, _ = x_ref.shape
    loads = [
        pltpu.make_async_copy(source, target, sem.at[i])
        for i, (source, target) in enumerate(((fwd_any, fwd_ref), (h_any, h_ref), (inv_any, inv_ref)))
    ]
    for load in loads:
        load.start()
    spread(lambda a: x_ref[:, a].reshape(half, LANES), first_ref, mid_ref)
    for load in loads:
        load.wait()

    def step(p):
        x = dot(fwd_ref[p], mid_ref[span(p, PAIR), :].astype(BF16))
        spec_ref[span(p, PAIR), :] = x
        back_ref[span(p, PAIR), :] = dot(inv_ref[p], times(x, h_ref[span(p, PAIR), :], conjugate))

    loop(half // 2, U2, step)
    tail = span(half // 2, PAIR)
    x = dot(fwd_ref[half // 2], mid_ref[:PAIR, :].astype(BF16))
    spec_ref[tail, :] = x
    store = pltpu.make_async_copy(spec_ref, spec_any, sem.at[3])
    store.start()
    back_ref[:PAIR, :] += dot(inv_ref[half // 2], times(x, h_ref[tail, :], conjugate))

    def emit(a, rows):
        out_ref[:, a] = rows.reshape(groups, per, LANES).astype(BF16)

    collect(last_ref, back_ref, emit)
    store.wait()


def gradient_kernel(scale, s_ref, g_ref, inv_ref, last_ref, out_ref, time_ref, back_ref):
    half = last_ref.shape[0]
    seq = out_ref.shape[1]

    def step(p):
        rows = span(p, PAIR)
        back_ref[rows, :] = dot(inv_ref[p], times(s_ref[rows, :], g_ref[rows, :], True))

    loop(half // 2, U2, step)
    tail = span(half // 2, PAIR)
    back_ref[:PAIR, :] += dot(inv_ref[half // 2], times(s_ref[tail, :], g_ref[tail, :], True))

    def emit(a, rows):
        time_ref[pl.ds(a, half, stride=FAST), :] = rows * scale

    collect(last_ref, back_ref, emit)

    def turn(i):
        out_ref[:, span(i, LANES)] = time_ref[span(i, LANES), :].T

    loop(seq // LANES, 8, turn)


def filter_spectrum(h, tabs):
    first, fwd = tabs[:2]
    seq = h.shape[1]
    return pl.pallas_call(
        filter_kernel,
        out_shape=sds((2 * seq + PAIR, LANES), F32),
        in_specs=[VM] * 3,
        out_specs=VM,
        scratch_shapes=[pltpu.VMEM((seq, LANES), F32), pltpu.VMEM((2 * seq, LANES), F32)],
        compiler_params=PARAMS,
        cost_estimate=cost(10**9, 8 * 2**20),
        name="filter_spectrum",
    )(h, first, fwd)


def convolve(x, spec, tabs, conjugate):
    fwd = tabs[1]
    rows = spec.shape[0]
    big = pltpu.VMEM((rows - PAIR, LANES), F32)
    return pl.pallas_call(
        functools.partial(convolve_kernel, conjugate),
        out_shape=(sds(x.shape, BF16), sds(spec.shape, F32)),
        in_specs=[VM, ANY, VM, ANY, ANY, VM],
        out_specs=(VM, ANY),
        scratch_shapes=[
            pltpu.VMEM(spec.shape, F32),
            pltpu.VMEM(fwd.shape, BF16),
            pltpu.VMEM(fwd.shape, BF16),
            pltpu.VMEM(spec.shape, F32),
            big,
            big,
            pltpu.SemaphoreType.DMA((4,)),
        ],
        compiler_params=PARAMS,
        cost_estimate=cost(2 * 10**9, 14 * 2**20),
        name="convolve",
    )(x, spec, *tabs)


def filter_gradient(scaled_spec, gated_spec, tabs, scale):
    inv, last = tabs[2:]
    seq = (scaled_spec.shape[0] - PAIR) // 2
    return pl.pallas_call(
        functools.partial(gradient_kernel, scale),
        out_shape=sds((LANES, seq), F32),
        in_specs=[VM] * 4,
        out_specs=VM,
        scratch_shapes=[pltpu.VMEM((seq, LANES), F32), pltpu.VMEM((2 * seq, LANES), F32)],
        compiler_params=PARAMS,
        cost_estimate=cost(10**9, 12 * 2**20),
        name="filter_gradient",
    )(scaled_spec, gated_spec, inv, last)


def permuted(value, hold_ref, emit):
    hold_ref[...] = value
    per = value.shape[0] // FAST
    for a in range(FAST):
        emit(a, hold_ref[pl.ds(a, per, stride=FAST), :].astype(BF16))


def gate_kernel(key_ref, value_ref, out_ref, hold_ref):
    product = key_ref[...].astype(F32) * value_ref[...].astype(F32)
    for g in range(WIDE // LANES):

        def emit(a, rows):
            out_ref[g, a] = rows

        permuted(product[:, g * LANES : (g + 1) * LANES], hold_ref, emit)


def gate(key_in, value_in, groups):
    rows, cols = key_in.shape
    block = pl.BlockSpec((rows, WIDE), lambda j: (0, j))
    return pl.pallas_call(
        gate_kernel,
        grid=(cols // WIDE,),
        out_shape=sds((groups, FAST, rows // FAST, LANES), BF16),
        in_specs=[block, block],
        out_specs=pl.BlockSpec((WIDE // LANES, FAST, rows // FAST, LANES), lambda j: (j, 0, 0, 0)),
        scratch_shapes=[pltpu.VMEM((rows, LANES), F32)],
        compiler_params=PARAMS,
        cost_estimate=cost(10**6, 3 * 2**20),
        name="gate",
    )(key_in, value_in)


WIDE = 256
CHIPS = 4


def pieces_of(x_ref, piece, lane, depth):
    return x_ref[piece, :, pl.ds(pl.multiple_of(lane * depth, depth), depth)]


def against(left, w_ref):
    return lax.dot_general(left, w_ref[...], (((1,), (1,)), ((), ())), preferred_element_type=F32)


def terms_kernel(dists, place_ref, *refs):
    count = 2 * sum(1 if d == 0 else 2 for d in dists)
    x_ref, ws, before, sum_ref = refs[0], refs[1 : 1 + count], refs[1 + count : -1], refs[-1]
    here, core = place_ref[0], place_ref[1]
    depth = ws[0].shape[1]

    def part(piece, near_ref, swap_ref):
        one = against(pieces_of(x_ref, piece, core, depth), near_ref)
        return one + against(pieces_of(x_ref, piece, 1 - core, depth), swap_ref)

    if before:
        sum_ref[...] = before[0][...]
    for d in dists:
        if d == 0:
            sum_ref[...] = part(here, ws[0], ws[1])
            ws = ws[2:]
            continue
        up, up_swap, down, down_swap = ws[:4]
        ws = ws[4:]

        @pl.when(here >= d)
        def _():
            sum_ref[...] += part(here - d, up, up_swap)

        @pl.when(here + d < CHIPS)
        def _():
            sum_ref[...] += part(here + d, down, down_swap)


def above(d):
    return lambda j, place: (jnp.where(place[0] >= d, j, 0), 0)


def below(d):
    return lambda j, place: (jnp.where(place[0] + d < CHIPS, j, 0), 0)


def terms(dists, place, x, ws, *before):
    _, rows, _ = x.shape
    cols, depth = ws[0].shape
    maps = []
    for d in dists:
        maps += [above(d), above(d)] + ([below(d), below(d)] if d else [])
    wide = pl.BlockSpec((rows, WIDE), lambda j, place: (0, j))
    return pl.pallas_call(
        functools.partial(terms_kernel, dists),
        out_shape=sds((rows, cols), F32),
        grid_spec=pltpu.PrefetchScalarGridSpec(
            num_scalar_prefetch=1,
            grid=(cols // WIDE,),
            in_specs=[pl.BlockSpec(x.shape, lambda j, place: (0, 0, 0))]
            + [pl.BlockSpec((WIDE, depth), m) for m in maps]
            + [wide] * len(before),
            out_specs=wide,
        ),
        compiler_params=PARAMS,
        cost_estimate=cost(2 * 10**9, 14 * 2**20),
        name="terms",
    )(place, x, *ws, *before)


def late_kernel(place_ref, *refs):
    x_ref, ws = refs[0], refs[1:5]
    sum_ref, query_ref, mix_ref, out_ref, total_ref, hold_ref = refs[5:]
    here, core = place_ref[0], place_ref[1]
    depth = ws[0].shape[1]

    def part(near_ref, swap_ref):
        one = against(pieces_of(x_ref, 0, core, depth), near_ref)
        return one + against(pieces_of(x_ref, 0, 1 - core, depth), swap_ref)

    total_ref[...] = sum_ref[...]

    @pl.when(here == CHIPS - 1)
    def _():
        total_ref[...] += part(ws[0], ws[1])

    @pl.when(here == 0)
    def _():
        total_ref[...] += part(ws[2], ws[3])

    mix = total_ref[...].astype(BF16)
    mix_ref[...] = mix
    scaled = mix.astype(F32) * query_ref[...].astype(F32)
    for g in range(WIDE // LANES):

        def emit(a, rows):
            out_ref[g, a] = rows

        permuted(scaled[:, g * LANES : (g + 1) * LANES], hold_ref, emit)


def mix_late(place, x, ws, total, query, groups):
    rows, cols = query.shape
    depth = ws[0].shape[1]
    maps = [above(CHIPS - 1)] * 2 + [below(CHIPS - 1)] * 2
    wide = pl.BlockSpec((rows, WIDE), lambda j, place: (0, j))
    parts = pl.BlockSpec((WIDE // LANES, FAST, rows // FAST, LANES), lambda j, place: (j, 0, 0, 0))
    return pl.pallas_call(
        late_kernel,
        out_shape=(sds((rows, cols), BF16), sds((groups, FAST, rows // FAST, LANES), BF16)),
        grid_spec=pltpu.PrefetchScalarGridSpec(
            num_scalar_prefetch=1,
            grid=(cols // WIDE,),
            in_specs=[pl.BlockSpec((1,) + x.shape[1:], lambda j, place: (jnp.where(place[0] == 0, CHIPS - 1, 0), 0, 0))]
            + [pl.BlockSpec((WIDE, depth), m) for m in maps]
            + [wide, wide],
            out_specs=(wide, parts),
            scratch_shapes=[
                pltpu.VMEM((rows, WIDE), F32),
                pltpu.VMEM((rows, LANES), F32),
            ],
        ),
        compiler_params=PARAMS,
        cost_estimate=cost(10**9, 8 * 2**20),
        name="mix_late",
    )(place, x, *ws, total, query)


def unpermuted(part_ref, g, hold_ref):
    per = part_ref.shape[2]
    for a in range(FAST):
        hold_ref[pl.ds(a, per, stride=FAST), :] = part_ref[g, a].astype(F32)
    return hold_ref[...]


def finish_kernel(count, *refs):
    part_ref, factors, outs, hold_ref = refs[0], refs[1 : 1 + count], refs[1 + count : 1 + 2 * count], refs[-1]
    for g in range(WIDE // LANES):
        value = unpermuted(part_ref, g, hold_ref)
        lanes = pl.ds(g * LANES, LANES)
        for factor_ref, out_ref in zip(factors, outs):
            out_ref[:, lanes] = (value * factor_ref[:, lanes].astype(F32)).astype(BF16)


def finish(parts, *factors):
    _, _, per, _ = parts.shape
    rows, cols = factors[0].shape
    count = len(factors)
    wide = pl.BlockSpec((rows, WIDE), lambda j: (0, j))
    part = pl.BlockSpec((WIDE // LANES, FAST, per, LANES), lambda j: (j, 0, 0, 0))
    return pl.pallas_call(
        functools.partial(finish_kernel, count),
        grid=(cols // WIDE,),
        out_shape=(sds((rows, cols), BF16),) * count,
        in_specs=[part] + [wide] * count,
        out_specs=(wide,) * count,
        scratch_shapes=[pltpu.VMEM((rows, LANES), F32)],
        compiler_params=PARAMS,
        cost_estimate=cost(10**6, (1 + 2 * count) * 2**20),
        name="finish",
    )(parts, *factors)


def exchange(parts):
    return lax.all_to_all(parts, "ctx", split_axis=0, concat_axis=0, tiled=True)


SWAP = [(i, i ^ 1) for i in range(2 * CHIPS)]


def hop(low, high, d):
    up = [(i, i + 2) for i in range(2 * (d - 1), 2 * CHIPS - 2)]
    down = [(i, i - 2) for i in range(2, 2 * (CHIPS - d + 1))]
    return lax.ppermute(low, "ctx", up), lax.ppermute(high, "ctx", down)


def with_swaps(low, high, d):
    low_swap = lax.ppermute(low, "ctx", [p for p in SWAP if p[0] >= 2 * d])
    high_swap = lax.ppermute(high, "ctx", [p for p in SWAP if p[0] < 2 * (CHIPS - d)])
    return [low, low_swap, high, high_swap]


def lane_body(grad_out, proj_out, query, key_in, value_in, filters):
    seq = filters.shape[1]
    groups = seq // key_in.shape[0]
    tabs = tables(seq)
    tie = lax.optimization_barrier
    ctx = lax.axis_index("ctx")
    place = jnp.stack([ctx // 2, ctx % 2]).astype(jnp.int32)

    low1, high1 = hop(proj_out, proj_out, 1)
    x = lax.all_gather(grad_out, "mp", axis=0)
    gated = exchange(gate(key_in, value_in, groups))
    spec = filter_spectrum(filters, tabs)
    low1, high1, spec, own = tie((low1, high1, spec, proj_out))

    low2, high2 = hop(low1, high1, 2)
    ws = [own, lax.ppermute(own, "ctx", SWAP)] + with_swaps(low1, high1, 1)
    conv_out, gated_spec = convolve(gated, spec, tabs, False)
    low2, high2, conv_out, *ws = tie((low2, high2, conv_out, *ws))

    low3, high3 = hop(low2, high2, 3)
    ws += with_swaps(low2, high2, 2)
    conv_back = exchange(conv_out)
    total = terms((0, 1, 2), place, x, ws)
    low3, high3, total = tie((low3, high3, total))

    ws = with_swaps(low3, high3, 3)
    grad_mix, scaled = mix_late(place, x, ws, total, query, groups)
    scaled, conv_back = tie((scaled, conv_back))
    scaled = exchange(scaled)
    grad_gated, scaled_spec = convolve(scaled, spec, tabs, True)
    grad_back = exchange(grad_gated)
    filter_grad = filter_gradient(scaled_spec, gated_spec, tabs, 1.0 / math.sqrt(seq))
    (grad_query,) = finish(conv_back, grad_mix)
    grad_key, grad_value = finish(grad_back, value_in, key_in)
    return (grad_query, grad_key, grad_value, filter_grad)


def body(grad_out, proj_out, query, key_in, value_in, filters):
    rows, cols = key_in.shape
    lanes, seq = filters.shape
    fits = (
        lax.axis_size("ctx") == 2 * CHIPS
        and lax.axis_size("mp") == 4
        and lanes == LANES
        and rows % (16 * FAST) == 0
        and cols == 2 * CHIPS * LANES
        and seq == 2 * CHIPS * rows
        and seq == FAST * LANES
        and grad_out.shape[1] == 2 * proj_out.shape[1]
    )
    args = (grad_out, proj_out, query, key_in, value_in, filters)
    return lane_body(*args) if fits else general_body(*args)


def solution(mesh):
    return jax.shard_map(
        body,
        mesh=mesh,
        in_specs=(
            P("ctx", "mp"),
            P("mp", "ctx"),
            P("ctx", "mp"),
            P("ctx", "mp"),
            P("ctx", "mp"),
            P(("mp", "ctx"), None),
        ),
        out_specs=(P("ctx", "mp"), P("ctx", "mp"), P("ctx", "mp"), P(("mp", "ctx"), None)),
        check_vma=False,
    )
```

```python
import functools
import math

import jax
import jax.numpy as jnp
import ml_dtypes
import numpy as np
from jax import lax
from jax.experimental import pallas as pl
from jax.experimental.pallas import tpu as pltpu
from jax.sharding import PartitionSpec as P


def phase_table(rows_n, cols_n, modulus):
    prod_idx = (
        jnp.arange(rows_n, dtype=jnp.int32)[:, None]
        * jnp.arange(cols_n, dtype=jnp.int32)[None, :]
        % modulus
    )
    angles = prod_idx.astype(jnp.float32) * (2.0 * math.pi / modulus)
    return (jnp.cos(angles), jnp.sin(angles))


def make_tables(length_all):
    size_second = min(128, length_all)
    size_first = length_all // size_second
    cos_first, sin_first = phase_table(size_first, size_first, size_first)
    twist_cos, twist_sin = phase_table(size_first, size_second, length_all)
    cos_second, sin_second = phase_table(size_second, size_second, size_second)
    return (cos_first, sin_first, twist_cos, twist_sin, cos_second, sin_second)


def contract(form, left, right):
    return jnp.einsum(form, left, right, precision=lax.Precision.HIGHEST)


def forward_real(signal, tables):
    cos_first, sin_first, twist_cos, twist_sin, cos_second, sin_second = tables
    part_re = contract("kn,cnm->ckm", cos_first, signal)
    part_im = -contract("kn,cnm->ckm", sin_first, signal)
    turned_re = part_re * twist_cos + part_im * twist_sin
    turned_im = part_im * twist_cos - part_re * twist_sin
    spec_re = contract("ckm,mj->ckj", turned_re, cos_second) + contract(
        "ckm,mj->ckj", turned_im, sin_second
    )
    spec_im = contract("ckm,mj->ckj", turned_im, cos_second) - contract(
        "ckm,mj->ckj", turned_re, sin_second
    )
    return (spec_re, spec_im)


def inverse_real(spec_re, spec_im, tables):
    cos_first, sin_first, twist_cos, twist_sin, cos_second, sin_second = tables
    back_re = contract("ckj,jm->ckm", spec_re, cos_second) - contract(
        "ckj,jm->ckm", spec_im, sin_second
    )
    back_im = contract("ckj,jm->ckm", spec_re, sin_second) + contract(
        "ckj,jm->ckm", spec_im, cos_second
    )
    twist_re = back_re * twist_cos - back_im * twist_sin
    twist_im = back_re * twist_sin + back_im * twist_cos
    return contract("nk,ckm->cnm", cos_first, twist_re) - contract(
        "nk,ckm->cnm", sin_first, twist_im
    )


def long_filter_grads(gated, scaled, kernel):
    channels, seq_len = kernel.shape
    length_all = 2 * seq_len
    tables = make_tables(length_all)
    spec_shape = (channels, tables[0].shape[0], tables[4].shape[0])

    def padded(values):
        wide = jnp.concatenate(
            [values.astype(jnp.float32), jnp.zeros((channels, seq_len), jnp.float32)], axis=1
        )
        return wide.reshape(spec_shape)

    def restore(spec_re, spec_im):
        return (
            inverse_real(spec_re, spec_im, tables).reshape(channels, length_all)[:, :seq_len]
            / length_all
        )

    gated_re, gated_im = forward_real(padded(gated), tables)
    scaled_re, scaled_im = forward_real(padded(scaled), tables)
    kernel_re, kernel_im = forward_real(padded(kernel), tables)
    conv_out = restore(
        kernel_re * gated_re - kernel_im * gated_im, kernel_re * gated_im + kernel_im * gated_re
    )
    grad_gated = restore(
        scaled_re * kernel_re + scaled_im * kernel_im, scaled_im * kernel_re - scaled_re * kernel_im
    )
    grad_kernel = restore(
        scaled_re * gated_re + scaled_im * gated_im, scaled_im * gated_re - scaled_re * gated_im
    )
    filter_grad = grad_kernel / math.sqrt(seq_len)
    return (conv_out.astype(jnp.bfloat16), grad_gated.astype(jnp.bfloat16), filter_grad)


def product(left, right):
    return (left.astype(jnp.float32) * right.astype(jnp.float32)).astype(jnp.bfloat16)


def general_body(grad_out, proj_out, query, key_in, value_in, filters):
    weight_rows = lax.all_gather(proj_out, "ctx", axis=1, tiled=True)
    grad_mix = lax.dot_general(
        lax.all_gather(grad_out, "mp", axis=1, tiled=True),
        weight_rows,
        (((1,), (1,)), ((), ())),
        preferred_element_type=jnp.float32,
    ).astype(jnp.bfloat16)
    gated = product(key_in, value_in)
    scaled = product(grad_mix, query)
    chan_gated, chan_scaled = (
        lax.all_to_all(gated.T, "ctx", split_axis=0, concat_axis=1, tiled=True),
        lax.all_to_all(scaled.T, "ctx", split_axis=0, concat_axis=1, tiled=True),
    )
    conv_out, grad_gated, filter_grad = long_filter_grads(chan_gated, chan_scaled, filters)
    back_grad, back_conv = (
        lax.all_to_all(grad_gated, "ctx", split_axis=1, concat_axis=0, tiled=True),
        lax.all_to_all(conv_out, "ctx", split_axis=1, concat_axis=0, tiled=True),
    )
    grad_query = product(grad_mix, back_conv.T)
    grad_key = product(back_grad.T, value_in)
    grad_value = product(back_grad.T, key_in)
    return (grad_query, grad_key, grad_value, filter_grad)


FAST = 32
SLOT = 2 * FAST
PAIR = 2 * SLOT
LANES = 128
CHIPS = 4
F32, BF16 = jnp.float32, jnp.bfloat16
PARAMS = pltpu.CompilerParams(vmem_limit_bytes=60 * 2**20)
VM = pl.BlockSpec(memory_space=pltpu.VMEM)
ANY = pl.BlockSpec(memory_space=pl.ANY)
U1, U2 = 16, 16


def sds(shape, dtype):
    return jax.ShapeDtypeStruct(shape, dtype)


def cost(flops, moved):
    return pl.CostEstimate(flops=flops // 10**6, bytes_accessed=moved // 10**3, transcendentals=0)


def tables(seq):
    size = 2 * seq
    slow = size // FAST
    half = slow // 2
    s = np.arange(half)
    angle = 2 * np.pi * ((s[:, None] * s[None, :]) % slow) / slow
    first = np.concatenate([np.cos(angle), -np.sin(angle)], 0)
    first[half] = 1.0 - 2.0 * (s % 2)
    weight = np.full((2 * half, 1), 2.0)
    weight[0] = weight[half] = 1.0
    last = (first * weight).T / size
    a = np.arange(FAST)
    k = np.arange(half + 1)[:, None] + slow * a[None, :]
    turn = 2 * np.pi * ((k[:, :, None] * a[None, None, :]) % size) / size
    c, d = np.cos(turn), np.sin(turn)
    fwd = np.concatenate([np.concatenate([c, d], 2), np.concatenate([-d, c], 2)], 1)
    inv = fwd.transpose(0, 2, 1).copy()
    fwd[0, :, FAST:] = 0.0
    inv[0, FAST:] = 0.0

    def paired(blocks):
        out = np.zeros((half // 2 + 1, PAIR, PAIR))
        out[:-1, :SLOT, :SLOT] = blocks[0:half:2]
        out[:-1, SLOT:, SLOT:] = blocks[1:half:2]
        return out

    fwd, inv, edge_fwd, edge_inv = paired(fwd), paired(inv), fwd[half], inv[half]
    fwd[-1, :SLOT, FAST:SLOT] = edge_fwd[:, :FAST]
    inv[-1, FAST:SLOT, :SLOT] = edge_inv[:FAST]
    blocks = np.arange(half).reshape(2 * CHIPS, -1)
    order = [np.concatenate([blocks[c ^ d] for d in range(2 * CHIPS)]) for c in range(2 * CHIPS)]
    firsts, lasts = np.stack([first[:, o] for o in order]), np.stack([last[o] for o in order])
    return [jnp.asarray(t.astype(ml_dtypes.bfloat16)) for t in (firsts, fwd, inv, lasts)]


def dot(left, right):
    return jnp.dot(left, right, preferred_element_type=F32)


def loop(count, unroll, step):
    def some(i, carry):
        for u in range(unroll):
            step(i * unroll + u)
        return carry

    lax.fori_loop(0, count // unroll, some, 0)


def span(start, size):
    return pl.ds(pl.multiple_of(start * size, size), size)


def spread(signal, first_ref, mid_ref):
    half = first_ref.shape[1]

    def step(a):
        out = dot(first_ref[...], signal(a))
        mid_ref[pl.ds(a, half, stride=SLOT), :] = out[:half]
        mid_ref[pl.ds(FAST + a, half, stride=SLOT), :] = out[half:]

    loop(FAST, U1, step)


def collect(last_ref, back_ref, emit):
    half = last_ref.shape[0]

    def step(a):
        re = back_ref[pl.ds(a, half, stride=SLOT), :]
        im = back_ref[pl.ds(FAST + a, half, stride=SLOT), :]
        emit(a, dot(last_ref[...], jnp.concatenate([re, im], 0).astype(BF16)))

    loop(FAST, U1, step)


def times(x, y, conjugate):
    parts = []
    for i in range(0, x.shape[0], SLOT):
        xr, xi, yr, yi = (v[i + j : i + j + FAST] for v in (x, y) for j in (0, FAST))
        if conjugate:
            parts += [xr * yr + xi * yi, xi * yr - xr * yi]
        else:
            parts += [xr * yr - xi * yi, xr * yi + xi * yr]
    return jnp.concatenate(parts, 0).astype(BF16)


def filter_kernel(h_ref, first_ref, fwd_ref, spec_ref, time_ref, mid_ref):
    half = first_ref.shape[1]
    seq = h_ref.shape[1]

    def turn(i):
        time_ref[span(i, LANES), :] = h_ref[:, span(i, LANES)].T

    loop(seq // LANES, 8, turn)
    spread(lambda a: time_ref[pl.ds(a, half, stride=FAST), :].astype(BF16), first_ref, mid_ref)

    def step(p):
        spec_ref[span(p, PAIR), :] = dot(fwd_ref[p], mid_ref[span(p, PAIR), :].astype(BF16))

    loop(half // 2, U2, step)
    spec_ref[span(half // 2, PAIR), :] = dot(fwd_ref[half // 2], mid_ref[:PAIR, :].astype(BF16))


def convolve_kernel(conjugate, count, place_ref, *refs):
    x_refs, (h_any, first_ref, fwd_any, inv_any, last_ref) = refs[:count], refs[count : count + 5]
    outs, (spec_any, h_ref, fwd_ref, inv_ref, spec_ref, mid_ref, back_ref, sem) = refs[count + 5 : -8], refs[-8:]
    first_ref, last_ref = first_ref.at[0], last_ref.at[0]
    half = first_ref.shape[1]
    loads = [
        pltpu.make_async_copy(source, target, sem.at[i])
        for i, (source, target) in enumerate(((fwd_any, fwd_ref), (h_any, h_ref), (inv_any, inv_ref)))
    ]
    for load in loads:
        load.start()
    if count == 1:
        spread(lambda a: x_refs[0][:, a].reshape(half, LANES), first_ref, mid_ref)
    else:
        spread(lambda a: jnp.concatenate([x_ref[a] for x_ref in x_refs], 0), first_ref, mid_ref)
    for load in loads:
        load.wait()

    def step(p):
        x = dot(fwd_ref[p], mid_ref[span(p, PAIR), :].astype(BF16))
        spec_ref[span(p, PAIR), :] = x
        back_ref[span(p, PAIR), :] = dot(inv_ref[p], times(x, h_ref[span(p, PAIR), :], conjugate))

    loop(half // 2, U2, step)
    tail = span(half // 2, PAIR)
    x = dot(fwd_ref[half // 2], mid_ref[:PAIR, :].astype(BF16))
    spec_ref[tail, :] = x
    store = pltpu.make_async_copy(spec_ref, spec_any, sem.at[3])
    store.start()
    back_ref[:PAIR, :] += dot(inv_ref[half // 2], times(x, h_ref[tail, :], conjugate))
    if len(outs) == 1:

        def emit(a, rows):
            outs[0][:, a] = rows.reshape(outs[0].shape[0], -1, LANES).astype(BF16)

        collect(last_ref, back_ref, emit)
    else:
        per = half // len(outs)

        def emit(a, rows):
            for i, out_ref in enumerate(outs):
                out_ref[a] = rows[i * per : (i + 1) * per].astype(BF16)

        collect(last_ref, back_ref, emit)
    store.wait()


def gradient_kernel(scale, s_ref, g_ref, inv_ref, last_ref, out_ref, time_ref, back_ref):
    half = last_ref.shape[0]
    seq = out_ref.shape[1]

    def step(p):
        rows = span(p, PAIR)
        back_ref[rows, :] = dot(inv_ref[p], times(s_ref[rows, :], g_ref[rows, :], True))

    loop(half // 2, U2, step)
    tail = span(half // 2, PAIR)
    back_ref[:PAIR, :] += dot(inv_ref[half // 2], times(s_ref[tail, :], g_ref[tail, :], True))

    def emit(a, rows):
        time_ref[pl.ds(a, half, stride=FAST), :] = rows * scale

    collect(last_ref, back_ref, emit)

    def turn(i):
        out_ref[:, span(i, LANES)] = time_ref[span(i, LANES), :].T

    loop(seq // LANES, 8, turn)


def filter_spectrum(h, tabs):
    first, fwd = tabs[:2]
    seq = h.shape[1]
    return pl.pallas_call(
        filter_kernel,
        out_shape=sds((2 * seq + PAIR, LANES), F32),
        in_specs=[VM] * 3,
        out_specs=VM,
        scratch_shapes=[pltpu.VMEM((seq, LANES), F32), pltpu.VMEM((2 * seq, LANES), F32)],
        compiler_params=PARAMS,
        cost_estimate=cost(10**9, 8 * 2**20),
        name="filter_spectrum",
    )(h, first, fwd)


def convolve(index, parts, spec, tabs, conjugate, whole):
    first, fwd, inv, last = tabs
    count = len(parts)
    groups = 2 * CHIPS
    half = last.shape[1]

    def own(table):
        return pl.BlockSpec((1,) + table.shape[1:], lambda i, index: (index[0], 0, 0))

    outs = (sds((FAST, half // groups, LANES), BF16),) * groups
    if whole:
        outs = (sds((groups, FAST, half // groups, LANES), BF16),)
    big = pltpu.VMEM((spec.shape[0] - PAIR, LANES), F32)
    *out, spec = pl.pallas_call(
        functools.partial(convolve_kernel, conjugate, count),
        out_shape=outs + (sds(spec.shape, F32),),
        grid_spec=pltpu.PrefetchScalarGridSpec(
            num_scalar_prefetch=1,
            grid=(1,),
            in_specs=[VM] * count + [ANY, own(first), ANY, ANY, own(last)],
            out_specs=(VM,) * len(outs) + (ANY,),
            scratch_shapes=[
                pltpu.VMEM(spec.shape, F32),
                pltpu.VMEM(fwd.shape, BF16),
                pltpu.VMEM(fwd.shape, BF16),
                pltpu.VMEM(spec.shape, F32),
                big,
                big,
                pltpu.SemaphoreType.DMA((4,)),
            ],
        ),
        compiler_params=PARAMS,
        cost_estimate=cost(2 * 10**9, 14 * 2**20),
        name="convolve",
    )(index, *parts, spec, *tabs)
    return out, spec


def filter_gradient(scaled_spec, gated_spec, tabs, scale):
    inv, last = tabs[2:]
    seq = (scaled_spec.shape[0] - PAIR) // 2
    return pl.pallas_call(
        functools.partial(gradient_kernel, scale),
        out_shape=sds((LANES, seq), F32),
        in_specs=[VM] * 4,
        out_specs=VM,
        scratch_shapes=[pltpu.VMEM((seq, LANES), F32), pltpu.VMEM((2 * seq, LANES), F32)],
        compiler_params=PARAMS,
        cost_estimate=cost(10**9, 12 * 2**20),
        name="filter_gradient",
    )(scaled_spec, gated_spec, inv, last)


def permuted(value, hold_ref, emit):
    hold_ref[...] = value
    per = value.shape[0] // FAST
    for a in range(FAST):
        emit(a, hold_ref[pl.ds(a, per, stride=FAST), :].astype(BF16))


def gate_kernel(key_ref, value_ref, out_ref, hold_ref):
    product = key_ref[...].astype(F32) * value_ref[...].astype(F32)
    for g in range(WIDE // LANES):

        def emit(a, rows):
            out_ref[g, a] = rows

        permuted(product[:, g * LANES : (g + 1) * LANES], hold_ref, emit)


def gate(key_in, value_in, groups):
    rows, cols = key_in.shape
    block = pl.BlockSpec((rows, WIDE), lambda j: (0, j))
    return pl.pallas_call(
        gate_kernel,
        grid=(cols // WIDE,),
        out_shape=sds((groups, FAST, rows // FAST, LANES), BF16),
        in_specs=[block, block],
        out_specs=pl.BlockSpec((WIDE // LANES, FAST, rows // FAST, LANES), lambda j: (j, 0, 0, 0)),
        scratch_shapes=[pltpu.VMEM((rows, LANES), F32)],
        compiler_params=PARAMS,
        cost_estimate=cost(10**6, 3 * 2**20),
        name="gate",
    )(key_in, value_in)


WIDE = 256


def pieces_of(x_ref, piece, lane, depth):
    return x_ref[piece, :, pl.ds(pl.multiple_of(lane * depth, depth), depth)]


def against(left, w_ref):
    return lax.dot_general(left, w_ref[...], (((1,), (1,)), ((), ())), preferred_element_type=F32)


def terms_kernel(dists, place_ref, *refs):
    count = 2 * sum(1 if d == 0 else 2 for d in dists)
    xs, ws, sum_ref, x_ref, sem = refs[:4], refs[4 : 4 + count], refs[4 + count], refs[-2], refs[-1]
    mine = place_ref[2]

    @pl.when(pl.program_id(0) == 0)
    def _():
        copies = [pltpu.make_async_copy(xs[i], x_ref.at[mine ^ i], sem.at[i]) for i in range(4)]
        for copy in copies:
            copy.start()
        for copy in copies:
            copy.wait()

    here, core = place_ref[0], place_ref[1]
    depth = ws[0].shape[1]

    def part(piece, near_ref, swap_ref):
        one = against(pieces_of(x_ref, piece, core, depth), near_ref)
        return one + against(pieces_of(x_ref, piece, 1 - core, depth), swap_ref)

    for d in dists:
        if d == 0:
            sum_ref[...] = part(here, ws[0], ws[1])
            ws = ws[2:]
            continue
        up, up_swap, down, down_swap = ws[:4]
        ws = ws[4:]

        @pl.when(here >= d)
        def _():
            sum_ref[...] += part(here - d, up, up_swap)

        @pl.when(here + d < CHIPS)
        def _():
            sum_ref[...] += part(here + d, down, down_swap)


def above(d):
    return lambda j, place: (jnp.where(place[0] >= d, j, 0), 0)


def below(d):
    return lambda j, place: (jnp.where(place[0] + d < CHIPS, j, 0), 0)


def terms(dists, place, xs, ws):
    rows, piece = xs[0].shape
    cols, depth = ws[0].shape
    maps = []
    for d in dists:
        maps += [above(d), above(d)] + ([below(d), below(d)] if d else [])
    wide = pl.BlockSpec((rows, WIDE), lambda j, place: (0, j))
    return pl.pallas_call(
        functools.partial(terms_kernel, dists),
        out_shape=sds((rows, cols), F32),
        grid_spec=pltpu.PrefetchScalarGridSpec(
            num_scalar_prefetch=1,
            grid=(cols // WIDE,),
            in_specs=[ANY] * 4 + [pl.BlockSpec((WIDE, depth), m) for m in maps],
            out_specs=wide,
            scratch_shapes=[pltpu.VMEM((4, rows, piece), BF16), pltpu.SemaphoreType.DMA((4,))],
        ),
        compiler_params=PARAMS,
        cost_estimate=cost(2 * 10**9, 14 * 2**20),
        name="terms",
    )(place, *xs, *ws)


def late_kernel(place_ref, *refs):
    xs, ws, sum_ref, query_ref, mix_ref = refs[:4], refs[4:10], refs[10], refs[11], refs[12]
    outs, (hold_ref, x_ref, sem) = refs[13:-3], refs[-3:]
    here, core, mine = place_ref[0], place_ref[1], place_ref[2]
    two_ref, three_ref = x_ref.at[pl.ds(0, 1)], x_ref.at[pl.ds(1, 1)]

    @pl.when(pl.program_id(0) == 0)
    def _():
        for start in (True, False):
            for slot, piece in enumerate((here ^ 2, CHIPS - 1 - here)):
                for i in range(4):

                    @pl.when(mine ^ piece == i)
                    def _():
                        copy = pltpu.make_async_copy(xs[i], x_ref.at[slot], sem.at[slot])
                        copy.start() if start else copy.wait()

    rows = sum_ref.shape[0]
    depth = ws[0].shape[1]
    per = rows // FAST

    def part(piece_ref, near_ref, swap_ref):
        one = against(pieces_of(piece_ref, 0, core, depth), near_ref)
        return one + against(pieces_of(piece_ref, 0, 1 - core, depth), swap_ref)

    def give(total):
        mix = total.astype(BF16)
        mix_ref[...] = mix
        scaled = mix.astype(F32) * query_ref[...].astype(F32)
        for g in range(2):
            hold_ref[g] = scaled[:, g * LANES : (g + 1) * LANES]

    for place, two, last in ((0, 2, True), (1, 2, False), (2, 0, False), (3, 0, True)):

        @pl.when(here == place)
        def _():
            total = sum_ref[...] + part(two_ref, ws[two], ws[two + 1])
            give(total + part(three_ref, ws[4], ws[5]) if last else total)

    for k in range(CHIPS):

        @pl.when(pl.program_id(0) == k)
        def _():
            for e in range(2):
                for a in range(FAST):
                    outs[2 * k + e][a] = hold_ref[e ^ core, pl.ds(a, per, stride=FAST), :].astype(BF16)


def mix_late(place, xs, ws, total, query):
    rows, cols = query.shape
    depth = ws[0].shape[1]

    def block(j, place):
        return j ^ place[0]

    def above(j, place):
        return (jnp.where(place[0] >= 2, block(j, place), 0), 0)

    def below(j, place):
        return (jnp.where(place[0] < 2, block(j, place), 0), 0)

    def last(j, place):
        return (jnp.where((place[0] == 0) | (place[0] == CHIPS - 1), block(j, place), 0), 0)

    wide = pl.BlockSpec((rows, WIDE), lambda j, place: (0, block(j, place)))
    part = pl.BlockSpec((FAST, rows // FAST, LANES), lambda j, place: (0, 0, 0))
    grad_mix, *scaled = pl.pallas_call(
        late_kernel,
        out_shape=(sds((rows, cols), BF16),) + (sds((FAST, rows // FAST, LANES), BF16),) * (2 * CHIPS),
        grid_spec=pltpu.PrefetchScalarGridSpec(
            num_scalar_prefetch=1,
            grid=(CHIPS,),
            in_specs=[ANY] * 4
            + [pl.BlockSpec((WIDE, depth), m) for m in (above, above, below, below, last, last)]
            + [wide, wide],
            out_specs=(wide,) + (part,) * (2 * CHIPS),
            scratch_shapes=[
                pltpu.VMEM((2, rows, LANES), F32),
                pltpu.VMEM((2,) + xs[0].shape, BF16),
                pltpu.SemaphoreType.DMA((2,)),
            ],
        ),
        compiler_params=PARAMS,
        cost_estimate=cost(10**9, 8 * 2**20),
        name="mix_late",
    )(place, *xs, *ws, total, query)
    return grad_mix, scaled


def finish_kernel(count, place_ref, *refs):
    parts, factors, outs = refs[: 2 * CHIPS], refs[2 * CHIPS : 2 * CHIPS + count], refs[2 * CHIPS + count : -1]
    hold_ref = refs[-1]
    core = place_ref[1]
    per = parts[0].shape[1]
    for k in range(CHIPS):

        @pl.when(pl.program_id(0) == k)
        def _():
            for e in range(2):
                for a in range(FAST):
                    hold_ref[e ^ core, pl.ds(a, per, stride=FAST), :] = parts[2 * k + e][a].astype(F32)

    for g in range(2):
        lanes = pl.ds(g * LANES, LANES)
        value = hold_ref[g]
        for factor_ref, out_ref in zip(factors, outs):
            out_ref[:, lanes] = (value * factor_ref[:, lanes].astype(F32)).astype(BF16)


def finish(place, parts, *factors):
    rows, cols = factors[0].shape
    count = len(factors)
    wide = pl.BlockSpec((rows, WIDE), lambda j, place: (0, j ^ place[0]))
    part = pl.BlockSpec(parts[0].shape, lambda j, place: (0, 0, 0))
    return pl.pallas_call(
        functools.partial(finish_kernel, count),
        out_shape=(sds((rows, cols), BF16),) * count,
        grid_spec=pltpu.PrefetchScalarGridSpec(
            num_scalar_prefetch=1,
            grid=(CHIPS,),
            in_specs=[part] * (2 * CHIPS) + [wide] * count,
            out_specs=(wide,) * count,
            scratch_shapes=[pltpu.VMEM((2, rows, LANES), F32)],
        ),
        compiler_params=PARAMS,
        cost_estimate=cost(10**6, (1 + 2 * count) * 2**20),
        name="finish",
    )(place, *parts, *factors)


def finish_whole_kernel(part_ref, factor_ref, out_ref, hold_ref):
    per = part_ref.shape[2]
    for g in range(2):
        for a in range(FAST):
            hold_ref[pl.ds(a, per, stride=FAST), :] = part_ref[g, a].astype(F32)
        lanes = pl.ds(g * LANES, LANES)
        out_ref[:, lanes] = (hold_ref[...] * factor_ref[:, lanes].astype(F32)).astype(BF16)


def finish_whole(parts, factor):
    rows, cols = factor.shape
    wide = pl.BlockSpec((rows, WIDE), lambda j: (0, j))
    part = pl.BlockSpec((2,) + parts.shape[1:], lambda j: (j, 0, 0, 0))
    return pl.pallas_call(
        finish_whole_kernel,
        out_shape=sds((rows, cols), BF16),
        grid=(CHIPS,),
        in_specs=[part, wide],
        out_specs=wide,
        scratch_shapes=[pltpu.VMEM((rows, LANES), F32)],
        compiler_params=PARAMS,
        cost_estimate=cost(10**6, 3 * 2**20),
        name="finish_whole",
    )(parts, factor)


def exchange(parts):
    return lax.all_to_all(parts, "ctx", split_axis=0, concat_axis=0, tiled=True)


def scatter(parts, first=0):
    ids = range(2 * CHIPS)
    return [lax.ppermute(p, "ctx", [(i, i ^ (first + d)) for i in ids]) if first + d else p for d, p in enumerate(parts)]


SWAP = [(i, i ^ 1) for i in range(2 * CHIPS)]


def hop(low, high, d):
    up = [(i, i + 2) for i in range(2 * (d - 1), 2 * CHIPS - 2)]
    down = [(i, i - 2) for i in range(2, 2 * (CHIPS - d + 1))]
    return lax.ppermute(low, "ctx", up), lax.ppermute(high, "ctx", down)


def with_swaps(low, high, d):
    low_swap = lax.ppermute(low, "ctx", [p for p in SWAP if p[0] >= 2 * d])
    high_swap = lax.ppermute(high, "ctx", [p for p in SWAP if p[0] < 2 * (CHIPS - d)])
    return [low, low_swap, high, high_swap]


def lane_body(grad_out, proj_out, query, key_in, value_in, filters):
    seq = filters.shape[1]
    groups = seq // key_in.shape[0]
    firsts, fwd, inv, lasts = tables(seq)
    tie = lax.optimization_barrier
    ctx = lax.axis_index("ctx")
    place = jnp.stack([ctx // 2, ctx % 2, lax.axis_index("mp")]).astype(jnp.int32)
    index = ctx.astype(jnp.int32)[None]

    def across(x, d):
        return lax.ppermute(x, "mp", [(i, i ^ d) for i in range(4)])

    low1, high1 = hop(proj_out, proj_out, 1)
    x1, x2 = across(grad_out, 1), across(grad_out, 2)
    gated = exchange(gate(key_in, value_in, groups))
    spec = filter_spectrum(filters, (firsts[0], fwd))
    low1, high1, spec, own = tie((low1, high1, spec, proj_out))

    low2, high2 = hop(low1, high1, 2)
    x3, _, _ = tie((grad_out, x1, x2))
    xs = [grad_out, x1, x2, across(x3, 3)]
    (conv,), gated_spec = convolve(index * 0, [gated], spec, (firsts, fwd, inv, lasts), False, True)
    own, low1, high1, _ = tie((own, low1, high1, conv))
    ws = [own, lax.ppermute(own, "ctx", SWAP)] + with_swaps(low1, high1, 1)
    low2, high2, _ = tie((low2, high2, conv))

    end = [(i, i + 2) for i in (4, 5)] + [(i, i - 2) for i in (2, 3)]
    end_swap = [p for p in SWAP if p[0] in (0, 1, 6, 7)]
    last = lax.ppermute(jnp.where(ctx >= CHIPS, low2, high2), "ctx", end)
    total = terms((0, 1), place, xs, ws)
    conv, _ = tie((conv, total))
    conv = exchange(conv)
    ws = with_swaps(low2, high2, 2)
    last, _ = tie((last, total))
    ws += [last, lax.ppermute(last, "ctx", end_swap)]
    grad_mix, scaled = mix_late(place, xs, ws, total, query)
    scaled = scatter(scaled)
    *scaled, conv = tie((*scaled, conv))
    back, scaled_spec = convolve(index, scaled, spec, (firsts, fwd, inv, lasts), True, False)
    back = scatter(back)
    filter_grad = filter_gradient(scaled_spec, gated_spec, (None, fwd, inv, lasts[0]), 1.0 / math.sqrt(seq))
    grad_query = finish_whole(conv, grad_mix)
    grad_key, grad_value = finish(place, back, value_in, key_in)
    return (grad_query, grad_key, grad_value, filter_grad)


def body(grad_out, proj_out, query, key_in, value_in, filters):
    rows, cols = key_in.shape
    lanes, seq = filters.shape
    fits = (
        lax.axis_size("ctx") == 2 * CHIPS
        and lax.axis_size("mp") == 4
        and lanes == LANES
        and rows % (16 * FAST) == 0
        and cols == 2 * CHIPS * LANES
        and seq == 2 * CHIPS * rows
        and seq == FAST * LANES
        and grad_out.shape[1] == 2 * proj_out.shape[1]
    )
    args = (grad_out, proj_out, query, key_in, value_in, filters)
    return lane_body(*args) if fits else general_body(*args)


def solution(mesh):
    return jax.shard_map(
        body,
        mesh=mesh,
        in_specs=(
            P("ctx", "mp"),
            P("mp", "ctx"),
            P("ctx", "mp"),
            P("ctx", "mp"),
            P("ctx", "mp"),
            P(("mp", "ctx"), None),
        ),
        out_specs=(P("ctx", "mp"), P("ctx", "mp"), P("ctx", "mp"), P(("mp", "ctx"), None)),
        check_vma=False,
    )
```

```python
import functools
import math

import jax
import jax.numpy as jnp
import ml_dtypes
import numpy as np
from jax import lax
from jax.experimental import pallas as pl
from jax.experimental.pallas import tpu as pltpu
from jax.sharding import PartitionSpec as P


def phase_table(rows_n, cols_n, modulus):
    prod_idx = (
        jnp.arange(rows_n, dtype=jnp.int32)[:, None]
        * jnp.arange(cols_n, dtype=jnp.int32)[None, :]
        % modulus
    )
    angles = prod_idx.astype(jnp.float32) * (2.0 * math.pi / modulus)
    return (jnp.cos(angles), jnp.sin(angles))


def make_tables(length_all):
    size_second = min(128, length_all)
    size_first = length_all // size_second
    cos_first, sin_first = phase_table(size_first, size_first, size_first)
    twist_cos, twist_sin = phase_table(size_first, size_second, length_all)
    cos_second, sin_second = phase_table(size_second, size_second, size_second)
    return (cos_first, sin_first, twist_cos, twist_sin, cos_second, sin_second)


def contract(form, left, right):
    return jnp.einsum(form, left, right, precision=lax.Precision.HIGHEST)


def forward_real(signal, tables):
    cos_first, sin_first, twist_cos, twist_sin, cos_second, sin_second = tables
    part_re = contract("kn,cnm->ckm", cos_first, signal)
    part_im = -contract("kn,cnm->ckm", sin_first, signal)
    turned_re = part_re * twist_cos + part_im * twist_sin
    turned_im = part_im * twist_cos - part_re * twist_sin
    spec_re = contract("ckm,mj->ckj", turned_re, cos_second) + contract(
        "ckm,mj->ckj", turned_im, sin_second
    )
    spec_im = contract("ckm,mj->ckj", turned_im, cos_second) - contract(
        "ckm,mj->ckj", turned_re, sin_second
    )
    return (spec_re, spec_im)


def inverse_real(spec_re, spec_im, tables):
    cos_first, sin_first, twist_cos, twist_sin, cos_second, sin_second = tables
    back_re = contract("ckj,jm->ckm", spec_re, cos_second) - contract(
        "ckj,jm->ckm", spec_im, sin_second
    )
    back_im = contract("ckj,jm->ckm", spec_re, sin_second) + contract(
        "ckj,jm->ckm", spec_im, cos_second
    )
    twist_re = back_re * twist_cos - back_im * twist_sin
    twist_im = back_re * twist_sin + back_im * twist_cos
    return contract("nk,ckm->cnm", cos_first, twist_re) - contract(
        "nk,ckm->cnm", sin_first, twist_im
    )


def long_filter_grads(gated, scaled, kernel):
    channels, seq_len = kernel.shape
    length_all = 2 * seq_len
    tables = make_tables(length_all)
    spec_shape = (channels, tables[0].shape[0], tables[4].shape[0])

    def padded(values):
        wide = jnp.concatenate(
            [values.astype(jnp.float32), jnp.zeros((channels, seq_len), jnp.float32)], axis=1
        )
        return wide.reshape(spec_shape)

    def restore(spec_re, spec_im):
        return (
            inverse_real(spec_re, spec_im, tables).reshape(channels, length_all)[:, :seq_len]
            / length_all
        )

    gated_re, gated_im = forward_real(padded(gated), tables)
    scaled_re, scaled_im = forward_real(padded(scaled), tables)
    kernel_re, kernel_im = forward_real(padded(kernel), tables)
    conv_out = restore(
        kernel_re * gated_re - kernel_im * gated_im, kernel_re * gated_im + kernel_im * gated_re
    )
    grad_gated = restore(
        scaled_re * kernel_re + scaled_im * kernel_im, scaled_im * kernel_re - scaled_re * kernel_im
    )
    grad_kernel = restore(
        scaled_re * gated_re + scaled_im * gated_im, scaled_im * gated_re - scaled_re * gated_im
    )
    filter_grad = grad_kernel / math.sqrt(seq_len)
    return (conv_out.astype(jnp.bfloat16), grad_gated.astype(jnp.bfloat16), filter_grad)


def product(left, right):
    return (left.astype(jnp.float32) * right.astype(jnp.float32)).astype(jnp.bfloat16)


def general_body(grad_out, proj_out, query, key_in, value_in, filters):
    weight_rows = lax.all_gather(proj_out, "ctx", axis=1, tiled=True)
    grad_mix = lax.dot_general(
        lax.all_gather(grad_out, "mp", axis=1, tiled=True),
        weight_rows,
        (((1,), (1,)), ((), ())),
        preferred_element_type=jnp.float32,
    ).astype(jnp.bfloat16)
    gated = product(key_in, value_in)
    scaled = product(grad_mix, query)
    chan_gated, chan_scaled = (
        lax.all_to_all(gated.T, "ctx", split_axis=0, concat_axis=1, tiled=True),
        lax.all_to_all(scaled.T, "ctx", split_axis=0, concat_axis=1, tiled=True),
    )
    conv_out, grad_gated, filter_grad = long_filter_grads(chan_gated, chan_scaled, filters)
    back_grad, back_conv = (
        lax.all_to_all(grad_gated, "ctx", split_axis=1, concat_axis=0, tiled=True),
        lax.all_to_all(conv_out, "ctx", split_axis=1, concat_axis=0, tiled=True),
    )
    grad_query = product(grad_mix, back_conv.T)
    grad_key = product(back_grad.T, value_in)
    grad_value = product(back_grad.T, key_in)
    return (grad_query, grad_key, grad_value, filter_grad)


FAST = 32
SLOT = 2 * FAST
PAIR = 2 * SLOT
STEP = SLOT + 8
GAP = FAST + 8
LANES = 128
CHIPS = 4
OUTWARD = (4, 5, 6, 7, 2, 3, 1, 0)
HOMEWARD = (2, 3, 6, 7, 4, 5, 1, 0)
F32, BF16 = jnp.float32, jnp.bfloat16
PARAMS = pltpu.CompilerParams(vmem_limit_bytes=60 * 2**20)
VM = pl.BlockSpec(memory_space=pltpu.VMEM)
ANY = pl.BlockSpec(memory_space=pl.ANY)
U1, U2 = 16, 32


def sds(shape, dtype):
    return jax.ShapeDtypeStruct(shape, dtype)


def cost(flops, moved):
    return pl.CostEstimate(flops=flops // 10**6, bytes_accessed=moved // 10**3, transcendentals=0)


def tables(seq):
    size = 2 * seq
    slow = size // FAST
    half = slow // 2
    s = np.arange(half)
    angle = 2 * np.pi * ((s[:, None] * s[None, :]) % slow) / slow
    first = np.concatenate([np.cos(angle), -np.sin(angle)], 0)
    first[half] = 1.0 - 2.0 * (s % 2)
    weight = np.full((2 * half, 1), 2.0)
    weight[0] = weight[half] = 1.0
    last = (first * weight).T / size
    a = np.arange(FAST)
    k = np.arange(half + 1)[:, None] + slow * a[None, :]
    turn = 2 * np.pi * ((k[:, :, None] * a[None, None, :]) % size) / size
    c, d = np.cos(turn), np.sin(turn)
    fwd = np.concatenate([np.concatenate([c, d], 2), np.concatenate([-d, c], 2)], 1)
    inv = fwd.transpose(0, 2, 1).copy()
    fwd[0, :, FAST:] = 0.0
    inv[0, FAST:] = 0.0

    def paired(blocks):
        out = np.zeros((half // 2 + 1, SLOT, PAIR))
        out[:-1, :, :SLOT] = blocks[0:half:2]
        out[:-1, :, SLOT:] = blocks[1:half:2]
        return out

    fwd, inv, edge_fwd, edge_inv = paired(fwd), paired(inv), fwd[half], inv[half]
    fwd[-1, :, FAST:SLOT] = edge_fwd[:, :FAST]
    inv[-1, FAST:, :SLOT] = edge_inv[:FAST]
    blocks = np.arange(half).reshape(2 * CHIPS, -1)

    def orders(reach):
        return [np.concatenate([blocks[c ^ d] for d in reach]) for c in range(2 * CHIPS)] + [np.arange(half)]

    firsts = np.stack([first[:, o] for o in orders(OUTWARD)])
    lasts = np.stack([last[o] for o in orders(HOMEWARD)])
    return [jnp.asarray(t.astype(ml_dtypes.bfloat16)) for t in (firsts, fwd, inv, lasts)]


def dot(left, right):
    return jnp.dot(left, right, preferred_element_type=F32)


def pair_dot(pair, rows):
    low = lax.broadcasted_iota(jnp.int32, pair.shape, 1) < SLOT
    zero = jnp.zeros_like(pair)
    return dot(jnp.concatenate([jnp.where(low, pair, zero), jnp.where(low, zero, pair)], 0), rows)


def loop(count, unroll, step):
    def some(i, carry):
        for u in range(unroll):
            step(i * unroll + u)
        return carry

    lax.fori_loop(0, count // unroll, some, 0)


def span(start, size):
    return pl.ds(pl.multiple_of(start * size, size), size)


def slots(ref, p):
    return [ref.at[pl.ds(pl.multiple_of(p * 2 * STEP + i * STEP, 8), SLOT), :] for i in range(2)]


def read_slots(ref, p):
    return jnp.concatenate([rows[...] for rows in slots(ref, p)], 0).astype(BF16)


def write_slots(ref, p, value):
    for i, rows in enumerate(slots(ref, p)):
        rows[...] = value[i * SLOT : (i + 1) * SLOT]


def gapped(ref, index, count):
    return [ref.at[pl.ds(pl.multiple_of((index * count + i) * GAP, 8), FAST), :] for i in range(count)]


def read_gapped(ref, index, count):
    return jnp.concatenate([rows[...] for rows in gapped(ref, index, count)], 0)


def write_gapped(ref, index, value):
    for i, rows in enumerate(gapped(ref, index, value.shape[0] // FAST)):
        rows[...] = value[i * FAST : (i + 1) * FAST]


def spread(signal, first_ref, mid_ref):
    half = first_ref.shape[1]

    def step(a):
        out = dot(first_ref[...], signal(a))
        mid_ref[pl.ds(a, half, stride=STEP), :] = out[:half]
        mid_ref[pl.ds(FAST + a, half, stride=STEP), :] = out[half:]

    loop(FAST, U1, step)


def collect(last_ref, back_ref, emit):
    half = last_ref.shape[0]

    def step(a):
        re = back_ref[pl.ds(a, half, stride=STEP), :]
        im = back_ref[pl.ds(FAST + a, half, stride=STEP), :]
        emit(a, dot(last_ref[...], jnp.concatenate([re, im], 0).astype(BF16)))

    loop(FAST, U1, step)


def times(x, y, conjugate):
    x, y = x.astype(F32), y.astype(F32)
    parts = []
    for i in range(0, x.shape[0], SLOT):
        xr, xi, yr, yi = (v[i + j : i + j + FAST] for v in (x, y) for j in (0, FAST))
        if conjugate:
            parts += [xr * yr + xi * yi, xi * yr - xr * yi]
        else:
            parts += [xr * yr - xi * yi, xr * yi + xi * yr]
    return jnp.concatenate(parts, 0).astype(BF16)


def filter_kernel(h_ref, first_ref, fwd_ref, spec_ref, time_ref, mid_ref):
    half = first_ref.shape[1]
    seq = h_ref.shape[1]

    def turn(i):
        write_gapped(time_ref, i, h_ref[:, span(i, LANES)].T)

    loop(seq // LANES, 8, turn)
    spread(lambda a: time_ref[pl.ds(a, half, stride=GAP), :].astype(BF16), first_ref, mid_ref)

    def step(p):
        spec_ref[span(p, PAIR), :] = pair_dot(fwd_ref[p], read_slots(mid_ref, p)).astype(BF16)

    loop(half // 2, U2, step)
    spec_ref[span(half // 2, PAIR), :] = pair_dot(fwd_ref[half // 2], read_slots(mid_ref, 0)).astype(BF16)


def convolve_kernel(conjugate, count, place_ref, *refs):
    x_refs, (h_any, first_ref, fwd_any, inv_any, last_ref) = refs[:count], refs[count : count + 5]
    outs, (spec_any, h_ref, fwd_ref, inv_ref, spec_ref, mid_ref, back_ref, sem) = refs[count + 5 : -8], refs[-8:]
    first_ref, last_ref = first_ref.at[0], last_ref.at[0]
    half = first_ref.shape[1]
    loads = [
        pltpu.make_async_copy(source, target, sem.at[i])
        for i, (source, target) in enumerate(((fwd_any, fwd_ref), (h_any, h_ref), (inv_any, inv_ref)))
    ]
    for load in loads:
        load.start()
    if count == 1:
        spread(lambda a: x_refs[0][:, a].reshape(half, LANES), first_ref, mid_ref)
    else:
        spread(lambda a: jnp.concatenate([x_ref[a] for x_ref in x_refs], 0), first_ref, mid_ref)
    for load in loads:
        load.wait()

    def step(p):
        x = pair_dot(fwd_ref[p], read_slots(mid_ref, p))
        spec_ref[span(p, PAIR), :] = x.astype(BF16)
        write_slots(back_ref, p, pair_dot(inv_ref[p], times(x, h_ref[span(p, PAIR), :], conjugate)))

    loop(half // 2, U2, step)
    tail = span(half // 2, PAIR)
    x = pair_dot(fwd_ref[half // 2], read_slots(mid_ref, 0))
    spec_ref[tail, :] = x.astype(BF16)
    store = pltpu.make_async_copy(spec_ref, spec_any, sem.at[3])
    store.start()
    back_ref[:SLOT, :] += pair_dot(inv_ref[half // 2], times(x, h_ref[tail, :], conjugate))[:SLOT]
    if len(outs) == 1:

        def emit(a, rows):
            outs[0][:, a] = rows.reshape(outs[0].shape[0], -1, LANES).astype(BF16)

        collect(last_ref, back_ref, emit)
    else:
        per = half // len(outs)

        def emit(a, rows):
            for i, out_ref in enumerate(outs):
                out_ref[a] = rows[i * per : (i + 1) * per].astype(BF16)

        collect(last_ref, back_ref, emit)
    store.wait()


def gradient_kernel(scale, s_ref, g_ref, inv_ref, last_ref, out_ref, time_ref, back_ref):
    half = last_ref.shape[0]
    seq = out_ref.shape[1]

    def step(p):
        rows = span(p, PAIR)
        write_slots(back_ref, p, pair_dot(inv_ref[p], times(s_ref[rows, :], g_ref[rows, :], True)))

    loop(half // 2, U2, step)
    tail = span(half // 2, PAIR)
    back_ref[:SLOT, :] += pair_dot(inv_ref[half // 2], times(s_ref[tail, :], g_ref[tail, :], True))[:SLOT]

    def emit(a, rows):
        time_ref[pl.ds(a, half, stride=GAP), :] = rows * scale

    collect(last_ref, back_ref, emit)

    def turn(i):
        out_ref[:, span(i, LANES)] = read_gapped(time_ref, i, LANES // FAST).T

    loop(seq // LANES, 8, turn)


def filter_spectrum(h, tabs):
    first, fwd = tabs[:2]
    seq = h.shape[1]
    return pl.pallas_call(
        filter_kernel,
        out_shape=sds((2 * seq + PAIR, LANES), BF16),
        in_specs=[VM] * 3,
        out_specs=VM,
        scratch_shapes=[pltpu.VMEM((seq // FAST * GAP, LANES), F32), pltpu.VMEM((seq // FAST * STEP, LANES), F32)],
        compiler_params=PARAMS,
        cost_estimate=cost(10**9, 8 * 2**20),
        name="filter_spectrum",
    )(h, first, fwd)


def convolve(index, parts, spec, tabs, conjugate, whole):
    first, fwd, inv, last = tabs
    count = len(parts)
    groups = 2 * CHIPS
    half = last.shape[1]

    def own(table):
        return pl.BlockSpec((1,) + table.shape[1:], lambda i, index: (index[0], 0, 0))

    outs = (sds((FAST, half // groups, LANES), BF16),) * groups
    if whole:
        outs = (sds((groups, FAST, half // groups, LANES), BF16),)
    big = pltpu.VMEM((half * STEP, LANES), F32)
    *out, spec = pl.pallas_call(
        functools.partial(convolve_kernel, conjugate, count),
        out_shape=outs + (sds(spec.shape, BF16),),
        grid_spec=pltpu.PrefetchScalarGridSpec(
            num_scalar_prefetch=1,
            grid=(1,),
            in_specs=[VM] * count + [ANY, own(first), ANY, ANY, own(last)],
            out_specs=(VM,) * len(outs) + (ANY,),
            scratch_shapes=[
                pltpu.VMEM(spec.shape, BF16),
                pltpu.VMEM(fwd.shape, BF16),
                pltpu.VMEM(fwd.shape, BF16),
                pltpu.VMEM(spec.shape, BF16),
                big,
                big,
                pltpu.SemaphoreType.DMA((4,)),
            ],
        ),
        compiler_params=PARAMS,
        cost_estimate=cost(2 * 10**9, 14 * 2**20),
        name="convolve",
    )(index, *parts, spec, *tabs)
    return out, spec


def filter_gradient(scaled_spec, gated_spec, tabs, scale):
    inv, last = tabs[2:]
    seq = (scaled_spec.shape[0] - PAIR) // 2
    return pl.pallas_call(
        functools.partial(gradient_kernel, scale),
        out_shape=sds((LANES, seq), F32),
        in_specs=[VM] * 4,
        out_specs=VM,
        scratch_shapes=[pltpu.VMEM((seq // FAST * GAP, LANES), F32), pltpu.VMEM((seq // FAST * STEP, LANES), F32)],
        compiler_params=PARAMS,
        cost_estimate=cost(10**9, 12 * 2**20),
        name="filter_gradient",
    )(scaled_spec, gated_spec, inv, last)


def permuted(value, hold_ref, emit):
    write_gapped(hold_ref, 0, value)
    per = value.shape[0] // FAST
    for a in range(FAST):
        emit(a, hold_ref[pl.ds(a, per, stride=GAP), :].astype(BF16))


def gate_kernel(key_ref, value_ref, out_ref, hold_ref):
    product = key_ref[...].astype(F32) * value_ref[...].astype(F32)
    for g in range(WIDE // LANES):

        def emit(a, rows):
            out_ref[g, a] = rows

        permuted(product[:, g * LANES : (g + 1) * LANES], hold_ref, emit)


def gate(key_in, value_in, groups):
    rows, cols = key_in.shape
    block = pl.BlockSpec((rows, WIDE), lambda j: (0, j))
    return pl.pallas_call(
        gate_kernel,
        grid=(cols // WIDE,),
        out_shape=sds((groups, FAST, rows // FAST, LANES), BF16),
        in_specs=[block, block],
        out_specs=pl.BlockSpec((WIDE // LANES, FAST, rows // FAST, LANES), lambda j: (j, 0, 0, 0)),
        scratch_shapes=[pltpu.VMEM((rows // FAST * GAP, LANES), F32)],
        compiler_params=PARAMS,
        cost_estimate=cost(10**6, 3 * 2**20),
        name="gate",
    )(key_in, value_in)


WIDE = 256
BATCH = 4


def pieces_of(x_ref, piece, lane, depth):
    return x_ref[piece, :, pl.ds(pl.multiple_of(lane * depth, depth), depth)]


def against(left, w_ref):
    return lax.dot_general(left, w_ref[...], (((1,), (1,)), ((), ())), preferred_element_type=F32)


def terms_kernel(dists, place_ref, *refs):
    count = 2 * sum(1 if d == 0 else 2 for d in dists)
    xs, ws, sum_ref, x_ref, sem = refs[:4], refs[4 : 4 + count], refs[4 + count], refs[-2], refs[-1]
    here, core, mine = place_ref[0], place_ref[1], place_ref[2]

    @pl.when(pl.program_id(0) == 0)
    def _():
        for start in (True, False):
            for i in range(4):

                @pl.when(jnp.abs((mine ^ i) - here) <= dists[-1])
                def _():
                    copy = pltpu.make_async_copy(xs[i], x_ref.at[mine ^ i], sem.at[i])
                    copy.start() if start else copy.wait()

    depth = ws[0].shape[1]

    def part(piece, near_ref, swap_ref):
        one = against(pieces_of(x_ref, piece, core, depth), near_ref)
        return one + against(pieces_of(x_ref, piece, 1 - core, depth), swap_ref)

    for d in dists:
        if d == 0:
            sum_ref[...] = part(here, ws[0], ws[1])
            ws = ws[2:]
            continue
        up, up_swap, down, down_swap = ws[:4]
        ws = ws[4:]

        @pl.when(here >= d)
        def _():
            sum_ref[...] += part(here - d, up, up_swap)

        @pl.when(here + d < CHIPS)
        def _():
            sum_ref[...] += part(here + d, down, down_swap)


def above(d):
    return lambda j, place: (jnp.where(place[0] >= d, j, 0), 0)


def below(d):
    return lambda j, place: (jnp.where(place[0] + d < CHIPS, j, 0), 0)


def terms(dists, place, xs, ws):
    rows, piece = xs[0].shape
    cols, depth = ws[0].shape
    maps = []
    for d in dists:
        maps += [above(d), above(d)] + ([below(d), below(d)] if d else [])
    wide = pl.BlockSpec((rows, WIDE), lambda j, place: (0, j))
    return pl.pallas_call(
        functools.partial(terms_kernel, dists),
        out_shape=sds((rows, cols), F32),
        grid_spec=pltpu.PrefetchScalarGridSpec(
            num_scalar_prefetch=1,
            grid=(cols // WIDE,),
            in_specs=[ANY] * 4 + [pl.BlockSpec((WIDE, depth), m) for m in maps],
            out_specs=wide,
            scratch_shapes=[pltpu.VMEM((4, rows, piece), BF16), pltpu.SemaphoreType.DMA((4,))],
        ),
        compiler_params=PARAMS,
        cost_estimate=cost(2 * 10**9, 14 * 2**20),
        name="terms",
    )(place, *xs, *ws)


def late_kernel(place_ref, *refs):
    xs, ws, sum_ref, query_ref, mix_ref = refs[:4], refs[4:10], refs[10], refs[11], refs[12]
    outs, (hold_ref, x_ref, sem) = refs[13:-3], refs[-3:]
    here, core, mine = place_ref[0], place_ref[1], place_ref[2]
    two_ref, three_ref = x_ref.at[pl.ds(0, 1)], x_ref.at[pl.ds(1, 1)]

    @pl.when(pl.program_id(0) == 0)
    def _():
        for start in (True, False):
            for slot, piece in enumerate((here ^ 2, CHIPS - 1 - here)):
                for i in range(4):

                    @pl.when(mine ^ piece == i)
                    def _():
                        copy = pltpu.make_async_copy(xs[i], x_ref.at[slot], sem.at[slot])
                        copy.start() if start else copy.wait()

    rows = sum_ref.shape[0]
    depth = ws[0].shape[1]
    per = rows // FAST

    def part(piece_ref, near_ref, swap_ref):
        one = against(pieces_of(piece_ref, 0, core, depth), near_ref)
        return one + against(pieces_of(piece_ref, 0, 1 - core, depth), swap_ref)

    def give(total):
        mix = total.astype(BF16)
        mix_ref[...] = mix
        scaled = mix.astype(F32) * query_ref[...].astype(F32)
        for g in range(BATCH):
            write_gapped(hold_ref.at[g], 0, scaled[:, g * LANES : (g + 1) * LANES])

    for place, two, last in ((0, 2, True), (1, 2, False), (2, 0, False), (3, 0, True)):

        @pl.when(here == place)
        def _():
            total = sum_ref[...] + part(two_ref, ws[two], ws[two + 1])
            give(total + part(three_ref, ws[4], ws[5]) if last else total)

    for k in range(2 * CHIPS // BATCH):

        @pl.when(pl.program_id(0) == k)
        def _():
            for e in range(BATCH):
                for a in range(FAST):
                    outs[OUTWARD.index(BATCH * k + e)][a] = hold_ref[e ^ (place_ref[3] % BATCH), pl.ds(a, per, stride=GAP), :].astype(BF16)


def mix_late(place, xs, ws, total, query):
    rows, cols = query.shape
    depth = ws[0].shape[1]

    def block(j, place):
        return j ^ (place[3] // BATCH)

    def above(j, place):
        return (jnp.where(place[0] >= 2, block(j, place), 0), 0)

    def below(j, place):
        return (jnp.where(place[0] < 2, block(j, place), 0), 0)

    def last(j, place):
        return (jnp.where((place[0] == 0) | (place[0] == CHIPS - 1), block(j, place), 0), 0)

    wide = pl.BlockSpec((rows, BATCH * LANES), lambda j, place: (0, block(j, place)))
    part = pl.BlockSpec((FAST, rows // FAST, LANES), lambda j, place: (0, 0, 0))
    grad_mix, *scaled = pl.pallas_call(
        late_kernel,
        out_shape=(sds((rows, cols), BF16),) + (sds((FAST, rows // FAST, LANES), BF16),) * (2 * CHIPS),
        grid_spec=pltpu.PrefetchScalarGridSpec(
            num_scalar_prefetch=1,
            grid=(2 * CHIPS // BATCH,),
            in_specs=[ANY] * 4
            + [pl.BlockSpec((BATCH * LANES, depth), m) for m in (above, above, below, below, last, last)]
            + [wide, wide],
            out_specs=(wide,) + (part,) * (2 * CHIPS),
            scratch_shapes=[
                pltpu.VMEM((BATCH, rows // FAST * GAP, LANES), F32),
                pltpu.VMEM((2,) + xs[0].shape, BF16),
                pltpu.SemaphoreType.DMA((2,)),
            ],
        ),
        compiler_params=PARAMS,
        cost_estimate=cost(10**9, 8 * 2**20),
        name="mix_late",
    )(place, *xs, *ws, total, query)
    return grad_mix, scaled


def finish_kernel(count, place_ref, *refs):
    parts, factors, outs = refs[: 2 * CHIPS], refs[2 * CHIPS : 2 * CHIPS + count], refs[2 * CHIPS + count : -1]
    hold_ref = refs[-1]
    here = place_ref[3] % BATCH
    per = parts[0].shape[1]
    for k in range(2 * CHIPS // BATCH):

        @pl.when(pl.program_id(0) == k)
        def _():
            for e in range(BATCH):
                for a in range(FAST):
                    hold_ref[e ^ here, pl.ds(a, per, stride=GAP), :] = parts[HOMEWARD.index(BATCH * k + e)][a].astype(F32)

    for g in range(BATCH):
        lanes = pl.ds(g * LANES, LANES)
        value = read_gapped(hold_ref.at[g], 0, per)
        for factor_ref, out_ref in zip(factors, outs):
            out_ref[:, lanes] = (value * factor_ref[:, lanes].astype(F32)).astype(BF16)


def finish(place, parts, *factors):
    rows, cols = factors[0].shape
    count = len(factors)
    block = pl.BlockSpec((rows, BATCH * LANES), lambda j, place: (0, j ^ (place[3] // BATCH)))
    part = pl.BlockSpec(parts[0].shape, lambda j, place: (0, 0, 0))
    return pl.pallas_call(
        functools.partial(finish_kernel, count),
        out_shape=(sds((rows, cols), BF16),) * count,
        grid_spec=pltpu.PrefetchScalarGridSpec(
            num_scalar_prefetch=1,
            grid=(2 * CHIPS // BATCH,),
            in_specs=[part] * (2 * CHIPS) + [block] * count,
            out_specs=(block,) * count,
            scratch_shapes=[pltpu.VMEM((BATCH, rows // FAST * GAP, LANES), F32)],
        ),
        compiler_params=PARAMS,
        cost_estimate=cost(10**6, (1 + 2 * count) * 2**20),
        name="finish",
    )(place, *parts, *factors)


def finish_whole_kernel(part_ref, factor_ref, out_ref, hold_ref):
    per = part_ref.shape[2]
    for g in range(2):
        for a in range(FAST):
            hold_ref[pl.ds(a, per, stride=GAP), :] = part_ref[g, a].astype(F32)
        lanes = pl.ds(g * LANES, LANES)
        out_ref[:, lanes] = (read_gapped(hold_ref, 0, per) * factor_ref[:, lanes].astype(F32)).astype(BF16)


def finish_whole(parts, factor):
    rows, cols = factor.shape
    wide = pl.BlockSpec((rows, WIDE), lambda j: (0, j))
    part = pl.BlockSpec((2,) + parts.shape[1:], lambda j: (j, 0, 0, 0))
    return pl.pallas_call(
        finish_whole_kernel,
        out_shape=sds((rows, cols), BF16),
        grid=(CHIPS,),
        in_specs=[part, wide],
        out_specs=wide,
        scratch_shapes=[pltpu.VMEM((rows // FAST * GAP, LANES), F32)],
        compiler_params=PARAMS,
        cost_estimate=cost(10**6, 3 * 2**20),
        name="finish_whole",
    )(parts, factor)


def exchange(parts):
    return lax.all_to_all(parts, "ctx", split_axis=0, concat_axis=0, tiled=True)


def scatter(parts, reach):
    ids = range(2 * CHIPS)
    return [lax.ppermute(part, "ctx", [(i, i ^ d) for i in ids]) if d else part for part, d in zip(parts, reach)]


SWAP = [(i, i ^ 1) for i in range(2 * CHIPS)]


def hop(low, high, d):
    up = [(i, i + 2) for i in range(2 * (d - 1), 2 * CHIPS - 2)]
    down = [(i, i - 2) for i in range(2, 2 * (CHIPS - d + 1))]
    return lax.ppermute(low, "ctx", up), lax.ppermute(high, "ctx", down)


def with_swaps(low, high, d):
    low_swap = lax.ppermute(low, "ctx", [p for p in SWAP if p[0] >= 2 * d])
    high_swap = lax.ppermute(high, "ctx", [p for p in SWAP if p[0] < 2 * (CHIPS - d)])
    return [low, low_swap, high, high_swap]


def lane_body(grad_out, proj_out, query, key_in, value_in, filters):
    seq = filters.shape[1]
    groups = seq // key_in.shape[0]
    firsts, fwd, inv, lasts = tables(seq)
    tie = lax.optimization_barrier
    ctx = lax.axis_index("ctx")
    place = jnp.stack([ctx // 2, ctx % 2, lax.axis_index("mp"), ctx]).astype(jnp.int32)
    index = ctx.astype(jnp.int32)[None]

    def across(x, d):
        return lax.ppermute(x, "mp", [(i, i ^ d) for i in range(4)])

    low1, high1 = hop(proj_out, proj_out, 1)
    x1, x2 = across(grad_out, 1), across(grad_out, 2)
    gated = exchange(gate(key_in, value_in, groups))
    spec = filter_spectrum(filters, (firsts[-1], fwd))
    low1, high1, spec, own = tie((low1, high1, spec, proj_out))

    low2, high2 = hop(low1, high1, 2)
    x3, _, _ = tie((grad_out, x1, x2))
    xs = [grad_out, x1, x2, across(x3, 3)]
    (conv,), gated_spec = convolve(jnp.full_like(index, 2 * CHIPS), [gated], spec, (firsts, fwd, inv, lasts), False, True)
    own, low1, high1, _ = tie((own, low1, high1, conv))
    ws = [own, lax.ppermute(own, "ctx", SWAP)] + with_swaps(low1, high1, 1)
    low2, high2, _ = tie((low2, high2, conv))

    end = [(i, i + 2) for i in (4, 5)] + [(i, i - 2) for i in (2, 3)]
    end_swap = [p for p in SWAP if p[0] in (0, 1, 6, 7)]
    last = lax.ppermute(jnp.where(ctx >= CHIPS, low2, high2), "ctx", end)
    total = terms((0, 1), place, xs, ws)
    conv, _ = tie((conv, total))
    conv = exchange(conv)
    ws = with_swaps(low2, high2, 2)
    last, _ = tie((last, total))
    ws += [last, lax.ppermute(last, "ctx", end_swap)]
    grad_mix, scaled = mix_late(place, xs, ws, total, query)
    scaled = scatter(scaled, OUTWARD)
    *scaled, conv = tie((*scaled, conv))
    back, scaled_spec = convolve(index, scaled, spec, (firsts, fwd, inv, lasts), True, False)
    back = scatter(back, HOMEWARD)
    filter_grad = filter_gradient(scaled_spec, gated_spec, (None, fwd, inv, lasts[-1]), 1.0 / math.sqrt(seq))
    grad_query = finish_whole(conv, grad_mix)
    grad_key, grad_value = finish(place, back, value_in, key_in)
    return (grad_query, grad_key, grad_value, filter_grad)


def body(grad_out, proj_out, query, key_in, value_in, filters):
    rows, cols = key_in.shape
    lanes, seq = filters.shape
    fits = (
        lax.axis_size("ctx") == 2 * CHIPS
        and lax.axis_size("mp") == 4
        and lanes == LANES
        and rows % (16 * FAST) == 0
        and cols == 2 * CHIPS * LANES
        and seq == 2 * CHIPS * rows
        and seq == FAST * LANES
        and grad_out.shape[1] == 2 * proj_out.shape[1]
    )
    args = (grad_out, proj_out, query, key_in, value_in, filters)
    return lane_body(*args) if fits else general_body(*args)


def solution(mesh):
    return jax.shard_map(
        body,
        mesh=mesh,
        in_specs=(
            P("ctx", "mp"),
            P("mp", "ctx"),
            P("ctx", "mp"),
            P("ctx", "mp"),
            P("ctx", "mp"),
            P(("mp", "ctx"), None),
        ),
        out_specs=(P("ctx", "mp"), P("ctx", "mp"), P("ctx", "mp"), P(("mp", "ctx"), None)),
        check_vma=False,
    )
```

```python
import functools
import math

import jax
import jax.numpy as jnp
import ml_dtypes
import numpy as np
from jax import lax
from jax.experimental import pallas as pl
from jax.experimental.pallas import tpu as pltpu
from jax.sharding import PartitionSpec as P


def phase_table(rows_n, cols_n, modulus):
    prod_idx = (
        jnp.arange(rows_n, dtype=jnp.int32)[:, None]
        * jnp.arange(cols_n, dtype=jnp.int32)[None, :]
        % modulus
    )
    angles = prod_idx.astype(jnp.float32) * (2.0 * math.pi / modulus)
    return (jnp.cos(angles), jnp.sin(angles))


def make_tables(length_all):
    size_second = min(128, length_all)
    size_first = length_all // size_second
    cos_first, sin_first = phase_table(size_first, size_first, size_first)
    twist_cos, twist_sin = phase_table(size_first, size_second, length_all)
    cos_second, sin_second = phase_table(size_second, size_second, size_second)
    return (cos_first, sin_first, twist_cos, twist_sin, cos_second, sin_second)


def contract(form, left, right):
    return jnp.einsum(form, left, right, precision=lax.Precision.HIGHEST)


def forward_real(signal, tables):
    cos_first, sin_first, twist_cos, twist_sin, cos_second, sin_second = tables
    part_re = contract("kn,cnm->ckm", cos_first, signal)
    part_im = -contract("kn,cnm->ckm", sin_first, signal)
    turned_re = part_re * twist_cos + part_im * twist_sin
    turned_im = part_im * twist_cos - part_re * twist_sin
    spec_re = contract("ckm,mj->ckj", turned_re, cos_second) + contract(
        "ckm,mj->ckj", turned_im, sin_second
    )
    spec_im = contract("ckm,mj->ckj", turned_im, cos_second) - contract(
        "ckm,mj->ckj", turned_re, sin_second
    )
    return (spec_re, spec_im)


def inverse_real(spec_re, spec_im, tables):
    cos_first, sin_first, twist_cos, twist_sin, cos_second, sin_second = tables
    back_re = contract("ckj,jm->ckm", spec_re, cos_second) - contract(
        "ckj,jm->ckm", spec_im, sin_second
    )
    back_im = contract("ckj,jm->ckm", spec_re, sin_second) + contract(
        "ckj,jm->ckm", spec_im, cos_second
    )
    twist_re = back_re * twist_cos - back_im * twist_sin
    twist_im = back_re * twist_sin + back_im * twist_cos
    return contract("nk,ckm->cnm", cos_first, twist_re) - contract(
        "nk,ckm->cnm", sin_first, twist_im
    )


def long_filter_grads(gated, scaled, kernel):
    channels, seq_len = kernel.shape
    length_all = 2 * seq_len
    tables = make_tables(length_all)
    spec_shape = (channels, tables[0].shape[0], tables[4].shape[0])

    def padded(values):
        wide = jnp.concatenate(
            [values.astype(jnp.float32), jnp.zeros((channels, seq_len), jnp.float32)], axis=1
        )
        return wide.reshape(spec_shape)

    def restore(spec_re, spec_im):
        return (
            inverse_real(spec_re, spec_im, tables).reshape(channels, length_all)[:, :seq_len]
            / length_all
        )

    gated_re, gated_im = forward_real(padded(gated), tables)
    scaled_re, scaled_im = forward_real(padded(scaled), tables)
    kernel_re, kernel_im = forward_real(padded(kernel), tables)
    conv_out = restore(
        kernel_re * gated_re - kernel_im * gated_im, kernel_re * gated_im + kernel_im * gated_re
    )
    grad_gated = restore(
        scaled_re * kernel_re + scaled_im * kernel_im, scaled_im * kernel_re - scaled_re * kernel_im
    )
    grad_kernel = restore(
        scaled_re * gated_re + scaled_im * gated_im, scaled_im * gated_re - scaled_re * gated_im
    )
    filter_grad = grad_kernel / math.sqrt(seq_len)
    return (conv_out.astype(jnp.bfloat16), grad_gated.astype(jnp.bfloat16), filter_grad)


def product(left, right):
    return (left.astype(jnp.float32) * right.astype(jnp.float32)).astype(jnp.bfloat16)


def general_body(grad_out, proj_out, query, key_in, value_in, filters):
    weight_rows = lax.all_gather(proj_out, "ctx", axis=1, tiled=True)
    grad_mix = lax.dot_general(
        lax.all_gather(grad_out, "mp", axis=1, tiled=True),
        weight_rows,
        (((1,), (1,)), ((), ())),
        preferred_element_type=jnp.float32,
    ).astype(jnp.bfloat16)
    gated = product(key_in, value_in)
    scaled = product(grad_mix, query)
    chan_gated, chan_scaled = (
        lax.all_to_all(gated.T, "ctx", split_axis=0, concat_axis=1, tiled=True),
        lax.all_to_all(scaled.T, "ctx", split_axis=0, concat_axis=1, tiled=True),
    )
    conv_out, grad_gated, filter_grad = long_filter_grads(chan_gated, chan_scaled, filters)
    back_grad, back_conv = (
        lax.all_to_all(grad_gated, "ctx", split_axis=1, concat_axis=0, tiled=True),
        lax.all_to_all(conv_out, "ctx", split_axis=1, concat_axis=0, tiled=True),
    )
    grad_query = product(grad_mix, back_conv.T)
    grad_key = product(back_grad.T, value_in)
    grad_value = product(back_grad.T, key_in)
    return (grad_query, grad_key, grad_value, filter_grad)


FAST = 32
SLOT = 2 * FAST
PAIR = 2 * SLOT
STEP = SLOT + 8
GAP = FAST + 8
LANES = 128
CHIPS = 4
OUTWARD = (6, 4, 2, 7, 5, 3, 1, 0)
HOMEWARD = (6, 2, 3, 7, 4, 5, 1, 0)
F32, BF16 = jnp.float32, jnp.bfloat16
PARAMS = pltpu.CompilerParams(vmem_limit_bytes=63 * 2**20)
VM = pl.BlockSpec(memory_space=pltpu.VMEM)
ANY = pl.BlockSpec(memory_space=pl.ANY)
U1, U2 = 16, 32


def sds(shape, dtype):
    return jax.ShapeDtypeStruct(shape, dtype)


def cost(flops, moved):
    return pl.CostEstimate(flops=flops // 10**6, bytes_accessed=moved // 10**3, transcendentals=0)


def tables(seq):
    size = 2 * seq
    slow = size // FAST
    half = slow // 2
    s = np.arange(half)
    angle = 2 * np.pi * ((s[:, None] * s[None, :]) % slow) / slow
    first = np.concatenate([np.cos(angle), -np.sin(angle)], 0)
    first[half] = 1.0 - 2.0 * (s % 2)
    weight = np.full((2 * half, 1), 2.0)
    weight[0] = weight[half] = 1.0
    last = (first * weight).T / size
    a = np.arange(FAST)
    k = np.arange(half + 1)[:, None] + slow * a[None, :]
    turn = 2 * np.pi * ((k[:, :, None] * a[None, None, :]) % size) / size
    c, d = np.cos(turn), np.sin(turn)
    fwd = np.concatenate([np.concatenate([c, d], 2), np.concatenate([-d, c], 2)], 1)
    inv = fwd.transpose(0, 2, 1).copy()
    fwd[0, :, FAST:] = 0.0
    inv[0, FAST:] = 0.0

    def paired(blocks):
        out = np.zeros((half // 2 + 1, SLOT, PAIR))
        out[:-1, :, :SLOT] = blocks[0:half:2]
        out[:-1, :, SLOT:] = blocks[1:half:2]
        return out

    fwd, inv, edge_fwd, edge_inv = paired(fwd), paired(inv), fwd[half], inv[half]
    fwd[-1, :, FAST:SLOT] = edge_fwd[:, :FAST]
    inv[-1, FAST:, :SLOT] = edge_inv[:FAST]
    blocks = np.arange(half).reshape(2 * CHIPS, -1)

    def orders(reach):
        return [np.concatenate([blocks[c ^ d] for d in reach]) for c in range(2 * CHIPS)] + [np.arange(half)]

    firsts = np.stack([first[:, o] for o in orders(OUTWARD)])
    lasts = np.stack([last[o] for o in orders(HOMEWARD)])
    return [jnp.asarray(t.astype(ml_dtypes.bfloat16)) for t in (firsts, fwd, inv, lasts)]


def dot(left, right):
    return jnp.dot(left, right, preferred_element_type=F32)


def pair_dot(pair, rows):
    low = lax.broadcasted_iota(jnp.int32, pair.shape, 1) < SLOT
    zero = jnp.zeros_like(pair)
    return dot(jnp.concatenate([jnp.where(low, pair, zero), jnp.where(low, zero, pair)], 0), rows)


def loop(count, unroll, step):
    def some(i, carry):
        for u in range(unroll):
            step(i * unroll + u)
        return carry

    lax.fori_loop(0, count // unroll, some, 0)


def span(start, size):
    return pl.ds(pl.multiple_of(start * size, size), size)


def slots(ref, p):
    return [ref.at[pl.ds(pl.multiple_of(p * 2 * STEP + i * STEP, 8), SLOT), :] for i in range(2)]


def read_slots(ref, p):
    return jnp.concatenate([rows[...] for rows in slots(ref, p)], 0).astype(BF16)


def write_slots(ref, p, value):
    for i, rows in enumerate(slots(ref, p)):
        rows[...] = value[i * SLOT : (i + 1) * SLOT]


def gapped(ref, index, count):
    return [ref.at[pl.ds(pl.multiple_of((index * count + i) * GAP, 8), FAST), :] for i in range(count)]


def read_gapped(ref, index, count):
    return jnp.concatenate([rows[...] for rows in gapped(ref, index, count)], 0)


def write_gapped(ref, index, value):
    for i, rows in enumerate(gapped(ref, index, value.shape[0] // FAST)):
        rows[...] = value[i * FAST : (i + 1) * FAST]


def spread(signal, first_ref, mid_ref):
    half = first_ref.shape[1]

    def step(a):
        out = dot(first_ref[...], signal(a))
        mid_ref[pl.ds(a, half, stride=STEP), :] = out[:half]
        mid_ref[pl.ds(FAST + a, half, stride=STEP), :] = out[half:]

    loop(FAST, U1, step)


def collect(last_ref, back_ref, emit):
    half = last_ref.shape[0]

    def step(a):
        re = back_ref[pl.ds(a, half, stride=STEP), :]
        im = back_ref[pl.ds(FAST + a, half, stride=STEP), :]
        emit(a, dot(last_ref[...], jnp.concatenate([re, im], 0).astype(BF16)))

    loop(FAST, U1, step)


def times(x, y, conjugate):
    x, y = x.astype(F32), y.astype(F32)
    parts = []
    for i in range(0, x.shape[0], SLOT):
        xr, xi, yr, yi = (v[i + j : i + j + FAST] for v in (x, y) for j in (0, FAST))
        if conjugate:
            parts += [xr * yr + xi * yi, xi * yr - xr * yi]
        else:
            parts += [xr * yr - xi * yi, xr * yi + xi * yr]
    return jnp.concatenate(parts, 0).astype(BF16)


def filter_kernel(h_ref, first_ref, fwd_ref, spec_ref, time_ref, mid_ref):
    half = first_ref.shape[1]
    seq = h_ref.shape[1]

    def turn(i):
        write_gapped(time_ref, i, h_ref[:, span(i, LANES)].T)

    loop(seq // LANES, 8, turn)
    spread(lambda a: time_ref[pl.ds(a, half, stride=GAP), :].astype(BF16), first_ref, mid_ref)

    def step(p):
        spec_ref[span(p, PAIR), :] = pair_dot(fwd_ref[p], read_slots(mid_ref, p)).astype(BF16)

    loop(half // 2, U2, step)
    spec_ref[span(half // 2, PAIR), :] = pair_dot(fwd_ref[half // 2], read_slots(mid_ref, 0)).astype(BF16)


def convolve_kernel(conjugate, count, place_ref, *refs):
    x_refs, (h_any, first_ref, fwd_any, inv_any, last_ref) = refs[:count], refs[count : count + 5]
    outs, (spec_any, h_ref, fwd_ref, inv_ref, spec_ref, mid_ref, back_ref, sem) = refs[count + 5 : -8], refs[-8:]
    first_ref, last_ref = first_ref.at[0], last_ref.at[0]
    half = first_ref.shape[1]
    loads = [
        pltpu.make_async_copy(source, target, sem.at[i])
        for i, (source, target) in enumerate(((fwd_any, fwd_ref), (h_any, h_ref), (inv_any, inv_ref)))
    ]
    for load in loads:
        load.start()
    if count == 1:
        spread(lambda a: x_refs[0][:, a].reshape(half, LANES), first_ref, mid_ref)
    else:
        spread(lambda a: jnp.concatenate([x_ref[a] for x_ref in x_refs], 0), first_ref, mid_ref)
    for load in loads:
        load.wait()

    def step(p):
        x = pair_dot(fwd_ref[p], read_slots(mid_ref, p))
        spec_ref[span(p, PAIR), :] = x.astype(BF16)
        write_slots(back_ref, p, pair_dot(inv_ref[p], times(x, h_ref[span(p, PAIR), :], conjugate)))

    loop(half // 2, U2, step)
    tail = span(half // 2, PAIR)
    x = pair_dot(fwd_ref[half // 2], read_slots(mid_ref, 0))
    spec_ref[tail, :] = x.astype(BF16)
    store = pltpu.make_async_copy(spec_ref, spec_any, sem.at[3])
    store.start()
    back_ref[:SLOT, :] += pair_dot(inv_ref[half // 2], times(x, h_ref[tail, :], conjugate))[:SLOT]
    if len(outs) == 1:

        def emit(a, rows):
            outs[0][:, a] = rows.reshape(outs[0].shape[0], -1, LANES).astype(BF16)

        collect(last_ref, back_ref, emit)
    else:
        per = half // len(outs)

        def emit(a, rows):
            for i, out_ref in enumerate(outs):
                out_ref[a] = rows[i * per : (i + 1) * per].astype(BF16)

        collect(last_ref, back_ref, emit)
    store.wait()


def gradient_kernel(scale, s_ref, g_ref, inv_ref, last_ref, out_ref, time_ref, back_ref):
    half = last_ref.shape[0]
    seq = out_ref.shape[1]

    def step(p):
        rows = span(p, PAIR)
        write_slots(back_ref, p, pair_dot(inv_ref[p], times(s_ref[rows, :], g_ref[rows, :], True)))

    loop(half // 2, U2, step)
    tail = span(half // 2, PAIR)
    back_ref[:SLOT, :] += pair_dot(inv_ref[half // 2], times(s_ref[tail, :], g_ref[tail, :], True))[:SLOT]

    def emit(a, rows):
        time_ref[pl.ds(a, half, stride=GAP), :] = rows * scale

    collect(last_ref, back_ref, emit)

    def turn(i):
        out_ref[:, span(i, LANES)] = read_gapped(time_ref, i, LANES // FAST).T

    loop(seq // LANES, 8, turn)


def filter_spectrum(h, tabs):
    first, fwd = tabs[:2]
    seq = h.shape[1]
    return pl.pallas_call(
        filter_kernel,
        out_shape=sds((2 * seq + PAIR, LANES), BF16),
        in_specs=[VM] * 3,
        out_specs=VM,
        scratch_shapes=[pltpu.VMEM((seq // FAST * GAP, LANES), F32), pltpu.VMEM((seq // FAST * STEP, LANES), F32)],
        compiler_params=PARAMS,
        cost_estimate=cost(10**9, 8 * 2**20),
        name="filter_spectrum",
    )(h, first, fwd)


def convolve(index, parts, spec, tabs, conjugate, whole):
    first, fwd, inv, last = tabs
    count = len(parts)
    groups = 2 * CHIPS
    half = last.shape[1]

    def own(table):
        return pl.BlockSpec((1,) + table.shape[1:], lambda i, index: (index[0], 0, 0))

    outs = (sds((FAST, half // groups, LANES), BF16),) * groups
    if whole:
        outs = (sds((groups, FAST, half // groups, LANES), BF16),)
    big = pltpu.VMEM((half * STEP, LANES), F32)
    *out, spec = pl.pallas_call(
        functools.partial(convolve_kernel, conjugate, count),
        out_shape=outs + (sds(spec.shape, BF16),),
        grid_spec=pltpu.PrefetchScalarGridSpec(
            num_scalar_prefetch=1,
            grid=(1,),
            in_specs=[VM] * count + [ANY, own(first), ANY, ANY, own(last)],
            out_specs=(VM,) * len(outs) + (ANY,),
            scratch_shapes=[
                pltpu.VMEM(spec.shape, BF16),
                pltpu.VMEM(fwd.shape, BF16),
                pltpu.VMEM(fwd.shape, BF16),
                pltpu.VMEM(spec.shape, BF16),
                big,
                big,
                pltpu.SemaphoreType.DMA((4,)),
            ],
        ),
        compiler_params=PARAMS,
        cost_estimate=cost(2 * 10**9, 14 * 2**20),
        name="convolve",
    )(index, *parts, spec, *tabs)
    return out, spec


def filter_gradient(scaled_spec, gated_spec, tabs, scale):
    inv, last = tabs[2:]
    seq = (scaled_spec.shape[0] - PAIR) // 2
    return pl.pallas_call(
        functools.partial(gradient_kernel, scale),
        out_shape=sds((LANES, seq), F32),
        in_specs=[VM] * 4,
        out_specs=VM,
        scratch_shapes=[pltpu.VMEM((seq // FAST * GAP, LANES), F32), pltpu.VMEM((seq // FAST * STEP, LANES), F32)],
        compiler_params=PARAMS,
        cost_estimate=cost(10**9, 12 * 2**20),
        name="filter_gradient",
    )(scaled_spec, gated_spec, inv, last)


def permuted(value, hold_ref, emit):
    write_gapped(hold_ref, 0, value)
    per = value.shape[0] // FAST
    for a in range(FAST):
        emit(a, hold_ref[pl.ds(a, per, stride=GAP), :].astype(BF16))


def gate_kernel(key_ref, value_ref, out_ref, hold_ref):
    product = key_ref[...].astype(F32) * value_ref[...].astype(F32)
    for g in range(WIDE // LANES):

        def emit(a, rows):
            out_ref[g, a] = rows

        permuted(product[:, g * LANES : (g + 1) * LANES], hold_ref, emit)


def gate(key_in, value_in, groups):
    rows, cols = key_in.shape
    block = pl.BlockSpec((rows, WIDE), lambda j: (0, j))
    return pl.pallas_call(
        gate_kernel,
        grid=(cols // WIDE,),
        out_shape=sds((groups, FAST, rows // FAST, LANES), BF16),
        in_specs=[block, block],
        out_specs=pl.BlockSpec((WIDE // LANES, FAST, rows // FAST, LANES), lambda j: (j, 0, 0, 0)),
        scratch_shapes=[pltpu.VMEM((rows // FAST * GAP, LANES), F32)],
        compiler_params=PARAMS,
        cost_estimate=cost(10**6, 3 * 2**20),
        name="gate",
    )(key_in, value_in)


WIDE = 256
BATCH = 4


def pieces_of(x_ref, piece, lane, depth):
    return x_ref[piece, :, pl.ds(pl.multiple_of(lane * depth, depth), depth)]


def against(left, w_ref):
    return lax.dot_general(left, w_ref[...], (((1,), (1,)), ((), ())), preferred_element_type=F32)


def is_end(place):
    return (place[0] == 0) | (place[0] == CHIPS - 1)


def terms_kernel(place_ref, *refs):
    xs, ws, (sum_ref, x_ref, sem) = refs[:4], refs[4:10], refs[-3:]
    here, core, mine = place_ref[0], place_ref[1], place_ref[2]
    depth = ws[0].shape[1]
    inside = jnp.logical_not(is_end(place_ref))

    @pl.when(pl.program_id(0) == 0)
    def _():
        for start in (True, False):
            for i in range(4):
                apart = mine ^ i ^ here

                @pl.when((apart < 2) | (inside & (apart == CHIPS - 1)))
                def _():
                    copy = pltpu.make_async_copy(xs[i], x_ref.at[mine ^ i], sem.at[i])
                    copy.start() if start else copy.wait()

    def part(piece, near_ref, swap_ref):
        one = against(pieces_of(x_ref, piece, core, depth), near_ref)
        return one + against(pieces_of(x_ref, piece, 1 - core, depth), swap_ref)

    total = part(here, ws[0], ws[1]) + part(here ^ 1, ws[2], ws[3])

    @pl.when(inside)
    def _():
        sum_ref[...] = total + part(CHIPS - 1 - here, ws[4], ws[5])

    @pl.when(is_end(place_ref))
    def _():
        sum_ref[...] = total


def always(j, place):
    return (j, 0)


def inside_only(j, place):
    return (jnp.where(is_end(place), 0, j), 0)


def terms(place, xs, ws):
    rows, piece = xs[0].shape
    cols, depth = ws[0].shape
    maps = [always] * 4 + [inside_only] * 2
    return pl.pallas_call(
        terms_kernel,
        out_shape=sds((rows, cols), F32),
        grid_spec=pltpu.PrefetchScalarGridSpec(
            num_scalar_prefetch=1,
            grid=(cols // WIDE,),
            in_specs=[ANY] * 4 + [pl.BlockSpec((WIDE, depth), m) for m in maps],
            out_specs=pl.BlockSpec((rows, WIDE), lambda j, place: (0, j)),
            scratch_shapes=[pltpu.VMEM((4, rows, piece), BF16), pltpu.SemaphoreType.DMA((4,))],
        ),
        compiler_params=PARAMS,
        cost_estimate=cost(2 * 10**9, 14 * 2**20),
        name="terms",
    )(place, *xs, *ws)


def late_kernel(place_ref, *refs):
    xs, ws, sum_ref, query_ref, mix_ref = refs[:4], refs[4:10], refs[10], refs[11], refs[12]
    outs, (hold_ref, x_ref, sem) = refs[13:-3], refs[-3:]
    here, core, mine = place_ref[0], place_ref[1], place_ref[2]
    two_ref, three_ref = x_ref.at[pl.ds(0, 1)], x_ref.at[pl.ds(1, 1)]

    ends = is_end(place_ref)

    @pl.when(pl.program_id(0) == 0)
    def _():
        for start in (True, False):
            for slot, piece, needed in ((0, here ^ 2, True), (1, CHIPS - 1 - here, ends)):
                for i in range(4):

                    @pl.when((mine ^ piece == i) & needed)
                    def _():
                        copy = pltpu.make_async_copy(xs[i], x_ref.at[slot], sem.at[slot])
                        copy.start() if start else copy.wait()

    depth = ws[0].shape[1]
    per = sum_ref.shape[0] // FAST

    def part(piece_ref, near_ref, swap_ref):
        one = against(pieces_of(piece_ref, 0, core, depth), near_ref)
        return one + against(pieces_of(piece_ref, 0, 1 - core, depth), swap_ref)

    def give(total):
        mix = total.astype(BF16)
        mix_ref[...] = mix
        scaled = mix.astype(F32) * query_ref[...].astype(F32)
        for g in range(BATCH):
            write_gapped(hold_ref.at[g], 0, scaled[:, g * LANES : (g + 1) * LANES])

    @pl.when(ends)
    def _():
        give(sum_ref[...] + part(two_ref, ws[2], ws[3]) + part(three_ref, ws[4], ws[5]))

    @pl.when(jnp.logical_not(ends))
    def _():
        give(sum_ref[...] + part(two_ref, ws[0], ws[1]))

    for k in range(2 * CHIPS // BATCH):

        @pl.when(pl.program_id(0) == k)
        def _():
            for e in range(BATCH):
                for a in range(FAST):
                    outs[OUTWARD.index(BATCH * k + e)][a] = hold_ref[e ^ (place_ref[3] % BATCH), pl.ds(a, per, stride=GAP), :].astype(BF16)


def mix_late(place, xs, ws, total, query):
    rows, cols = query.shape
    depth = ws[0].shape[1]

    def block(j, place):
        return j ^ (place[3] // BATCH)

    def inner(j, place):
        return (jnp.where(is_end(place), 0, block(j, place)), 0)

    def outer(j, place):
        return (jnp.where(is_end(place), block(j, place), 0), 0)

    wide = pl.BlockSpec((rows, BATCH * LANES), lambda j, place: (0, block(j, place)))
    part = pl.BlockSpec((FAST, rows // FAST, LANES), lambda j, place: (0, 0, 0))
    grad_mix, *scaled = pl.pallas_call(
        late_kernel,
        out_shape=(sds((rows, cols), BF16),) + (sds((FAST, rows // FAST, LANES), BF16),) * (2 * CHIPS),
        grid_spec=pltpu.PrefetchScalarGridSpec(
            num_scalar_prefetch=1,
            grid=(2 * CHIPS // BATCH,),
            in_specs=[ANY] * 4
            + [pl.BlockSpec((BATCH * LANES, depth), m) for m in (inner, inner, outer, outer, outer, outer)]
            + [wide, wide],
            out_specs=(wide,) + (part,) * (2 * CHIPS),
            scratch_shapes=[
                pltpu.VMEM((BATCH, rows // FAST * GAP, LANES), F32),
                pltpu.VMEM((2,) + xs[0].shape, BF16),
                pltpu.SemaphoreType.DMA((2,)),
            ],
        ),
        compiler_params=PARAMS,
        cost_estimate=cost(10**9, 8 * 2**20),
        name="mix_late",
    )(place, *xs, *ws, total, query)
    return grad_mix, scaled


def finish_kernel(count, place_ref, *refs):
    parts, factors, outs = refs[: 2 * CHIPS], refs[2 * CHIPS : 2 * CHIPS + count], refs[2 * CHIPS + count : -1]
    hold_ref = refs[-1]
    here = place_ref[3] % BATCH
    per = parts[0].shape[1]
    for k in range(2 * CHIPS // BATCH):

        @pl.when(pl.program_id(0) == k)
        def _():
            for e in range(BATCH):
                for a in range(FAST):
                    hold_ref[e ^ here, pl.ds(a, per, stride=GAP), :] = parts[HOMEWARD.index(BATCH * k + e)][a].astype(F32)

    for g in range(BATCH):
        lanes = pl.ds(g * LANES, LANES)
        value = read_gapped(hold_ref.at[g], 0, per)
        for factor_ref, out_ref in zip(factors, outs):
            out_ref[:, lanes] = (value * factor_ref[:, lanes].astype(F32)).astype(BF16)


def finish(place, parts, *factors):
    rows, cols = factors[0].shape
    count = len(factors)
    block = pl.BlockSpec((rows, BATCH * LANES), lambda j, place: (0, j ^ (place[3] // BATCH)))
    part = pl.BlockSpec(parts[0].shape, lambda j, place: (0, 0, 0))
    return pl.pallas_call(
        functools.partial(finish_kernel, count),
        out_shape=(sds((rows, cols), BF16),) * count,
        grid_spec=pltpu.PrefetchScalarGridSpec(
            num_scalar_prefetch=1,
            grid=(2 * CHIPS // BATCH,),
            in_specs=[part] * (2 * CHIPS) + [block] * count,
            out_specs=(block,) * count,
            scratch_shapes=[pltpu.VMEM((BATCH, rows // FAST * GAP, LANES), F32)],
        ),
        compiler_params=PARAMS,
        cost_estimate=cost(10**6, (1 + 2 * count) * 2**20),
        name="finish",
    )(place, *parts, *factors)


def finish_whole_kernel(part_ref, factor_ref, out_ref, hold_ref):
    per = part_ref.shape[2]
    for g in range(2):
        for a in range(FAST):
            hold_ref[pl.ds(a, per, stride=GAP), :] = part_ref[g, a].astype(F32)
        lanes = pl.ds(g * LANES, LANES)
        out_ref[:, lanes] = (read_gapped(hold_ref, 0, per) * factor_ref[:, lanes].astype(F32)).astype(BF16)


def finish_whole(parts, factor):
    rows, cols = factor.shape
    wide = pl.BlockSpec((rows, WIDE), lambda j: (0, j))
    part = pl.BlockSpec((2,) + parts.shape[1:], lambda j: (j, 0, 0, 0))
    return pl.pallas_call(
        finish_whole_kernel,
        out_shape=sds((rows, cols), BF16),
        grid=(CHIPS,),
        in_specs=[part, wide],
        out_specs=wide,
        scratch_shapes=[pltpu.VMEM((rows // FAST * GAP, LANES), F32)],
        compiler_params=PARAMS,
        cost_estimate=cost(10**6, 3 * 2**20),
        name="finish_whole",
    )(parts, factor)


def exchange(parts):
    return lax.all_to_all(parts, "ctx", split_axis=0, concat_axis=0, tiled=True)


def scatter(parts, reach):
    ids = range(2 * CHIPS)
    return [lax.ppermute(part, "ctx", [(i, i ^ d) for i in ids]) if d else part for part, d in zip(parts, reach)]


SWAP = [(i, i ^ 1) for i in range(8)]
SIDE = [(i, i ^ 2) for i in range(8)]
MIDDLE = [(2, 4), (3, 5), (4, 2), (5, 3)]
OUT = [(2, 0), (3, 1), (4, 6), (5, 7)]
INNER_SWAP, END_SWAP = SWAP[2:6], SWAP[:2] + SWAP[6:]


def to(x, pairs):
    return lax.ppermute(x, "ctx", pairs)


def lane_body(grad_out, proj_out, query, key_in, value_in, filters):
    seq = filters.shape[1]
    groups = seq // key_in.shape[0]
    firsts, fwd, inv, lasts = tables(seq)
    tie = lax.optimization_barrier
    ctx = lax.axis_index("ctx")
    place = jnp.stack([ctx // 2, ctx % 2, lax.axis_index("mp"), ctx]).astype(jnp.int32)
    index = ctx.astype(jnp.int32)[None]

    def across(x, d):
        return lax.ppermute(x, "mp", [(i, i ^ d) for i in range(4)])

    side, middle = to(proj_out, SIDE), to(proj_out, MIDDLE)
    x1, x2 = across(grad_out, 1), across(grad_out, 2)
    gated = exchange(gate(key_in, value_in, groups))
    spec = filter_spectrum(filters, (firsts[-1], fwd))
    side, middle, spec = tie((side, middle, spec))

    crossed, sent_out = to(side, MIDDLE), to(middle, OUT)
    ws = [side, to(side, SWAP), middle, to(middle, INNER_SWAP)]
    x3, own, *_ = tie((grad_out, proj_out, x1, x2, ws[1], ws[3]))
    ws = [own, to(own, SWAP)] + ws
    xs = [grad_out, x1, x2, across(x3, 3)]
    (conv,), gated_spec = convolve(jnp.full_like(index, 2 * CHIPS), [gated], spec, (firsts, fwd, inv, lasts), False, True)
    crossed, _ = tie((crossed, conv))

    last = to(crossed, OUT)
    total = terms(place, xs, ws)
    conv, _ = tie((conv, total))
    conv = exchange(conv)
    ws = [crossed, to(crossed, INNER_SWAP), sent_out, to(sent_out, END_SWAP)]
    last, _ = tie((last, total))
    ws += [last, to(last, END_SWAP)]
    grad_mix, scaled = mix_late(place, xs, ws, total, query)
    scaled = scatter(scaled, OUTWARD)
    *scaled, conv = tie((*scaled, conv))
    back, scaled_spec = convolve(index, scaled, spec, (firsts, fwd, inv, lasts), True, False)
    back = scatter(back, HOMEWARD)
    filter_grad = filter_gradient(scaled_spec, gated_spec, (None, fwd, inv, lasts[-1]), 1.0 / math.sqrt(seq))
    grad_query = finish_whole(conv, grad_mix)
    grad_key, grad_value = finish(place, back, value_in, key_in)
    return (grad_query, grad_key, grad_value, filter_grad)


def body(grad_out, proj_out, query, key_in, value_in, filters):
    rows, cols = key_in.shape
    lanes, seq = filters.shape
    fits = (
        lax.axis_size("ctx") == 2 * CHIPS
        and lax.axis_size("mp") == 4
        and lanes == LANES
        and rows % (16 * FAST) == 0
        and cols == 2 * CHIPS * LANES
        and seq == 2 * CHIPS * rows
        and seq == FAST * LANES
        and grad_out.shape[1] == 2 * proj_out.shape[1]
    )
    args = (grad_out, proj_out, query, key_in, value_in, filters)
    return lane_body(*args) if fits else general_body(*args)


def solution(mesh):
    return jax.shard_map(
        body,
        mesh=mesh,
        in_specs=(
            P("ctx", "mp"),
            P("mp", "ctx"),
            P("ctx", "mp"),
            P("ctx", "mp"),
            P("ctx", "mp"),
            P(("mp", "ctx"), None),
        ),
        out_specs=(P("ctx", "mp"), P("ctx", "mp"), P("ctx", "mp"), P(("mp", "ctx"), None)),
        check_vma=False,
    )
```

```python
import functools
import math

import jax
import jax.numpy as jnp
import ml_dtypes
import numpy as np
from jax import lax
from jax.experimental import pallas as pl
from jax.experimental.pallas import tpu as pltpu
from jax.sharding import PartitionSpec as P


def phase_table(rows_n, cols_n, modulus):
    prod_idx = (
        jnp.arange(rows_n, dtype=jnp.int32)[:, None]
        * jnp.arange(cols_n, dtype=jnp.int32)[None, :]
        % modulus
    )
    angles = prod_idx.astype(jnp.float32) * (2.0 * math.pi / modulus)
    return (jnp.cos(angles), jnp.sin(angles))


def make_tables(length_all):
    size_second = min(128, length_all)
    size_first = length_all // size_second
    cos_first, sin_first = phase_table(size_first, size_first, size_first)
    twist_cos, twist_sin = phase_table(size_first, size_second, length_all)
    cos_second, sin_second = phase_table(size_second, size_second, size_second)
    return (cos_first, sin_first, twist_cos, twist_sin, cos_second, sin_second)


def contract(form, left, right):
    return jnp.einsum(form, left, right, precision=lax.Precision.HIGHEST)


def forward_real(signal, tables):
    cos_first, sin_first, twist_cos, twist_sin, cos_second, sin_second = tables
    part_re = contract("kn,cnm->ckm", cos_first, signal)
    part_im = -contract("kn,cnm->ckm", sin_first, signal)
    turned_re = part_re * twist_cos + part_im * twist_sin
    turned_im = part_im * twist_cos - part_re * twist_sin
    spec_re = contract("ckm,mj->ckj", turned_re, cos_second) + contract(
        "ckm,mj->ckj", turned_im, sin_second
    )
    spec_im = contract("ckm,mj->ckj", turned_im, cos_second) - contract(
        "ckm,mj->ckj", turned_re, sin_second
    )
    return (spec_re, spec_im)


def inverse_real(spec_re, spec_im, tables):
    cos_first, sin_first, twist_cos, twist_sin, cos_second, sin_second = tables
    back_re = contract("ckj,jm->ckm", spec_re, cos_second) - contract(
        "ckj,jm->ckm", spec_im, sin_second
    )
    back_im = contract("ckj,jm->ckm", spec_re, sin_second) + contract(
        "ckj,jm->ckm", spec_im, cos_second
    )
    twist_re = back_re * twist_cos - back_im * twist_sin
    twist_im = back_re * twist_sin + back_im * twist_cos
    return contract("nk,ckm->cnm", cos_first, twist_re) - contract(
        "nk,ckm->cnm", sin_first, twist_im
    )


def long_filter_grads(gated, scaled, kernel):
    channels, seq_len = kernel.shape
    length_all = 2 * seq_len
    tables = make_tables(length_all)
    spec_shape = (channels, tables[0].shape[0], tables[4].shape[0])

    def padded(values):
        wide = jnp.concatenate(
            [values.astype(jnp.float32), jnp.zeros((channels, seq_len), jnp.float32)], axis=1
        )
        return wide.reshape(spec_shape)

    def restore(spec_re, spec_im):
        return (
            inverse_real(spec_re, spec_im, tables).reshape(channels, length_all)[:, :seq_len]
            / length_all
        )

    gated_re, gated_im = forward_real(padded(gated), tables)
    scaled_re, scaled_im = forward_real(padded(scaled), tables)
    kernel_re, kernel_im = forward_real(padded(kernel), tables)
    conv_out = restore(
        kernel_re * gated_re - kernel_im * gated_im, kernel_re * gated_im + kernel_im * gated_re
    )
    grad_gated = restore(
        scaled_re * kernel_re + scaled_im * kernel_im, scaled_im * kernel_re - scaled_re * kernel_im
    )
    grad_kernel = restore(
        scaled_re * gated_re + scaled_im * gated_im, scaled_im * gated_re - scaled_re * gated_im
    )
    filter_grad = grad_kernel / math.sqrt(seq_len)
    return (conv_out.astype(jnp.bfloat16), grad_gated.astype(jnp.bfloat16), filter_grad)


def product(left, right):
    return (left.astype(jnp.float32) * right.astype(jnp.float32)).astype(jnp.bfloat16)


def general_body(grad_out, proj_out, query, key_in, value_in, filters):
    weight_rows = lax.all_gather(proj_out, "ctx", axis=1, tiled=True)
    grad_mix = lax.dot_general(
        lax.all_gather(grad_out, "mp", axis=1, tiled=True),
        weight_rows,
        (((1,), (1,)), ((), ())),
        preferred_element_type=jnp.float32,
    ).astype(jnp.bfloat16)
    gated = product(key_in, value_in)
    scaled = product(grad_mix, query)
    chan_gated, chan_scaled = (
        lax.all_to_all(gated.T, "ctx", split_axis=0, concat_axis=1, tiled=True),
        lax.all_to_all(scaled.T, "ctx", split_axis=0, concat_axis=1, tiled=True),
    )
    conv_out, grad_gated, filter_grad = long_filter_grads(chan_gated, chan_scaled, filters)
    back_grad, back_conv = (
        lax.all_to_all(grad_gated, "ctx", split_axis=1, concat_axis=0, tiled=True),
        lax.all_to_all(conv_out, "ctx", split_axis=1, concat_axis=0, tiled=True),
    )
    grad_query = product(grad_mix, back_conv.T)
    grad_key = product(back_grad.T, value_in)
    grad_value = product(back_grad.T, key_in)
    return (grad_query, grad_key, grad_value, filter_grad)


FAST = 32
SLOT = 2 * FAST
PAIR = 2 * SLOT
STEP = SLOT + 8
GAP = FAST + 8
LANES = 128
CHIPS = 4
OUTWARD = (6, 4, 2, 7, 5, 3, 1, 0)
HOMEWARD = (6, 2, 3, 7, 4, 5, 1, 0)
F32, BF16 = jnp.float32, jnp.bfloat16
PARAMS = pltpu.CompilerParams(vmem_limit_bytes=63 * 2**20)
SMALL = pltpu.CompilerParams(vmem_limit_bytes=52 * 2**20)
VM = pl.BlockSpec(memory_space=pltpu.VMEM)
ANY = pl.BlockSpec(memory_space=pl.ANY)
HBM = pl.BlockSpec(memory_space=pltpu.HBM)
U1, U2 = 32, 64


def sds(shape, dtype):
    return jax.ShapeDtypeStruct(shape, dtype)


def cost(flops, moved):
    return pl.CostEstimate(flops=flops // 10**6, bytes_accessed=moved // 10**3, transcendentals=0)


def tables(seq):
    size = 2 * seq
    slow = size // FAST
    half = slow // 2
    s = np.arange(half)
    angle = 2 * np.pi * ((s[:, None] * s[None, :]) % slow) / slow
    first = np.concatenate([np.cos(angle), -np.sin(angle)], 0)
    first[half] = 1.0 - 2.0 * (s % 2)
    weight = np.full((2 * half, 1), 2.0)
    weight[0] = weight[half] = 1.0
    last = (first * weight).T / size
    a = np.arange(FAST)
    k = np.arange(half + 1)[:, None] + slow * a[None, :]
    turn = 2 * np.pi * ((k[:, :, None] * a[None, None, :]) % size) / size
    c, d = np.cos(turn), np.sin(turn)
    fwd = np.concatenate([np.concatenate([c, d], 2), np.concatenate([-d, c], 2)], 1)
    inv = fwd.transpose(0, 2, 1).copy()
    fwd[0, :, FAST:] = 0.0
    inv[0, FAST:] = 0.0

    def paired(blocks):
        out = np.zeros((half // 2 + 1, SLOT, PAIR))
        out[:-1, :, :SLOT] = blocks[0:half:2]
        out[:-1, :, SLOT:] = blocks[1:half:2]
        return out

    fwd, inv, edge_fwd, edge_inv = paired(fwd), paired(inv), fwd[half], inv[half]
    fwd[-1, :, FAST:SLOT] = edge_fwd[:, :FAST]
    inv[-1, FAST:, :SLOT] = edge_inv[:FAST]
    blocks = np.arange(half).reshape(2 * CHIPS, -1)

    def orders(reach):
        return [np.concatenate([blocks[c ^ d] for d in reach]) for c in range(2 * CHIPS)] + [np.arange(half)]

    firsts = np.stack([first[:, o] for o in orders(OUTWARD)])
    lasts = np.stack([last[o] for o in orders(HOMEWARD)])
    return [jnp.asarray(t.astype(ml_dtypes.bfloat16)) for t in (firsts, fwd, inv, lasts)]


def dot(left, right):
    return jnp.dot(left, right, preferred_element_type=F32)


def pair_dot(pair, rows):
    low = lax.broadcasted_iota(jnp.int32, pair.shape, 1) < SLOT
    zero = jnp.zeros_like(pair)
    return dot(jnp.concatenate([jnp.where(low, pair, zero), jnp.where(low, zero, pair)], 0), rows)


def loop(count, unroll, step):
    def some(i, carry):
        for u in range(unroll):
            step(i * unroll + u)
        return carry

    lax.fori_loop(0, count // unroll, some, 0)


def span(start, size):
    return pl.ds(pl.multiple_of(start * size, size), size)


def slots(ref, p):
    return [ref.at[pl.ds(pl.multiple_of(p * 2 * STEP + i * STEP, 8), SLOT), :] for i in range(2)]


def read_slots(ref, p):
    return jnp.concatenate([rows[...] for rows in slots(ref, p)], 0).astype(BF16)


def write_slots(ref, p, value):
    for i, rows in enumerate(slots(ref, p)):
        rows[...] = value[i * SLOT : (i + 1) * SLOT]


def gapped(ref, index, count):
    return [ref.at[pl.ds(pl.multiple_of((index * count + i) * GAP, 8), FAST), :] for i in range(count)]


def read_gapped(ref, index, count):
    return jnp.concatenate([rows[...] for rows in gapped(ref, index, count)], 0)


def write_gapped(ref, index, value):
    for i, rows in enumerate(gapped(ref, index, value.shape[0] // FAST)):
        rows[...] = value[i * FAST : (i + 1) * FAST]


def spread(signal, first_ref, mid_ref):
    half = first_ref.shape[1]

    def step(a):
        out = dot(first_ref[...], signal(a))
        mid_ref[pl.ds(a, half, stride=STEP), :] = out[:half]
        mid_ref[pl.ds(FAST + a, half, stride=STEP), :] = out[half:]

    loop(FAST, U1, step)


def collect(last_ref, back_ref, emit):
    half = last_ref.shape[0]

    def step(a):
        re = back_ref[pl.ds(a, half, stride=STEP), :]
        im = back_ref[pl.ds(FAST + a, half, stride=STEP), :]
        emit(a, dot(last_ref[...], jnp.concatenate([re, im], 0).astype(BF16)))

    loop(FAST, U1, step)


def times(x, y, conjugate):
    x, y = x.astype(F32), y.astype(F32)
    parts = []
    for i in range(0, x.shape[0], SLOT):
        xr, xi, yr, yi = (v[i + j : i + j + FAST] for v in (x, y) for j in (0, FAST))
        if conjugate:
            parts += [xr * yr + xi * yi, xi * yr - xr * yi]
        else:
            parts += [xr * yr - xi * yi, xr * yi + xi * yr]
    return jnp.concatenate(parts, 0).astype(BF16)


def filter_kernel(h_ref, first_ref, fwd_ref, spec_ref, time_ref, mid_ref):
    half = first_ref.shape[1]
    seq = h_ref.shape[1]

    def turn(i):
        write_gapped(time_ref, i, h_ref[:, span(i, LANES)].T)

    loop(seq // LANES, 8, turn)
    spread(lambda a: time_ref[pl.ds(a, half, stride=GAP), :].astype(BF16), first_ref, mid_ref)

    def step(p):
        spec_ref[span(p, PAIR), :] = pair_dot(fwd_ref[p], read_slots(mid_ref, p)).astype(BF16)

    loop(half // 2, U2, step)
    spec_ref[span(half // 2, PAIR), :] = pair_dot(fwd_ref[half // 2], read_slots(mid_ref, 0)).astype(BF16)


def convolve_kernel(conjugate, count, place_ref, *refs):
    x_refs, (h_any, first_ref, fwd_any, inv_any, last_ref) = refs[:count], refs[count : count + 5]
    outs, (spec_any, h_ref, fwd_ref, inv_ref, spec_ref, mid_ref, back_ref, sem) = refs[count + 5 : -8], refs[-8:]
    first_ref, last_ref = first_ref.at[0], last_ref.at[0]
    half = first_ref.shape[1]
    loads = [
        pltpu.make_async_copy(source, target, sem.at[i])
        for i, (source, target) in enumerate(((fwd_any, fwd_ref), (h_any, h_ref), (inv_any, inv_ref)))
    ]
    for load in loads:
        load.start()
    if count == 1:
        spread(lambda a: x_refs[0][:, a].reshape(half, LANES), first_ref, mid_ref)
    else:
        spread(lambda a: jnp.concatenate([x_ref[a] for x_ref in x_refs], 0), first_ref, mid_ref)
    for load in loads:
        load.wait()

    def step(p):
        x = pair_dot(fwd_ref[p], read_slots(mid_ref, p))
        spec_ref[span(p, PAIR), :] = x.astype(BF16)
        write_slots(back_ref, p, pair_dot(inv_ref[p], times(x, h_ref[span(p, PAIR), :], conjugate)))

    loop(half // 2, U2, step)
    tail = span(half // 2, PAIR)
    x = pair_dot(fwd_ref[half // 2], read_slots(mid_ref, 0))
    spec_ref[tail, :] = x.astype(BF16)
    store = pltpu.make_async_copy(spec_ref, spec_any, sem.at[3])
    store.start()
    back_ref[:SLOT, :] += pair_dot(inv_ref[half // 2], times(x, h_ref[tail, :], conjugate))[:SLOT]
    if len(outs) == 1:

        def emit(a, rows):
            outs[0][:, a] = rows.reshape(outs[0].shape[0], -1, LANES).astype(BF16)

        collect(last_ref, back_ref, emit)
    else:
        per = half // len(outs)

        def emit(a, rows):
            for i, out_ref in enumerate(outs):
                out_ref[a] = rows[i * per : (i + 1) * per].astype(BF16)

        collect(last_ref, back_ref, emit)
    store.wait()


def gradient_kernel(scale, s_ref, g_ref, inv_ref, last_ref, out_ref, time_ref, back_ref):
    half = last_ref.shape[0]
    seq = out_ref.shape[1]

    def step(p):
        rows = span(p, PAIR)
        write_slots(back_ref, p, pair_dot(inv_ref[p], times(s_ref[rows, :], g_ref[rows, :], True)))

    loop(half // 2, U2, step)
    tail = span(half // 2, PAIR)
    back_ref[:SLOT, :] += pair_dot(inv_ref[half // 2], times(s_ref[tail, :], g_ref[tail, :], True))[:SLOT]

    def emit(a, rows):
        time_ref[pl.ds(a, half, stride=GAP), :] = rows * scale

    collect(last_ref, back_ref, emit)

    def turn(i):
        out_ref[:, span(i, LANES)] = read_gapped(time_ref, i, LANES // FAST).T

    loop(seq // LANES, 8, turn)


def filter_spectrum(h, tabs):
    first, fwd = tabs[:2]
    seq = h.shape[1]
    return pl.pallas_call(
        filter_kernel,
        out_shape=sds((2 * seq + PAIR, LANES), BF16),
        in_specs=[VM] * 3,
        out_specs=VM,
        scratch_shapes=[pltpu.VMEM((seq // FAST * GAP, LANES), F32), pltpu.VMEM((seq // FAST * STEP, LANES), F32)],
        compiler_params=PARAMS,
        cost_estimate=cost(10**9, 8 * 2**20),
        name="filter_spectrum",
    )(h, first, fwd)


def convolve(index, parts, spec, tabs, conjugate, whole):
    first, fwd, inv, last = tabs
    count = len(parts)
    groups = 2 * CHIPS
    half = last.shape[1]

    def own(table):
        return pl.BlockSpec((1,) + table.shape[1:], lambda i, index: (index[0], 0, 0))

    outs = (sds((FAST, half // groups, LANES), BF16),) * groups
    if whole:
        outs = (sds((groups, FAST, half // groups, LANES), BF16),)
    big = pltpu.VMEM((half * STEP, LANES), F32)
    *out, spec = pl.pallas_call(
        functools.partial(convolve_kernel, conjugate, count),
        out_shape=outs + (sds(spec.shape, BF16),),
        grid_spec=pltpu.PrefetchScalarGridSpec(
            num_scalar_prefetch=1,
            grid=(1,),
            in_specs=[VM] * count + [HBM, own(first), HBM, HBM, own(last)],
            out_specs=(VM,) * len(outs) + (HBM,),
            scratch_shapes=[
                pltpu.VMEM(spec.shape, BF16),
                pltpu.VMEM(fwd.shape, BF16),
                pltpu.VMEM(fwd.shape, BF16),
                pltpu.VMEM(spec.shape, BF16),
                big,
                big,
                pltpu.SemaphoreType.DMA((4,)),
            ],
        ),
        compiler_params=SMALL,
        cost_estimate=cost(2 * 10**9, 14 * 2**20),
        name="convolve",
    )(index, *parts, spec, *tabs)
    return out, spec


def filter_gradient(scaled_spec, gated_spec, tabs, scale):
    inv, last = tabs[2:]
    seq = (scaled_spec.shape[0] - PAIR) // 2
    return pl.pallas_call(
        functools.partial(gradient_kernel, scale),
        out_shape=sds((LANES, seq), F32),
        in_specs=[VM] * 4,
        out_specs=VM,
        scratch_shapes=[pltpu.VMEM((seq // FAST * GAP, LANES), F32), pltpu.VMEM((seq // FAST * STEP, LANES), F32)],
        compiler_params=PARAMS,
        cost_estimate=cost(10**9, 12 * 2**20),
        name="filter_gradient",
    )(scaled_spec, gated_spec, inv, last)


def permuted(value, hold_ref, emit):
    write_gapped(hold_ref, 0, value)
    per = value.shape[0] // FAST
    for a in range(FAST):
        emit(a, hold_ref[pl.ds(a, per, stride=GAP), :].astype(BF16))


def gate_kernel(key_ref, value_ref, out_ref, hold_ref):
    product = key_ref[...].astype(F32) * value_ref[...].astype(F32)
    for g in range(WIDE // LANES):

        def emit(a, rows):
            out_ref[g, a] = rows

        permuted(product[:, g * LANES : (g + 1) * LANES], hold_ref, emit)


def gate(key_in, value_in, groups):
    rows, cols = key_in.shape
    block = pl.BlockSpec((rows, WIDE), lambda j: (0, j))
    return pl.pallas_call(
        gate_kernel,
        grid=(cols // WIDE,),
        out_shape=sds((groups, FAST, rows // FAST, LANES), BF16),
        in_specs=[block, block],
        out_specs=pl.BlockSpec((WIDE // LANES, FAST, rows // FAST, LANES), lambda j: (j, 0, 0, 0)),
        scratch_shapes=[pltpu.VMEM((rows // FAST * GAP, LANES), F32)],
        compiler_params=PARAMS,
        cost_estimate=cost(10**6, 3 * 2**20),
        name="gate",
    )(key_in, value_in)


WIDE = 256
BATCH = 4


def pieces_of(x_ref, piece, lane, depth):
    return x_ref[piece, :, pl.ds(pl.multiple_of(lane * depth, depth), depth)]


def against(left, w_ref):
    return lax.dot_general(left, w_ref[...], (((1,), (1,)), ((), ())), preferred_element_type=F32)


def is_end(place):
    return (place[0] == 0) | (place[0] == CHIPS - 1)


def terms_kernel(place_ref, *refs):
    xs, ws, (sum_ref, x_ref, sem) = refs[:4], refs[4:10], refs[-3:]
    here, core, mine = place_ref[0], place_ref[1], place_ref[2]
    depth = ws[0].shape[1]
    inside = jnp.logical_not(is_end(place_ref))

    @pl.when(pl.program_id(0) == 0)
    def _():
        for start in (True, False):
            for i in range(4):
                apart = mine ^ i ^ here

                @pl.when((apart < 2) | (inside & (apart == CHIPS - 1)))
                def _():
                    copy = pltpu.make_async_copy(xs[i], x_ref.at[mine ^ i], sem.at[i])
                    copy.start() if start else copy.wait()

    def part(piece, near_ref, swap_ref):
        one = against(pieces_of(x_ref, piece, core, depth), near_ref)
        return one + against(pieces_of(x_ref, piece, 1 - core, depth), swap_ref)

    total = part(here, ws[0], ws[1]) + part(here ^ 1, ws[2], ws[3])

    @pl.when(inside)
    def _():
        sum_ref[...] = total + part(CHIPS - 1 - here, ws[4], ws[5])

    @pl.when(is_end(place_ref))
    def _():
        sum_ref[...] = total


def always(j, place):
    return (j, 0)


def inside_only(j, place):
    return (jnp.where(is_end(place), 0, j), 0)


def terms(place, xs, ws):
    rows, piece = xs[0].shape
    cols, depth = ws[0].shape
    maps = [always] * 4 + [inside_only] * 2
    return pl.pallas_call(
        terms_kernel,
        out_shape=sds((rows, cols), F32),
        grid_spec=pltpu.PrefetchScalarGridSpec(
            num_scalar_prefetch=1,
            grid=(cols // WIDE,),
            in_specs=[ANY] * 4 + [pl.BlockSpec((WIDE, depth), m) for m in maps],
            out_specs=pl.BlockSpec((rows, WIDE), lambda j, place: (0, j)),
            scratch_shapes=[pltpu.VMEM((4, rows, piece), BF16), pltpu.SemaphoreType.DMA((4,))],
        ),
        compiler_params=PARAMS,
        cost_estimate=cost(2 * 10**9, 14 * 2**20),
        name="terms",
    )(place, *xs, *ws)


def late_kernel(place_ref, *refs):
    xs, ws, sum_ref, query_ref, mix_ref = refs[:4], refs[4:10], refs[10], refs[11], refs[12]
    outs, (hold_ref, x_ref, sem) = refs[13:-3], refs[-3:]
    here, core, mine = place_ref[0], place_ref[1], place_ref[2]
    two_ref, three_ref = x_ref.at[pl.ds(0, 1)], x_ref.at[pl.ds(1, 1)]

    ends = is_end(place_ref)

    def fetch(start, slot, piece, needed):
        for i in range(4):

            @pl.when((pl.program_id(0) == 0) & (mine ^ piece == i) & needed)
            def _():
                copy = pltpu.make_async_copy(xs[i], x_ref.at[slot], sem.at[slot])
                copy.start() if start else copy.wait()

    fetch(True, 0, here ^ 2, True)
    fetch(True, 1, CHIPS - 1 - here, ends)
    fetch(False, 0, here ^ 2, True)
    depth = ws[0].shape[1]
    per = sum_ref.shape[0] // FAST

    def part(piece_ref, near_ref, swap_ref):
        one = against(pieces_of(piece_ref, 0, core, depth), near_ref)
        return one + against(pieces_of(piece_ref, 0, 1 - core, depth), swap_ref)

    def give(total):
        mix = total.astype(BF16)
        mix_ref[...] = mix
        scaled = mix.astype(F32) * query_ref[...].astype(F32)
        for g in range(BATCH):
            write_gapped(hold_ref.at[g], 0, scaled[:, g * LANES : (g + 1) * LANES])

    @pl.when(ends)
    def _():
        total = sum_ref[...] + part(two_ref, ws[2], ws[3])
        fetch(False, 1, CHIPS - 1 - here, ends)
        give(total + part(three_ref, ws[4], ws[5]))

    @pl.when(jnp.logical_not(ends))
    def _():
        give(sum_ref[...] + part(two_ref, ws[0], ws[1]))

    for k in range(2 * CHIPS // BATCH):

        @pl.when(pl.program_id(0) == k)
        def _():
            for e in range(BATCH):
                for a in range(FAST):
                    outs[OUTWARD.index(BATCH * k + e)][a] = hold_ref[e ^ (place_ref[3] % BATCH), pl.ds(a, per, stride=GAP), :].astype(BF16)


def mix_late(place, xs, ws, total, query):
    rows, cols = query.shape
    depth = ws[0].shape[1]

    def block(j, place):
        return j ^ (place[3] // BATCH)

    def inner(j, place):
        return (jnp.where(is_end(place), 0, block(j, place)), 0)

    def outer(j, place):
        return (jnp.where(is_end(place), block(j, place), 0), 0)

    wide = pl.BlockSpec((rows, BATCH * LANES), lambda j, place: (0, block(j, place)))
    part = pl.BlockSpec((FAST, rows // FAST, LANES), lambda j, place: (0, 0, 0))
    grad_mix, *scaled = pl.pallas_call(
        late_kernel,
        out_shape=(sds((rows, cols), BF16),) + (sds((FAST, rows // FAST, LANES), BF16),) * (2 * CHIPS),
        grid_spec=pltpu.PrefetchScalarGridSpec(
            num_scalar_prefetch=1,
            grid=(2 * CHIPS // BATCH,),
            in_specs=[ANY] * 4
            + [pl.BlockSpec((BATCH * LANES, depth), m) for m in (inner, inner, outer, outer, outer, outer)]
            + [wide, wide],
            out_specs=(wide,) + (part,) * (2 * CHIPS),
            scratch_shapes=[
                pltpu.VMEM((BATCH, rows // FAST * GAP, LANES), F32),
                pltpu.VMEM((2,) + xs[0].shape, BF16),
                pltpu.SemaphoreType.DMA((2,)),
            ],
        ),
        compiler_params=PARAMS,
        cost_estimate=cost(10**9, 8 * 2**20),
        name="mix_late",
    )(place, *xs, *ws, total, query)
    return grad_mix, scaled


def finish_kernel(count, place_ref, *refs):
    parts, factors, outs = refs[: 2 * CHIPS], refs[2 * CHIPS : 2 * CHIPS + count], refs[2 * CHIPS + count : -1]
    hold_ref = refs[-1]
    here = place_ref[3] % BATCH
    per = parts[0].shape[1]
    for k in range(2 * CHIPS // BATCH):

        @pl.when(pl.program_id(0) == k)
        def _():
            for e in range(BATCH):
                for a in range(FAST):
                    hold_ref[e ^ here, pl.ds(a, per, stride=GAP), :] = parts[HOMEWARD.index(BATCH * k + e)][a].astype(F32)

    for g in range(BATCH):
        lanes = pl.ds(g * LANES, LANES)
        value = read_gapped(hold_ref.at[g], 0, per)
        for factor_ref, out_ref in zip(factors, outs):
            out_ref[:, lanes] = (value * factor_ref[:, lanes].astype(F32)).astype(BF16)


def finish(place, parts, *factors):
    rows, cols = factors[0].shape
    count = len(factors)
    block = pl.BlockSpec((rows, BATCH * LANES), lambda j, place: (0, j ^ (place[3] // BATCH)))
    part = pl.BlockSpec(parts[0].shape, lambda j, place: (0, 0, 0))
    return pl.pallas_call(
        functools.partial(finish_kernel, count),
        out_shape=(sds((rows, cols), BF16),) * count,
        grid_spec=pltpu.PrefetchScalarGridSpec(
            num_scalar_prefetch=1,
            grid=(2 * CHIPS // BATCH,),
            in_specs=[part] * (2 * CHIPS) + [block] * count,
            out_specs=(block,) * count,
            scratch_shapes=[pltpu.VMEM((BATCH, rows // FAST * GAP, LANES), F32)],
        ),
        compiler_params=PARAMS,
        cost_estimate=cost(10**6, (1 + 2 * count) * 2**20),
        name="finish",
    )(place, *parts, *factors)


def finish_whole_kernel(part_ref, factor_ref, out_ref, hold_ref):
    per = part_ref.shape[2]
    for g in range(2):
        for a in range(FAST):
            hold_ref[pl.ds(a, per, stride=GAP), :] = part_ref[g, a].astype(F32)
        lanes = pl.ds(g * LANES, LANES)
        out_ref[:, lanes] = (read_gapped(hold_ref, 0, per) * factor_ref[:, lanes].astype(F32)).astype(BF16)


def finish_whole(parts, factor):
    rows, cols = factor.shape
    wide = pl.BlockSpec((rows, WIDE), lambda j: (0, j))
    part = pl.BlockSpec((2,) + parts.shape[1:], lambda j: (j, 0, 0, 0))
    return pl.pallas_call(
        finish_whole_kernel,
        out_shape=sds((rows, cols), BF16),
        grid=(CHIPS,),
        in_specs=[part, wide],
        out_specs=wide,
        scratch_shapes=[pltpu.VMEM((rows // FAST * GAP, LANES), F32)],
        compiler_params=PARAMS,
        cost_estimate=cost(10**6, 3 * 2**20),
        name="finish_whole",
    )(parts, factor)


def exchange(parts):
    return lax.all_to_all(parts, "ctx", split_axis=0, concat_axis=0, tiled=True)


def scatter(parts, reach):
    ids = range(2 * CHIPS)
    return [lax.ppermute(part, "ctx", [(i, i ^ d) for i in ids]) if d else part for part, d in zip(parts, reach)]


SWAP = [(i, i ^ 1) for i in range(8)]
SIDE = [(i, i ^ 2) for i in range(8)]
MIDDLE = [(2, 4), (3, 5), (4, 2), (5, 3)]
OUT = [(2, 0), (3, 1), (4, 6), (5, 7)]
INNER_SWAP, END_SWAP = SWAP[2:6], SWAP[:2] + SWAP[6:]


def to(x, pairs):
    return lax.ppermute(x, "ctx", pairs)


def lane_body(grad_out, proj_out, query, key_in, value_in, filters):
    seq = filters.shape[1]
    groups = seq // key_in.shape[0]
    firsts, fwd, inv, lasts = tables(seq)
    tie = lax.optimization_barrier
    ctx = lax.axis_index("ctx")
    place = jnp.stack([ctx // 2, ctx % 2, lax.axis_index("mp"), ctx]).astype(jnp.int32)
    index = ctx.astype(jnp.int32)[None]

    def across(x, d):
        return lax.ppermute(x, "mp", [(i, i ^ d) for i in range(4)])

    side, middle = to(proj_out, SIDE), to(proj_out, MIDDLE)
    x1, x2 = across(grad_out, 1), across(grad_out, 2)
    gated = exchange(gate(key_in, value_in, groups))
    spec = filter_spectrum(filters, (firsts[-1], fwd))
    side, middle, spec = tie((side, middle, spec))

    crossed, sent_out = to(side, MIDDLE), to(middle, OUT)
    ws = [side, to(side, SWAP), middle, to(middle, INNER_SWAP)]
    x3, own, *_ = tie((grad_out, proj_out, x1, x2, ws[1], ws[3]))
    ws = [own, to(own, SWAP)] + ws
    xs = [grad_out, x1, x2, across(x3, 3)]
    (conv,), gated_spec = convolve(jnp.full_like(index, 2 * CHIPS), [gated], spec, (firsts, fwd, inv, lasts), False, True)
    crossed, _ = tie((crossed, conv))

    last = to(crossed, OUT)
    total = terms(place, xs, ws)
    conv, _ = tie((conv, total))
    conv = exchange(conv)
    ws = [crossed, to(crossed, INNER_SWAP), sent_out, to(sent_out, END_SWAP)]
    last, _ = tie((last, total))
    ws += [last, to(last, END_SWAP)]
    grad_mix, scaled = mix_late(place, xs, ws, total, query)
    scaled = scatter(scaled, OUTWARD)
    *scaled, conv = tie((*scaled, conv))
    back, scaled_spec = convolve(index, scaled, spec, (firsts, fwd, inv, lasts), True, False)
    back = scatter(back, HOMEWARD)
    filter_grad = filter_gradient(scaled_spec, gated_spec, (None, fwd, inv, lasts[-1]), 1.0 / math.sqrt(seq))
    grad_query = finish_whole(conv, grad_mix)
    grad_key, grad_value = finish(place, back, value_in, key_in)
    return (grad_query, grad_key, grad_value, filter_grad)


def body(grad_out, proj_out, query, key_in, value_in, filters):
    rows, cols = key_in.shape
    lanes, seq = filters.shape
    fits = (
        lax.axis_size("ctx") == 2 * CHIPS
        and lax.axis_size("mp") == 4
        and lanes == LANES
        and rows % (16 * FAST) == 0
        and cols == 2 * CHIPS * LANES
        and seq == 2 * CHIPS * rows
        and seq == FAST * LANES
        and grad_out.shape[1] == 2 * proj_out.shape[1]
    )
    args = (grad_out, proj_out, query, key_in, value_in, filters)
    return lane_body(*args) if fits else general_body(*args)


def solution(mesh):
    return jax.shard_map(
        body,
        mesh=mesh,
        in_specs=(
            P("ctx", "mp"),
            P("mp", "ctx"),
            P("ctx", "mp"),
            P("ctx", "mp"),
            P("ctx", "mp"),
            P(("mp", "ctx"), None),
        ),
        out_specs=(P("ctx", "mp"), P("ctx", "mp"), P("ctx", "mp"), P(("mp", "ctx"), None)),
        check_vma=False,
    )
```

```python
import functools
import math

import jax
import jax.numpy as jnp
import ml_dtypes
import numpy as np
from jax import lax
from jax.experimental import pallas as pl
from jax.experimental.pallas import tpu as pltpu
from jax.sharding import PartitionSpec as P


def phase_table(rows_n, cols_n, modulus):
    prod_idx = (
        jnp.arange(rows_n, dtype=jnp.int32)[:, None]
        * jnp.arange(cols_n, dtype=jnp.int32)[None, :]
        % modulus
    )
    angles = prod_idx.astype(jnp.float32) * (2.0 * math.pi / modulus)
    return (jnp.cos(angles), jnp.sin(angles))


def make_tables(length_all):
    size_second = min(128, length_all)
    size_first = length_all // size_second
    cos_first, sin_first = phase_table(size_first, size_first, size_first)
    twist_cos, twist_sin = phase_table(size_first, size_second, length_all)
    cos_second, sin_second = phase_table(size_second, size_second, size_second)
    return (cos_first, sin_first, twist_cos, twist_sin, cos_second, sin_second)


def contract(form, left, right):
    return jnp.einsum(form, left, right, precision=lax.Precision.HIGHEST)


def forward_real(signal, tables):
    cos_first, sin_first, twist_cos, twist_sin, cos_second, sin_second = tables
    part_re = contract("kn,cnm->ckm", cos_first, signal)
    part_im = -contract("kn,cnm->ckm", sin_first, signal)
    turned_re = part_re * twist_cos + part_im * twist_sin
    turned_im = part_im * twist_cos - part_re * twist_sin
    spec_re = contract("ckm,mj->ckj", turned_re, cos_second) + contract(
        "ckm,mj->ckj", turned_im, sin_second
    )
    spec_im = contract("ckm,mj->ckj", turned_im, cos_second) - contract(
        "ckm,mj->ckj", turned_re, sin_second
    )
    return (spec_re, spec_im)


def inverse_real(spec_re, spec_im, tables):
    cos_first, sin_first, twist_cos, twist_sin, cos_second, sin_second = tables
    back_re = contract("ckj,jm->ckm", spec_re, cos_second) - contract(
        "ckj,jm->ckm", spec_im, sin_second
    )
    back_im = contract("ckj,jm->ckm", spec_re, sin_second) + contract(
        "ckj,jm->ckm", spec_im, cos_second
    )
    twist_re = back_re * twist_cos - back_im * twist_sin
    twist_im = back_re * twist_sin + back_im * twist_cos
    return contract("nk,ckm->cnm", cos_first, twist_re) - contract(
        "nk,ckm->cnm", sin_first, twist_im
    )


def long_filter_grads(gated, scaled, kernel):
    channels, seq_len = kernel.shape
    length_all = 2 * seq_len
    tables = make_tables(length_all)
    spec_shape = (channels, tables[0].shape[0], tables[4].shape[0])

    def padded(values):
        wide = jnp.concatenate(
            [values.astype(jnp.float32), jnp.zeros((channels, seq_len), jnp.float32)], axis=1
        )
        return wide.reshape(spec_shape)

    def restore(spec_re, spec_im):
        return (
            inverse_real(spec_re, spec_im, tables).reshape(channels, length_all)[:, :seq_len]
            / length_all
        )

    gated_re, gated_im = forward_real(padded(gated), tables)
    scaled_re, scaled_im = forward_real(padded(scaled), tables)
    kernel_re, kernel_im = forward_real(padded(kernel), tables)
    conv_out = restore(
        kernel_re * gated_re - kernel_im * gated_im, kernel_re * gated_im + kernel_im * gated_re
    )
    grad_gated = restore(
        scaled_re * kernel_re + scaled_im * kernel_im, scaled_im * kernel_re - scaled_re * kernel_im
    )
    grad_kernel = restore(
        scaled_re * gated_re + scaled_im * gated_im, scaled_im * gated_re - scaled_re * gated_im
    )
    filter_grad = grad_kernel / math.sqrt(seq_len)
    return (conv_out.astype(jnp.bfloat16), grad_gated.astype(jnp.bfloat16), filter_grad)


def product(left, right):
    return (left.astype(jnp.float32) * right.astype(jnp.float32)).astype(jnp.bfloat16)


def general_body(grad_out, proj_out, query, key_in, value_in, filters):
    weight_rows = lax.all_gather(proj_out, "ctx", axis=1, tiled=True)
    grad_mix = lax.dot_general(
        lax.all_gather(grad_out, "mp", axis=1, tiled=True),
        weight_rows,
        (((1,), (1,)), ((), ())),
        preferred_element_type=jnp.float32,
    ).astype(jnp.bfloat16)
    gated = product(key_in, value_in)
    scaled = product(grad_mix, query)
    chan_gated, chan_scaled = (
        lax.all_to_all(gated.T, "ctx", split_axis=0, concat_axis=1, tiled=True),
        lax.all_to_all(scaled.T, "ctx", split_axis=0, concat_axis=1, tiled=True),
    )
    conv_out, grad_gated, filter_grad = long_filter_grads(chan_gated, chan_scaled, filters)
    back_grad, back_conv = (
        lax.all_to_all(grad_gated, "ctx", split_axis=1, concat_axis=0, tiled=True),
        lax.all_to_all(conv_out, "ctx", split_axis=1, concat_axis=0, tiled=True),
    )
    grad_query = product(grad_mix, back_conv.T)
    grad_key = product(back_grad.T, value_in)
    grad_value = product(back_grad.T, key_in)
    return (grad_query, grad_key, grad_value, filter_grad)


FAST = 32
SLOT = 2 * FAST
PAIR = 2 * SLOT
STEP = SLOT + 8
GAP = FAST + 8
LANES = 128
CHIPS = 4
OUTWARD = (6, 4, 2, 7, 5, 3, 1, 0)
HOMEWARD = (6, 2, 3, 7, 4, 5, 1, 0)
F32, BF16 = jnp.float32, jnp.bfloat16
PARAMS = pltpu.CompilerParams(vmem_limit_bytes=63 * 2**20)
SMALL = pltpu.CompilerParams(vmem_limit_bytes=52 * 2**20)
VM = pl.BlockSpec(memory_space=pltpu.VMEM)
ANY = pl.BlockSpec(memory_space=pl.ANY)
HBM = pl.BlockSpec(memory_space=pltpu.HBM)
U1, U2 = 32, 64


def sds(shape, dtype):
    return jax.ShapeDtypeStruct(shape, dtype)


def cost(flops, moved):
    return pl.CostEstimate(flops=flops // 10**6, bytes_accessed=moved // 10**3, transcendentals=0)


def tables(seq):
    size = 2 * seq
    slow = size // FAST
    half = slow // 2
    s = np.arange(half)
    angle = 2 * np.pi * ((s[:, None] * s[None, :]) % slow) / slow
    first = np.concatenate([np.cos(angle), -np.sin(angle)], 0)
    first[half] = 1.0 - 2.0 * (s % 2)
    weight = np.full((2 * half, 1), 2.0)
    weight[0] = weight[half] = 1.0
    last = (first * weight).T / size
    a = np.arange(FAST)
    k = np.arange(half + 1)[:, None] + slow * a[None, :]
    turn = 2 * np.pi * ((k[:, :, None] * a[None, None, :]) % size) / size
    c, d = np.cos(turn), np.sin(turn)
    fwd = np.concatenate([np.concatenate([c, d], 2), np.concatenate([-d, c], 2)], 1)
    inv = fwd.transpose(0, 2, 1).copy()
    fwd[0, :, FAST:] = 0.0
    inv[0, FAST:] = 0.0

    def paired(blocks):
        out = np.zeros((half // 2 + 1, SLOT, PAIR))
        out[:-1, :, :SLOT] = blocks[0:half:2]
        out[:-1, :, SLOT:] = blocks[1:half:2]
        return out

    fwd, inv, edge_fwd, edge_inv = paired(fwd), paired(inv), fwd[half], inv[half]
    fwd[-1, :, FAST:SLOT] = edge_fwd[:, :FAST]
    inv[-1, FAST:, :SLOT] = edge_inv[:FAST]
    blocks = np.arange(half).reshape(2 * CHIPS, -1)

    def orders(reach):
        return [np.concatenate([blocks[c ^ d] for d in reach]) for c in range(2 * CHIPS)] + [np.arange(half)]

    firsts = np.stack([first[:, o] for o in orders(OUTWARD)])
    lasts = np.stack([last[o] for o in orders(HOMEWARD)])
    return [jnp.asarray(t.astype(ml_dtypes.bfloat16)) for t in (firsts, fwd, inv, lasts)]


def dot(left, right):
    return jnp.dot(left, right, preferred_element_type=F32)


def pair_dot(pair, rows):
    low = lax.broadcasted_iota(jnp.int32, pair.shape, 1) < SLOT
    zero = jnp.zeros_like(pair)
    return dot(jnp.concatenate([jnp.where(low, pair, zero), jnp.where(low, zero, pair)], 0), rows)


def loop(count, unroll, step):
    def some(i, carry):
        for u in range(unroll):
            step(i * unroll + u)
        return carry

    lax.fori_loop(0, count // unroll, some, 0)


def span(start, size):
    return pl.ds(pl.multiple_of(start * size, size), size)


def slots(ref, p):
    return [ref.at[pl.ds(pl.multiple_of(p * 2 * STEP + i * STEP, 8), SLOT), :] for i in range(2)]


def read_slots(ref, p):
    return jnp.concatenate([rows[...] for rows in slots(ref, p)], 0).astype(BF16)


def write_slots(ref, p, value):
    for i, rows in enumerate(slots(ref, p)):
        rows[...] = value[i * SLOT : (i + 1) * SLOT]


def gapped(ref, index, count):
    return [ref.at[pl.ds(pl.multiple_of((index * count + i) * GAP, 8), FAST), :] for i in range(count)]


def read_gapped(ref, index, count):
    return jnp.concatenate([rows[...] for rows in gapped(ref, index, count)], 0)


def write_gapped(ref, index, value):
    for i, rows in enumerate(gapped(ref, index, value.shape[0] // FAST)):
        rows[...] = value[i * FAST : (i + 1) * FAST]


def spread(signal, first_ref, mid_ref):
    half = first_ref.shape[1]

    def step(a):
        out = dot(first_ref[...], signal(a))
        mid_ref[pl.ds(a, half, stride=STEP), :] = out[:half]
        mid_ref[pl.ds(FAST + a, half, stride=STEP), :] = out[half:]

    loop(FAST, U1, step)


def collect(last_ref, back_ref, emit):
    half = last_ref.shape[0]

    def step(a):
        re = back_ref[pl.ds(a, half, stride=STEP), :]
        im = back_ref[pl.ds(FAST + a, half, stride=STEP), :]
        emit(a, dot(last_ref[...], jnp.concatenate([re, im], 0).astype(BF16)))

    loop(FAST, U1, step)


def times(x, y, conjugate):
    x, y = x.astype(F32), y.astype(F32)
    parts = []
    for i in range(0, x.shape[0], SLOT):
        xr, xi, yr, yi = (v[i + j : i + j + FAST] for v in (x, y) for j in (0, FAST))
        if conjugate:
            parts += [xr * yr + xi * yi, xi * yr - xr * yi]
        else:
            parts += [xr * yr - xi * yi, xr * yi + xi * yr]
    return jnp.concatenate(parts, 0).astype(BF16)


def filter_kernel(h_ref, first_ref, fwd_ref, spec_ref, time_ref, mid_ref):
    half = first_ref.shape[1]
    seq = h_ref.shape[1]

    def turn(i):
        write_gapped(time_ref, i, h_ref[:, span(i, LANES)].T)

    loop(seq // LANES, 8, turn)
    spread(lambda a: time_ref[pl.ds(a, half, stride=GAP), :].astype(BF16), first_ref, mid_ref)

    def step(p):
        spec_ref[span(p, PAIR), :] = pair_dot(fwd_ref[p], read_slots(mid_ref, p)).astype(BF16)

    loop(half // 2, U2, step)
    spec_ref[span(half // 2, PAIR), :] = pair_dot(fwd_ref[half // 2], read_slots(mid_ref, 0)).astype(BF16)


def convolve_kernel(conjugate, count, place_ref, *refs):
    x_refs, (h_any, first_ref, fwd_any, inv_any, last_ref) = refs[:count], refs[count : count + 5]
    outs, (spec_any, h_ref, fwd_ref, inv_ref, spec_ref, mid_ref, back_ref, sem) = refs[count + 5 : -8], refs[-8:]
    first_ref, last_ref = first_ref.at[0], last_ref.at[0]
    half = first_ref.shape[1]
    loads = [
        pltpu.make_async_copy(source, target, sem.at[i])
        for i, (source, target) in enumerate(((fwd_any, fwd_ref), (h_any, h_ref), (inv_any, inv_ref)))
    ]
    for load in loads:
        load.start()
    if count == 1:
        spread(lambda a: x_refs[0][:, a].reshape(half, LANES), first_ref, mid_ref)
    else:
        spread(lambda a: jnp.concatenate([x_ref[a] for x_ref in x_refs], 0), first_ref, mid_ref)
    for load in loads:
        load.wait()

    def step(p):
        x = pair_dot(fwd_ref[p], read_slots(mid_ref, p))
        spec_ref[span(p, PAIR), :] = x.astype(BF16)
        write_slots(back_ref, p, pair_dot(inv_ref[p], times(x, h_ref[span(p, PAIR), :], conjugate)))

    loop(half // 2, U2, step)
    tail = span(half // 2, PAIR)
    x = pair_dot(fwd_ref[half // 2], read_slots(mid_ref, 0))
    spec_ref[tail, :] = x.astype(BF16)
    store = pltpu.make_async_copy(spec_ref, spec_any, sem.at[3])
    store.start()
    back_ref[:SLOT, :] += pair_dot(inv_ref[half // 2], times(x, h_ref[tail, :], conjugate))[:SLOT]
    if len(outs) == 1:

        def emit(a, rows):
            outs[0][:, a] = rows.reshape(outs[0].shape[0], -1, LANES).astype(BF16)

        collect(last_ref, back_ref, emit)
    else:
        per = half // len(outs)

        def emit(a, rows):
            for i, out_ref in enumerate(outs):
                out_ref[a] = rows[i * per : (i + 1) * per].astype(BF16)

        collect(last_ref, back_ref, emit)
    store.wait()


def gradient_kernel(scale, s_ref, g_ref, inv_ref, last_ref, out_ref, time_ref, back_ref):
    half = last_ref.shape[0]
    seq = out_ref.shape[1]

    def step(p):
        rows = span(p, PAIR)
        write_slots(back_ref, p, pair_dot(inv_ref[p], times(s_ref[rows, :], g_ref[rows, :], True)))

    loop(half // 2, U2, step)
    tail = span(half // 2, PAIR)
    back_ref[:SLOT, :] += pair_dot(inv_ref[half // 2], times(s_ref[tail, :], g_ref[tail, :], True))[:SLOT]

    def emit(a, rows):
        time_ref[pl.ds(a, half, stride=GAP), :] = rows * scale

    collect(last_ref, back_ref, emit)

    def turn(i):
        out_ref[:, span(i, LANES)] = read_gapped(time_ref, i, LANES // FAST).T

    loop(seq // LANES, 8, turn)


def filter_spectrum(h, tabs):
    first, fwd = tabs[:2]
    seq = h.shape[1]
    return pl.pallas_call(
        filter_kernel,
        out_shape=sds((2 * seq + PAIR, LANES), BF16),
        in_specs=[VM] * 3,
        out_specs=VM,
        scratch_shapes=[pltpu.VMEM((seq // FAST * GAP, LANES), F32), pltpu.VMEM((seq // FAST * STEP, LANES), F32)],
        compiler_params=PARAMS,
        cost_estimate=cost(10**9, 8 * 2**20),
        name="filter_spectrum",
    )(h, first, fwd)


def convolve(index, parts, spec, tabs, conjugate, whole):
    first, fwd, inv, last = tabs
    count = len(parts)
    groups = 2 * CHIPS
    half = last.shape[1]

    def own(table):
        return pl.BlockSpec((1,) + table.shape[1:], lambda i, index: (index[0], 0, 0))

    outs = (sds((FAST, half // groups, LANES), BF16),) * groups
    if whole:
        outs = (sds((groups, FAST, half // groups, LANES), BF16),)
    big = pltpu.VMEM((half * STEP, LANES), F32)
    *out, spec = pl.pallas_call(
        functools.partial(convolve_kernel, conjugate, count),
        out_shape=outs + (sds(spec.shape, BF16),),
        grid_spec=pltpu.PrefetchScalarGridSpec(
            num_scalar_prefetch=1,
            grid=(1,),
            in_specs=[VM] * count + [HBM, own(first), HBM, HBM, own(last)],
            out_specs=(VM,) * len(outs) + (HBM,),
            scratch_shapes=[
                pltpu.VMEM(spec.shape, BF16),
                pltpu.VMEM(fwd.shape, BF16),
                pltpu.VMEM(fwd.shape, BF16),
                pltpu.VMEM(spec.shape, BF16),
                big,
                big,
                pltpu.SemaphoreType.DMA((4,)),
            ],
        ),
        compiler_params=SMALL,
        cost_estimate=cost(2 * 10**9, 14 * 2**20),
        name="convolve",
    )(index, *parts, spec, *tabs)
    return out, spec


def filter_gradient(scaled_spec, gated_spec, tabs, scale):
    inv, last = tabs[2:]
    seq = (scaled_spec.shape[0] - PAIR) // 2
    return pl.pallas_call(
        functools.partial(gradient_kernel, scale),
        out_shape=sds((LANES, seq), F32),
        in_specs=[VM] * 4,
        out_specs=VM,
        scratch_shapes=[pltpu.VMEM((seq // FAST * GAP, LANES), F32), pltpu.VMEM((seq // FAST * STEP, LANES), F32)],
        compiler_params=PARAMS,
        cost_estimate=cost(10**9, 12 * 2**20),
        name="filter_gradient",
    )(scaled_spec, gated_spec, inv, last)


def permuted(value, hold_ref, emit):
    write_gapped(hold_ref, 0, value)
    per = value.shape[0] // FAST
    for a in range(FAST):
        emit(a, hold_ref[pl.ds(a, per, stride=GAP), :].astype(BF16))


def gate_kernel(key_ref, value_ref, out_ref, hold_ref):
    product = key_ref[...].astype(F32) * value_ref[...].astype(F32)
    for g in range(WIDE // LANES):

        def emit(a, rows):
            out_ref[g, a] = rows

        permuted(product[:, g * LANES : (g + 1) * LANES], hold_ref, emit)


def gate(key_in, value_in, groups):
    rows, cols = key_in.shape
    block = pl.BlockSpec((rows, WIDE), lambda j: (0, j))
    return pl.pallas_call(
        gate_kernel,
        grid=(cols // WIDE,),
        out_shape=sds((groups, FAST, rows // FAST, LANES), BF16),
        in_specs=[block, block],
        out_specs=pl.BlockSpec((WIDE // LANES, FAST, rows // FAST, LANES), lambda j: (j, 0, 0, 0)),
        scratch_shapes=[pltpu.VMEM((rows // FAST * GAP, LANES), F32)],
        compiler_params=PARAMS,
        cost_estimate=cost(10**6, 3 * 2**20),
        name="gate",
    )(key_in, value_in)


WIDE = 256
BATCH = 4


def pieces_of(x_ref, piece, lane, depth):
    return x_ref[piece, :, pl.ds(pl.multiple_of(lane * depth, depth), depth)]


def against(left, w_ref):
    return lax.dot_general(left, w_ref[...], (((1,), (1,)), ((), ())), preferred_element_type=F32)


def is_end(place):
    return (place[0] == 0) | (place[0] == CHIPS - 1)


def terms_kernel(place_ref, *refs):
    xs, ws, (sum_ref, x_ref, sem) = refs[:4], refs[4:10], refs[-3:]
    here, core, mine = place_ref[0], place_ref[1], place_ref[2]
    depth = ws[0].shape[1]
    inside = jnp.logical_not(is_end(place_ref))

    @pl.when(pl.program_id(0) == 0)
    def _():
        for start in (True, False):
            for i in range(4):
                apart = mine ^ i ^ here

                @pl.when((apart < 2) | (inside & (apart == CHIPS - 1)))
                def _():
                    copy = pltpu.make_async_copy(xs[i], x_ref.at[mine ^ i], sem.at[i])
                    copy.start() if start else copy.wait()

    def part(piece, near_ref, swap_ref):
        one = against(pieces_of(x_ref, piece, core, depth), near_ref)
        return one + against(pieces_of(x_ref, piece, 1 - core, depth), swap_ref)

    total = part(here, ws[0], ws[1]) + part(here ^ 1, ws[2], ws[3])

    @pl.when(inside)
    def _():
        sum_ref[...] = total + part(CHIPS - 1 - here, ws[4], ws[5])

    @pl.when(is_end(place_ref))
    def _():
        sum_ref[...] = total


def always(j, place):
    return (j, 0)


def inside_only(j, place):
    return (jnp.where(is_end(place), 0, j), 0)


def terms(place, xs, ws):
    rows, piece = xs[0].shape
    cols, depth = ws[0].shape
    maps = [always] * 4 + [inside_only] * 2
    return pl.pallas_call(
        terms_kernel,
        out_shape=sds((rows, cols), F32),
        grid_spec=pltpu.PrefetchScalarGridSpec(
            num_scalar_prefetch=1,
            grid=(cols // WIDE,),
            in_specs=[ANY] * 4 + [pl.BlockSpec((WIDE, depth), m) for m in maps],
            out_specs=pl.BlockSpec((rows, WIDE), lambda j, place: (0, j)),
            scratch_shapes=[pltpu.VMEM((4, rows, piece), BF16), pltpu.SemaphoreType.DMA((4,))],
        ),
        compiler_params=PARAMS,
        cost_estimate=cost(2 * 10**9, 14 * 2**20),
        name="terms",
    )(place, *xs, *ws)


def late_kernel(place_ref, *refs):
    xs, ws, sum_ref, query_ref, mix_ref = refs[:4], refs[4:10], refs[10], refs[11], refs[12]
    outs, (hold_ref, x_ref, sem) = refs[13:-3], refs[-3:]
    here, core, mine = place_ref[0], place_ref[1], place_ref[2]
    two_ref, three_ref = x_ref.at[pl.ds(0, 1)], x_ref.at[pl.ds(1, 1)]

    ends = is_end(place_ref)

    def fetch(start, slot, piece, needed):
        for i in range(4):

            @pl.when((pl.program_id(0) == 0) & (mine ^ piece == i) & needed)
            def _():
                copy = pltpu.make_async_copy(xs[i], x_ref.at[slot], sem.at[slot])
                copy.start() if start else copy.wait()

    fetch(True, 0, here ^ 2, True)
    fetch(True, 1, CHIPS - 1 - here, ends)
    fetch(False, 0, here ^ 2, True)
    depth = ws[0].shape[1]
    per = sum_ref.shape[0] // FAST

    def part(piece_ref, near_ref, swap_ref):
        one = against(pieces_of(piece_ref, 0, core, depth), near_ref)
        return one + against(pieces_of(piece_ref, 0, 1 - core, depth), swap_ref)

    def give(total):
        mix = total.astype(BF16)
        mix_ref[...] = mix
        scaled = mix.astype(F32) * query_ref[...].astype(F32)
        for g in range(BATCH):
            write_gapped(hold_ref.at[g], 0, scaled[:, g * LANES : (g + 1) * LANES])

    @pl.when(ends)
    def _():
        total = sum_ref[...] + part(two_ref, ws[2], ws[3])
        fetch(False, 1, CHIPS - 1 - here, ends)
        give(total + part(three_ref, ws[4], ws[5]))

    @pl.when(jnp.logical_not(ends))
    def _():
        give(sum_ref[...] + part(two_ref, ws[0], ws[1]))

    for k in range(2 * CHIPS // BATCH):

        @pl.when(pl.program_id(0) == k)
        def _():
            for e in range(BATCH):
                for a in range(FAST):
                    outs[OUTWARD.index(BATCH * k + e)][a] = hold_ref[e ^ (place_ref[3] % BATCH), pl.ds(a, per, stride=GAP), :].astype(BF16)


def mix_late(place, xs, ws, total, query):
    rows, cols = query.shape
    depth = ws[0].shape[1]

    def block(j, place):
        return j ^ (place[3] // BATCH)

    def inner(j, place):
        return (jnp.where(is_end(place), 0, block(j, place)), 0)

    def outer(j, place):
        return (jnp.where(is_end(place), block(j, place), 0), 0)

    wide = pl.BlockSpec((rows, BATCH * LANES), lambda j, place: (0, block(j, place)))
    part = pl.BlockSpec((FAST, rows // FAST, LANES), lambda j, place: (0, 0, 0))
    grad_mix, *scaled = pl.pallas_call(
        late_kernel,
        out_shape=(sds((rows, cols), BF16),) + (sds((FAST, rows // FAST, LANES), BF16),) * (2 * CHIPS),
        grid_spec=pltpu.PrefetchScalarGridSpec(
            num_scalar_prefetch=1,
            grid=(2 * CHIPS // BATCH,),
            in_specs=[ANY] * 4
            + [pl.BlockSpec((BATCH * LANES, depth), m) for m in (inner, inner, outer, outer, outer, outer)]
            + [wide, wide],
            out_specs=(wide,) + (part,) * (2 * CHIPS),
            scratch_shapes=[
                pltpu.VMEM((BATCH, rows // FAST * GAP, LANES), F32),
                pltpu.VMEM((2,) + xs[0].shape, BF16),
                pltpu.SemaphoreType.DMA((2,)),
            ],
        ),
        compiler_params=PARAMS,
        cost_estimate=cost(10**9, 8 * 2**20),
        name="mix_late",
    )(place, *xs, *ws, total, query)
    return grad_mix, scaled


def finish_kernel(count, place_ref, *refs):
    parts, factors, outs = refs[: 2 * CHIPS], refs[2 * CHIPS : 2 * CHIPS + count], refs[2 * CHIPS + count : -1]
    hold_ref = refs[-1]
    here = place_ref[3] % BATCH
    per = parts[0].shape[1]
    for k in range(2 * CHIPS // BATCH):

        @pl.when(pl.program_id(0) == k)
        def _():
            for e in range(BATCH):
                for a in range(FAST):
                    hold_ref[e ^ here, pl.ds(a, per, stride=GAP), :] = parts[HOMEWARD.index(BATCH * k + e)][a].astype(F32)

    for g in range(BATCH):
        lanes = pl.ds(g * LANES, LANES)
        value = read_gapped(hold_ref.at[g], 0, per)
        for factor_ref, out_ref in zip(factors, outs):
            out_ref[:, lanes] = (value * factor_ref[:, lanes].astype(F32)).astype(BF16)


def finish(place, parts, *factors):
    rows, cols = factors[0].shape
    count = len(factors)
    block = pl.BlockSpec((rows, BATCH * LANES), lambda j, place: (0, j ^ (place[3] // BATCH)))
    part = pl.BlockSpec(parts[0].shape, lambda j, place: (0, 0, 0))
    return pl.pallas_call(
        functools.partial(finish_kernel, count),
        out_shape=(sds((rows, cols), BF16),) * count,
        grid_spec=pltpu.PrefetchScalarGridSpec(
            num_scalar_prefetch=1,
            grid=(2 * CHIPS // BATCH,),
            in_specs=[part] * (2 * CHIPS) + [block] * count,
            out_specs=(block,) * count,
            scratch_shapes=[pltpu.VMEM((BATCH, rows // FAST * GAP, LANES), F32)],
        ),
        compiler_params=SMALL,
        cost_estimate=cost(10**6, (1 + 2 * count) * 2**20),
        name="finish",
    )(place, *parts, *factors)


def finish_whole_kernel(part_ref, factor_ref, out_ref, hold_ref):
    per = part_ref.shape[2]
    for g in range(2):
        for a in range(FAST):
            hold_ref[pl.ds(a, per, stride=GAP), :] = part_ref[g, a].astype(F32)
        lanes = pl.ds(g * LANES, LANES)
        out_ref[:, lanes] = (read_gapped(hold_ref, 0, per) * factor_ref[:, lanes].astype(F32)).astype(BF16)


def finish_whole(parts, factor):
    rows, cols = factor.shape
    wide = pl.BlockSpec((rows, WIDE), lambda j: (0, j))
    part = pl.BlockSpec((2,) + parts.shape[1:], lambda j: (j, 0, 0, 0))
    return pl.pallas_call(
        finish_whole_kernel,
        out_shape=sds((rows, cols), BF16),
        grid=(CHIPS,),
        in_specs=[part, wide],
        out_specs=wide,
        scratch_shapes=[pltpu.VMEM((rows // FAST * GAP, LANES), F32)],
        compiler_params=PARAMS,
        cost_estimate=cost(10**6, 3 * 2**20),
        name="finish_whole",
    )(parts, factor)


def exchange(parts):
    return lax.all_to_all(parts, "ctx", split_axis=0, concat_axis=0, tiled=True)


def scatter(parts, reach):
    ids = range(2 * CHIPS)
    return [lax.ppermute(part, "ctx", [(i, i ^ d) for i in ids]) if d else part for part, d in zip(parts, reach)]


SWAP = [(i, i ^ 1) for i in range(8)]
SIDE = [(i, i ^ 2) for i in range(8)]
MIDDLE = [(2, 4), (3, 5), (4, 2), (5, 3)]
OUT = [(2, 0), (3, 1), (4, 6), (5, 7)]
INNER_SWAP, END_SWAP = SWAP[2:6], SWAP[:2] + SWAP[6:]


def to(x, pairs):
    return lax.ppermute(x, "ctx", pairs)


def lane_body(grad_out, proj_out, query, key_in, value_in, filters):
    seq = filters.shape[1]
    groups = seq // key_in.shape[0]
    firsts, fwd, inv, lasts = tables(seq)
    tie = lax.optimization_barrier
    ctx = lax.axis_index("ctx")
    place = jnp.stack([ctx // 2, ctx % 2, lax.axis_index("mp"), ctx]).astype(jnp.int32)
    index = ctx.astype(jnp.int32)[None]

    def across(x, d):
        return lax.ppermute(x, "mp", [(i, i ^ d) for i in range(4)])

    side, middle = to(proj_out, SIDE), to(proj_out, MIDDLE)
    x1, x2 = across(grad_out, 1), across(grad_out, 2)
    gated = exchange(gate(key_in, value_in, groups))
    spec = filter_spectrum(filters, (firsts[-1], fwd))
    side, middle, spec = tie((side, middle, spec))

    crossed, sent_out = to(side, MIDDLE), to(middle, OUT)
    ws = [side, to(side, SWAP), middle, to(middle, INNER_SWAP)]
    x3, own, *_ = tie((grad_out, proj_out, x1, x2, ws[1], ws[3]))
    ws = [own, to(own, SWAP)] + ws
    xs = [grad_out, x1, x2, across(x3, 3)]
    (conv,), gated_spec = convolve(jnp.full_like(index, 2 * CHIPS), [gated], spec, (firsts, fwd, inv, lasts), False, True)
    crossed, _ = tie((crossed, conv))

    last = to(crossed, OUT)
    total = terms(place, xs, ws)
    conv, _ = tie((conv, total))
    conv = exchange(conv)
    ws = [crossed, to(crossed, INNER_SWAP), sent_out, to(sent_out, END_SWAP)]
    last, _ = tie((last, total))
    ws += [last, to(last, END_SWAP)]
    grad_mix, scaled = mix_late(place, xs, ws, total, query)
    scaled = scatter(scaled, OUTWARD)
    *scaled, conv = tie((*scaled, conv))
    back, scaled_spec = convolve(index, scaled, spec, (firsts, fwd, inv, lasts), True, False)
    back = scatter(back, HOMEWARD)
    filter_grad = filter_gradient(scaled_spec, gated_spec, (None, fwd, inv, lasts[-1]), 1.0 / math.sqrt(seq))
    grad_query = finish_whole(conv, grad_mix)
    grad_key, grad_value = finish(place, back, value_in, key_in)
    return (grad_query, grad_key, grad_value, filter_grad)


def body(grad_out, proj_out, query, key_in, value_in, filters):
    rows, cols = key_in.shape
    lanes, seq = filters.shape
    fits = (
        lax.axis_size("ctx") == 2 * CHIPS
        and lax.axis_size("mp") == 4
        and lanes == LANES
        and rows % (16 * FAST) == 0
        and cols == 2 * CHIPS * LANES
        and seq == 2 * CHIPS * rows
        and seq == FAST * LANES
        and grad_out.shape[1] == 2 * proj_out.shape[1]
    )
    args = (grad_out, proj_out, query, key_in, value_in, filters)
    return lane_body(*args) if fits else general_body(*args)


def solution(mesh):
    return jax.shard_map(
        body,
        mesh=mesh,
        in_specs=(
            P("ctx", "mp"),
            P("mp", "ctx"),
            P("ctx", "mp"),
            P("ctx", "mp"),
            P("ctx", "mp"),
            P(("mp", "ctx"), None),
        ),
        out_specs=(P("ctx", "mp"), P("ctx", "mp"), P("ctx", "mp"), P(("mp", "ctx"), None)),
        check_vma=False,
    )
```

```python
import functools
import math

import jax
import jax.numpy as jnp
import ml_dtypes
import numpy as np
from jax import lax
from jax.experimental import pallas as pl
from jax.experimental.pallas import tpu as pltpu
from jax.sharding import PartitionSpec as P


def phase_table(rows_n, cols_n, modulus):
    prod_idx = (
        jnp.arange(rows_n, dtype=jnp.int32)[:, None]
        * jnp.arange(cols_n, dtype=jnp.int32)[None, :]
        % modulus
    )
    angles = prod_idx.astype(jnp.float32) * (2.0 * math.pi / modulus)
    return (jnp.cos(angles), jnp.sin(angles))


def make_tables(length_all):
    size_second = min(128, length_all)
    size_first = length_all // size_second
    cos_first, sin_first = phase_table(size_first, size_first, size_first)
    twist_cos, twist_sin = phase_table(size_first, size_second, length_all)
    cos_second, sin_second = phase_table(size_second, size_second, size_second)
    return (cos_first, sin_first, twist_cos, twist_sin, cos_second, sin_second)


def contract(form, left, right):
    return jnp.einsum(form, left, right, precision=lax.Precision.HIGHEST)


def forward_real(signal, tables):
    cos_first, sin_first, twist_cos, twist_sin, cos_second, sin_second = tables
    part_re = contract("kn,cnm->ckm", cos_first, signal)
    part_im = -contract("kn,cnm->ckm", sin_first, signal)
    turned_re = part_re * twist_cos + part_im * twist_sin
    turned_im = part_im * twist_cos - part_re * twist_sin
    spec_re = contract("ckm,mj->ckj", turned_re, cos_second) + contract(
        "ckm,mj->ckj", turned_im, sin_second
    )
    spec_im = contract("ckm,mj->ckj", turned_im, cos_second) - contract(
        "ckm,mj->ckj", turned_re, sin_second
    )
    return (spec_re, spec_im)


def inverse_real(spec_re, spec_im, tables):
    cos_first, sin_first, twist_cos, twist_sin, cos_second, sin_second = tables
    back_re = contract("ckj,jm->ckm", spec_re, cos_second) - contract(
        "ckj,jm->ckm", spec_im, sin_second
    )
    back_im = contract("ckj,jm->ckm", spec_re, sin_second) + contract(
        "ckj,jm->ckm", spec_im, cos_second
    )
    twist_re = back_re * twist_cos - back_im * twist_sin
    twist_im = back_re * twist_sin + back_im * twist_cos
    return contract("nk,ckm->cnm", cos_first, twist_re) - contract(
        "nk,ckm->cnm", sin_first, twist_im
    )


def long_filter_grads(gated, scaled, kernel):
    channels, seq_len = kernel.shape
    length_all = 2 * seq_len
    tables = make_tables(length_all)
    spec_shape = (channels, tables[0].shape[0], tables[4].shape[0])

    def padded(values):
        wide = jnp.concatenate(
            [values.astype(jnp.float32), jnp.zeros((channels, seq_len), jnp.float32)], axis=1
        )
        return wide.reshape(spec_shape)

    def restore(spec_re, spec_im):
        return (
            inverse_real(spec_re, spec_im, tables).reshape(channels, length_all)[:, :seq_len]
            / length_all
        )

    gated_re, gated_im = forward_real(padded(gated), tables)
    scaled_re, scaled_im = forward_real(padded(scaled), tables)
    kernel_re, kernel_im = forward_real(padded(kernel), tables)
    conv_out = restore(
        kernel_re * gated_re - kernel_im * gated_im, kernel_re * gated_im + kernel_im * gated_re
    )
    grad_gated = restore(
        scaled_re * kernel_re + scaled_im * kernel_im, scaled_im * kernel_re - scaled_re * kernel_im
    )
    grad_kernel = restore(
        scaled_re * gated_re + scaled_im * gated_im, scaled_im * gated_re - scaled_re * gated_im
    )
    filter_grad = grad_kernel / math.sqrt(seq_len)
    return (conv_out.astype(jnp.bfloat16), grad_gated.astype(jnp.bfloat16), filter_grad)


def product(left, right):
    return (left.astype(jnp.float32) * right.astype(jnp.float32)).astype(jnp.bfloat16)


def general_body(grad_out, proj_out, query, key_in, value_in, filters):
    weight_rows = lax.all_gather(proj_out, "ctx", axis=1, tiled=True)
    grad_mix = lax.dot_general(
        lax.all_gather(grad_out, "mp", axis=1, tiled=True),
        weight_rows,
        (((1,), (1,)), ((), ())),
        preferred_element_type=jnp.float32,
    ).astype(jnp.bfloat16)
    gated = product(key_in, value_in)
    scaled = product(grad_mix, query)
    chan_gated, chan_scaled = (
        lax.all_to_all(gated.T, "ctx", split_axis=0, concat_axis=1, tiled=True),
        lax.all_to_all(scaled.T, "ctx", split_axis=0, concat_axis=1, tiled=True),
    )
    conv_out, grad_gated, filter_grad = long_filter_grads(chan_gated, chan_scaled, filters)
    back_grad, back_conv = (
        lax.all_to_all(grad_gated, "ctx", split_axis=1, concat_axis=0, tiled=True),
        lax.all_to_all(conv_out, "ctx", split_axis=1, concat_axis=0, tiled=True),
    )
    grad_query = product(grad_mix, back_conv.T)
    grad_key = product(back_grad.T, value_in)
    grad_value = product(back_grad.T, key_in)
    return (grad_query, grad_key, grad_value, filter_grad)


FAST = 32
SLOT = 2 * FAST
PAIR = 2 * SLOT
STEP = SLOT + 8
GAP = FAST + 8
LANES = 128
CHIPS = 4
OUTWARD = (6, 4, 2, 7, 5, 3, 1, 0)
HOMEWARD = (6, 2, 3, 7, 4, 5, 1, 0)
F32, BF16 = jnp.float32, jnp.bfloat16
PARAMS = pltpu.CompilerParams(vmem_limit_bytes=63 * 2**20)
SMALL = pltpu.CompilerParams(vmem_limit_bytes=52 * 2**20)
VM = pl.BlockSpec(memory_space=pltpu.VMEM)
ANY = pl.BlockSpec(memory_space=pl.ANY)
HBM = pl.BlockSpec(memory_space=pltpu.HBM)
U1, U2 = 32, 64


def sds(shape, dtype):
    return jax.ShapeDtypeStruct(shape, dtype)


def cost(flops, moved):
    return pl.CostEstimate(flops=flops // 10**6, bytes_accessed=moved // 10**3, transcendentals=0)


def tables(seq):
    size = 2 * seq
    slow = size // FAST
    half = slow // 2
    s = np.arange(half)
    angle = 2 * np.pi * ((s[:, None] * s[None, :]) % slow) / slow
    first = np.concatenate([np.cos(angle), -np.sin(angle)], 0)
    first[half] = 1.0 - 2.0 * (s % 2)
    weight = np.full((2 * half, 1), 2.0)
    weight[0] = weight[half] = 1.0
    last = (first * weight).T / size
    a = np.arange(FAST)
    k = np.arange(half + 1)[:, None] + slow * a[None, :]
    turn = 2 * np.pi * ((k[:, :, None] * a[None, None, :]) % size) / size
    c, d = np.cos(turn), np.sin(turn)
    fwd = np.concatenate([np.concatenate([c, d], 2), np.concatenate([-d, c], 2)], 1)
    inv = fwd.transpose(0, 2, 1).copy()
    fwd[0, :, FAST:] = 0.0
    inv[0, FAST:] = 0.0

    def paired(blocks):
        out = np.zeros((half // 2 + 1, SLOT, PAIR))
        out[:-1, :, :SLOT] = blocks[0:half:2]
        out[:-1, :, SLOT:] = blocks[1:half:2]
        return out

    fwd, inv, edge_fwd, edge_inv = paired(fwd), paired(inv), fwd[half], inv[half]
    fwd[-1, :, FAST:SLOT] = edge_fwd[:, :FAST]
    inv[-1, FAST:, :SLOT] = edge_inv[:FAST]
    blocks = np.arange(half).reshape(2 * CHIPS, -1)

    def orders(reach):
        return [np.concatenate([blocks[c ^ d] for d in reach]) for c in range(2 * CHIPS)] + [np.arange(half)]

    firsts = np.stack([first[:, o] for o in orders(OUTWARD)])
    lasts = np.stack([last[o] for o in orders(HOMEWARD)])
    return [jnp.asarray(t.astype(ml_dtypes.bfloat16)) for t in (firsts, fwd, inv, lasts)]


def dot(left, right):
    return jnp.dot(left, right, preferred_element_type=F32)


def pair_dot(pair, rows):
    low = lax.broadcasted_iota(jnp.int32, pair.shape, 1) < SLOT
    zero = jnp.zeros_like(pair)
    return dot(jnp.concatenate([jnp.where(low, pair, zero), jnp.where(low, zero, pair)], 0), rows)


def loop(count, unroll, step):
    def some(i, carry):
        for u in range(unroll):
            step(i * unroll + u)
        return carry

    lax.fori_loop(0, count // unroll, some, 0)


def span(start, size):
    return pl.ds(pl.multiple_of(start * size, size), size)


def slots(ref, p):
    return [ref.at[pl.ds(pl.multiple_of(p * 2 * STEP + i * STEP, 8), SLOT), :] for i in range(2)]


def read_slots(ref, p):
    return jnp.concatenate([rows[...] for rows in slots(ref, p)], 0).astype(BF16)


def write_slots(ref, p, value):
    for i, rows in enumerate(slots(ref, p)):
        rows[...] = value[i * SLOT : (i + 1) * SLOT]


def gapped(ref, index, count):
    return [ref.at[pl.ds(pl.multiple_of((index * count + i) * GAP, 8), FAST), :] for i in range(count)]


def read_gapped(ref, index, count):
    return jnp.concatenate([rows[...] for rows in gapped(ref, index, count)], 0)


def write_gapped(ref, index, value):
    for i, rows in enumerate(gapped(ref, index, value.shape[0] // FAST)):
        rows[...] = value[i * FAST : (i + 1) * FAST]


def spread(signal, first_ref, mid_ref):
    half = first_ref.shape[1]

    def step(a):
        out = dot(first_ref[...], signal(a))
        mid_ref[pl.ds(a, half, stride=STEP), :] = out[:half]
        mid_ref[pl.ds(FAST + a, half, stride=STEP), :] = out[half:]

    loop(FAST, U1, step)


def collect(last_ref, back_ref, emit):
    half = last_ref.shape[0]

    def step(a):
        re = back_ref[pl.ds(a, half, stride=STEP), :]
        im = back_ref[pl.ds(FAST + a, half, stride=STEP), :]
        emit(a, dot(last_ref[...], jnp.concatenate([re, im], 0).astype(BF16)))

    loop(FAST, U1, step)


def times(x, y, conjugate):
    x, y = x.astype(F32), y.astype(F32)
    parts = []
    for i in range(0, x.shape[0], SLOT):
        xr, xi, yr, yi = (v[i + j : i + j + FAST] for v in (x, y) for j in (0, FAST))
        if conjugate:
            parts += [xr * yr + xi * yi, xi * yr - xr * yi]
        else:
            parts += [xr * yr - xi * yi, xr * yi + xi * yr]
    return jnp.concatenate(parts, 0).astype(BF16)


def filter_kernel(h_ref, first_ref, fwd_ref, spec_ref, time_ref, mid_ref):
    half = first_ref.shape[1]
    seq = h_ref.shape[1]

    def turn(i):
        write_gapped(time_ref, i, h_ref[:, span(i, LANES)].T)

    loop(seq // LANES, 8, turn)
    spread(lambda a: time_ref[pl.ds(a, half, stride=GAP), :].astype(BF16), first_ref, mid_ref)

    def step(p):
        spec_ref[span(p, PAIR), :] = pair_dot(fwd_ref[p], read_slots(mid_ref, p)).astype(BF16)

    loop(half // 2, U2, step)
    spec_ref[span(half // 2, PAIR), :] = pair_dot(fwd_ref[half // 2], read_slots(mid_ref, 0)).astype(BF16)


def convolve_kernel(conjugate, count, place_ref, *refs):
    x_refs, (h_any, first_ref, fwd_any, inv_any, last_ref) = refs[:count], refs[count : count + 5]
    outs, (spec_any, h_ref, fwd_ref, inv_ref, spec_ref, mid_ref, back_ref, sem) = refs[count + 5 : -8], refs[-8:]
    first_ref, last_ref = first_ref.at[0], last_ref.at[0]
    half = first_ref.shape[1]
    loads = [
        pltpu.make_async_copy(source, target, sem.at[i])
        for i, (source, target) in enumerate(((fwd_any, fwd_ref), (h_any, h_ref), (inv_any, inv_ref)))
    ]
    for load in loads:
        load.start()
    if count == 1:
        spread(lambda a: x_refs[0][:, a].reshape(half, LANES), first_ref, mid_ref)
    else:
        spread(lambda a: jnp.concatenate([x_ref[a] for x_ref in x_refs], 0), first_ref, mid_ref)
    for load in loads:
        load.wait()

    def step(p):
        x = pair_dot(fwd_ref[p], read_slots(mid_ref, p))
        spec_ref[span(p, PAIR), :] = x.astype(BF16)
        write_slots(back_ref, p, pair_dot(inv_ref[p], times(x, h_ref[span(p, PAIR), :], conjugate)))

    loop(half // 2, U2, step)
    tail = span(half // 2, PAIR)
    x = pair_dot(fwd_ref[half // 2], read_slots(mid_ref, 0))
    spec_ref[tail, :] = x.astype(BF16)
    store = pltpu.make_async_copy(spec_ref, spec_any, sem.at[3])
    store.start()
    back_ref[:SLOT, :] += pair_dot(inv_ref[half // 2], times(x, h_ref[tail, :], conjugate))[:SLOT]
    if len(outs) == 1:

        def emit(a, rows):
            outs[0][:, a] = rows.reshape(outs[0].shape[0], -1, LANES).astype(BF16)

        collect(last_ref, back_ref, emit)
    else:
        per = half // len(outs)

        def emit(a, rows):
            for i, out_ref in enumerate(outs):
                out_ref[a] = rows[i * per : (i + 1) * per].astype(BF16)

        collect(last_ref, back_ref, emit)
    store.wait()


def gradient_kernel(scale, s_ref, g_ref, inv_ref, last_ref, out_ref, time_ref, back_ref):
    half = last_ref.shape[0]
    seq = out_ref.shape[1]

    def step(p):
        rows = span(p, PAIR)
        write_slots(back_ref, p, pair_dot(inv_ref[p], times(s_ref[rows, :], g_ref[rows, :], True)))

    loop(half // 2, U2, step)
    tail = span(half // 2, PAIR)
    back_ref[:SLOT, :] += pair_dot(inv_ref[half // 2], times(s_ref[tail, :], g_ref[tail, :], True))[:SLOT]

    def emit(a, rows):
        time_ref[pl.ds(a, half, stride=GAP), :] = rows * scale

    collect(last_ref, back_ref, emit)

    def turn(i):
        out_ref[:, span(i, LANES)] = read_gapped(time_ref, i, LANES // FAST).T

    loop(seq // LANES, 8, turn)


def filter_spectrum(h, tabs):
    first, fwd = tabs[:2]
    seq = h.shape[1]
    return pl.pallas_call(
        filter_kernel,
        out_shape=sds((2 * seq + PAIR, LANES), BF16),
        in_specs=[VM] * 3,
        out_specs=VM,
        scratch_shapes=[pltpu.VMEM((seq // FAST * GAP, LANES), F32), pltpu.VMEM((seq // FAST * STEP, LANES), F32)],
        compiler_params=PARAMS,
        cost_estimate=cost(10**9, 8 * 2**20),
        name="filter_spectrum",
    )(h, first, fwd)


def convolve(index, parts, spec, tabs, conjugate, whole):
    first, fwd, inv, last = tabs
    count = len(parts)
    groups = 2 * CHIPS
    half = last.shape[1]

    def own(table):
        return pl.BlockSpec((1,) + table.shape[1:], lambda i, index: (index[0], 0, 0))

    outs = (sds((FAST, half // groups, LANES), BF16),) * groups
    if whole:
        outs = (sds((groups, FAST, half // groups, LANES), BF16),)
    big = pltpu.VMEM((half * STEP, LANES), F32)
    *out, spec = pl.pallas_call(
        functools.partial(convolve_kernel, conjugate, count),
        out_shape=outs + (sds(spec.shape, BF16),),
        grid_spec=pltpu.PrefetchScalarGridSpec(
            num_scalar_prefetch=1,
            grid=(1,),
            in_specs=[VM] * count + [HBM, own(first), HBM, HBM, own(last)],
            out_specs=(VM,) * len(outs) + (HBM,),
            scratch_shapes=[
                pltpu.VMEM(spec.shape, BF16),
                pltpu.VMEM(fwd.shape, BF16),
                pltpu.VMEM(fwd.shape, BF16),
                pltpu.VMEM(spec.shape, BF16),
                big,
                big,
                pltpu.SemaphoreType.DMA((4,)),
            ],
        ),
        compiler_params=SMALL,
        cost_estimate=cost(2 * 10**9, 14 * 2**20),
        name="convolve",
    )(index, *parts, spec, *tabs)
    return out, spec


def filter_gradient(scaled_spec, gated_spec, tabs, scale):
    inv, last = tabs[2:]
    seq = (scaled_spec.shape[0] - PAIR) // 2
    return pl.pallas_call(
        functools.partial(gradient_kernel, scale),
        out_shape=sds((LANES, seq), F32),
        in_specs=[VM] * 4,
        out_specs=VM,
        scratch_shapes=[pltpu.VMEM((seq // FAST * GAP, LANES), F32), pltpu.VMEM((seq // FAST * STEP, LANES), F32)],
        compiler_params=PARAMS,
        cost_estimate=cost(10**9, 12 * 2**20),
        name="filter_gradient",
    )(scaled_spec, gated_spec, inv, last)


def permuted(value, hold_ref, emit):
    write_gapped(hold_ref, 0, value)
    per = value.shape[0] // FAST
    for a in range(FAST):
        emit(a, hold_ref[pl.ds(a, per, stride=GAP), :].astype(BF16))


def gate_kernel(key_ref, value_ref, out_ref, hold_ref):
    product = key_ref[...].astype(F32) * value_ref[...].astype(F32)
    for g in range(BATCH):

        def emit(a, rows):
            out_ref[g, a] = rows

        permuted(product[:, g * LANES : (g + 1) * LANES], hold_ref, emit)


def gate(key_in, value_in, groups):
    rows, cols = key_in.shape
    block = pl.BlockSpec((rows, BATCH * LANES), lambda j: (0, j))
    return pl.pallas_call(
        gate_kernel,
        grid=(cols // (BATCH * LANES),),
        out_shape=sds((groups, FAST, rows // FAST, LANES), BF16),
        in_specs=[block, block],
        out_specs=pl.BlockSpec((BATCH, FAST, rows // FAST, LANES), lambda j: (j, 0, 0, 0)),
        scratch_shapes=[pltpu.VMEM((rows // FAST * GAP, LANES), F32)],
        compiler_params=PARAMS,
        cost_estimate=cost(10**6, 3 * 2**20),
        name="gate",
    )(key_in, value_in)


WIDE = 256
BATCH = 4


def pieces_of(x_ref, piece, lane, depth):
    return x_ref[piece, :, pl.ds(pl.multiple_of(lane * depth, depth), depth)]


def against(left, w_ref):
    return lax.dot_general(left, w_ref[...], (((1,), (1,)), ((), ())), preferred_element_type=F32)


def is_end(place):
    return (place[0] == 0) | (place[0] == CHIPS - 1)


def terms_kernel(place_ref, *refs):
    xs, ws, (sum_ref, x_ref, sem) = refs[:4], refs[4:10], refs[-3:]
    here, core, mine = place_ref[0], place_ref[1], place_ref[2]
    depth = ws[0].shape[1]
    inside = jnp.logical_not(is_end(place_ref))

    @pl.when(pl.program_id(0) == 0)
    def _():
        for start in (True, False):
            for i in range(4):
                apart = mine ^ i ^ here

                @pl.when((apart < 2) | (inside & (apart == CHIPS - 1)))
                def _():
                    copy = pltpu.make_async_copy(xs[i], x_ref.at[mine ^ i], sem.at[i])
                    copy.start() if start else copy.wait()

    def part(piece, near_ref, swap_ref):
        one = against(pieces_of(x_ref, piece, core, depth), near_ref)
        return one + against(pieces_of(x_ref, piece, 1 - core, depth), swap_ref)

    total = part(here, ws[0], ws[1]) + part(here ^ 1, ws[2], ws[3])

    @pl.when(inside)
    def _():
        sum_ref[...] = total + part(CHIPS - 1 - here, ws[4], ws[5])

    @pl.when(is_end(place_ref))
    def _():
        sum_ref[...] = total


def always(j, place):
    return (j, 0)


def inside_only(j, place):
    return (jnp.where(is_end(place), 0, j), 0)


def terms(place, xs, ws):
    rows, piece = xs[0].shape
    cols, depth = ws[0].shape
    maps = [always] * 4 + [inside_only] * 2
    return pl.pallas_call(
        terms_kernel,
        out_shape=sds((rows, cols), F32),
        grid_spec=pltpu.PrefetchScalarGridSpec(
            num_scalar_prefetch=1,
            grid=(cols // WIDE,),
            in_specs=[ANY] * 4 + [pl.BlockSpec((WIDE, depth), m) for m in maps],
            out_specs=pl.BlockSpec((rows, WIDE), lambda j, place: (0, j)),
            scratch_shapes=[pltpu.VMEM((4, rows, piece), BF16), pltpu.SemaphoreType.DMA((4,))],
        ),
        compiler_params=PARAMS,
        cost_estimate=cost(2 * 10**9, 14 * 2**20),
        name="terms",
    )(place, *xs, *ws)


def late_kernel(place_ref, *refs):
    xs, ws, sum_ref, query_ref, mix_ref = refs[:4], refs[4:10], refs[10], refs[11], refs[12]
    outs, (hold_ref, x_ref, sem) = refs[13:-3], refs[-3:]
    here, core, mine = place_ref[0], place_ref[1], place_ref[2]
    two_ref, three_ref = x_ref.at[pl.ds(0, 1)], x_ref.at[pl.ds(1, 1)]

    ends = is_end(place_ref)

    def fetch(start, slot, piece, needed):
        for i in range(4):

            @pl.when((pl.program_id(0) == 0) & (mine ^ piece == i) & needed)
            def _():
                copy = pltpu.make_async_copy(xs[i], x_ref.at[slot], sem.at[slot])
                copy.start() if start else copy.wait()

    fetch(True, 0, here ^ 2, True)
    fetch(True, 1, CHIPS - 1 - here, ends)
    fetch(False, 0, here ^ 2, True)
    depth = ws[0].shape[1]
    per = sum_ref.shape[0] // FAST

    def part(piece_ref, near_ref, swap_ref):
        one = against(pieces_of(piece_ref, 0, core, depth), near_ref)
        return one + against(pieces_of(piece_ref, 0, 1 - core, depth), swap_ref)

    def give(total):
        mix = total.astype(BF16)
        mix_ref[...] = mix
        scaled = mix.astype(F32) * query_ref[...].astype(F32)
        for g in range(BATCH):
            write_gapped(hold_ref.at[g], 0, scaled[:, g * LANES : (g + 1) * LANES])

    @pl.when(ends)
    def _():
        total = sum_ref[...] + part(two_ref, ws[2], ws[3])
        fetch(False, 1, CHIPS - 1 - here, ends)
        give(total + part(three_ref, ws[4], ws[5]))

    @pl.when(jnp.logical_not(ends))
    def _():
        give(sum_ref[...] + part(two_ref, ws[0], ws[1]))

    for k in range(2 * CHIPS // BATCH):

        @pl.when(pl.program_id(0) == k)
        def _():
            for e in range(BATCH):
                for a in range(FAST):
                    outs[OUTWARD.index(BATCH * k + e)][a] = hold_ref[e ^ (place_ref[3] % BATCH), pl.ds(a, per, stride=GAP), :].astype(BF16)


def mix_late(place, xs, ws, total, query):
    rows, cols = query.shape
    depth = ws[0].shape[1]

    def block(j, place):
        return j ^ (place[3] // BATCH)

    def inner(j, place):
        return (jnp.where(is_end(place), 0, block(j, place)), 0)

    def outer(j, place):
        return (jnp.where(is_end(place), block(j, place), 0), 0)

    wide = pl.BlockSpec((rows, BATCH * LANES), lambda j, place: (0, block(j, place)))
    part = pl.BlockSpec((FAST, rows // FAST, LANES), lambda j, place: (0, 0, 0))
    grad_mix, *scaled = pl.pallas_call(
        late_kernel,
        out_shape=(sds((rows, cols), BF16),) + (sds((FAST, rows // FAST, LANES), BF16),) * (2 * CHIPS),
        grid_spec=pltpu.PrefetchScalarGridSpec(
            num_scalar_prefetch=1,
            grid=(2 * CHIPS // BATCH,),
            in_specs=[ANY] * 4
            + [pl.BlockSpec((BATCH * LANES, depth), m) for m in (inner, inner, outer, outer, outer, outer)]
            + [wide, wide],
            out_specs=(wide,) + (part,) * (2 * CHIPS),
            scratch_shapes=[
                pltpu.VMEM((BATCH, rows // FAST * GAP, LANES), F32),
                pltpu.VMEM((2,) + xs[0].shape, BF16),
                pltpu.SemaphoreType.DMA((2,)),
            ],
        ),
        compiler_params=PARAMS,
        cost_estimate=cost(10**9, 8 * 2**20),
        name="mix_late",
    )(place, *xs, *ws, total, query)
    return grad_mix, scaled


def finish_kernel(count, place_ref, *refs):
    parts, factors, outs = refs[: 2 * CHIPS], refs[2 * CHIPS : 2 * CHIPS + count], refs[2 * CHIPS + count : -1]
    hold_ref = refs[-1]
    here = place_ref[3] % BATCH
    per = parts[0].shape[1]
    for k in range(2 * CHIPS // BATCH):

        @pl.when(pl.program_id(0) == k)
        def _():
            for e in range(BATCH):
                for a in range(FAST):
                    hold_ref[e ^ here, pl.ds(a, per, stride=GAP), :] = parts[HOMEWARD.index(BATCH * k + e)][a].astype(F32)

    for g in range(BATCH):
        lanes = pl.ds(g * LANES, LANES)
        value = read_gapped(hold_ref.at[g], 0, per)
        for factor_ref, out_ref in zip(factors, outs):
            out_ref[:, lanes] = (value * factor_ref[:, lanes].astype(F32)).astype(BF16)


def finish(place, parts, *factors):
    rows, cols = factors[0].shape
    count = len(factors)
    block = pl.BlockSpec((rows, BATCH * LANES), lambda j, place: (0, j ^ (place[3] // BATCH)))
    part = pl.BlockSpec(parts[0].shape, lambda j, place: (0, 0, 0))
    return pl.pallas_call(
        functools.partial(finish_kernel, count),
        out_shape=(sds((rows, cols), BF16),) * count,
        grid_spec=pltpu.PrefetchScalarGridSpec(
            num_scalar_prefetch=1,
            grid=(2 * CHIPS // BATCH,),
            in_specs=[part] * (2 * CHIPS) + [block] * count,
            out_specs=(block,) * count,
            scratch_shapes=[pltpu.VMEM((BATCH, rows // FAST * GAP, LANES), F32)],
        ),
        compiler_params=PARAMS,
        cost_estimate=cost(10**6, (1 + 2 * count) * 2**20),
        name="finish",
    )(place, *parts, *factors)


def finish_whole_kernel(part_ref, factor_ref, out_ref, hold_ref):
    per = part_ref.shape[2]
    for g in range(2):
        for a in range(FAST):
            hold_ref[pl.ds(a, per, stride=GAP), :] = part_ref[g, a].astype(F32)
        lanes = pl.ds(g * LANES, LANES)
        out_ref[:, lanes] = (read_gapped(hold_ref, 0, per) * factor_ref[:, lanes].astype(F32)).astype(BF16)


def finish_whole(parts, factor):
    rows, cols = factor.shape
    wide = pl.BlockSpec((rows, WIDE), lambda j: (0, j))
    part = pl.BlockSpec((2,) + parts.shape[1:], lambda j: (j, 0, 0, 0))
    return pl.pallas_call(
        finish_whole_kernel,
        out_shape=sds((rows, cols), BF16),
        grid=(CHIPS,),
        in_specs=[part, wide],
        out_specs=wide,
        scratch_shapes=[pltpu.VMEM((rows // FAST * GAP, LANES), F32)],
        compiler_params=PARAMS,
        cost_estimate=cost(10**6, 3 * 2**20),
        name="finish_whole",
    )(parts, factor)


def exchange(parts):
    return lax.all_to_all(parts, "ctx", split_axis=0, concat_axis=0, tiled=True)


def scatter(parts, reach):
    ids = range(2 * CHIPS)
    return [lax.ppermute(part, "ctx", [(i, i ^ d) for i in ids]) if d else part for part, d in zip(parts, reach)]


SWAP = [(i, i ^ 1) for i in range(8)]
SIDE = [(i, i ^ 2) for i in range(8)]
MIDDLE = [(2, 4), (3, 5), (4, 2), (5, 3)]
OUT = [(2, 0), (3, 1), (4, 6), (5, 7)]
INNER_SWAP, END_SWAP = SWAP[2:6], SWAP[:2] + SWAP[6:]


def to(x, pairs):
    return lax.ppermute(x, "ctx", pairs)


def lane_body(grad_out, proj_out, query, key_in, value_in, filters):
    seq = filters.shape[1]
    groups = seq // key_in.shape[0]
    firsts, fwd, inv, lasts = tables(seq)
    tie = lax.optimization_barrier
    ctx = lax.axis_index("ctx")
    place = jnp.stack([ctx // 2, ctx % 2, lax.axis_index("mp"), ctx]).astype(jnp.int32)
    index = ctx.astype(jnp.int32)[None]

    def across(x, d):
        return lax.ppermute(x, "mp", [(i, i ^ d) for i in range(4)])

    side, middle = to(proj_out, SIDE), to(proj_out, MIDDLE)
    x1, x2 = across(grad_out, 1), across(grad_out, 2)
    gated = exchange(gate(key_in, value_in, groups))
    spec = filter_spectrum(filters, (firsts[-1], fwd))
    side, middle, spec = tie((side, middle, spec))

    crossed, sent_out = to(side, MIDDLE), to(middle, OUT)
    ws = [side, to(side, SWAP), middle, to(middle, INNER_SWAP)]
    x3, own, *_ = tie((grad_out, proj_out, x1, x2, ws[1], ws[3]))
    ws = [own, to(own, SWAP)] + ws
    xs = [grad_out, x1, x2, across(x3, 3)]
    (conv,), gated_spec = convolve(jnp.full_like(index, 2 * CHIPS), [gated], spec, (firsts, fwd, inv, lasts), False, True)
    crossed, _ = tie((crossed, conv))

    last = to(crossed, OUT)
    total = terms(place, xs, ws)
    conv, _ = tie((conv, total))
    conv = exchange(conv)
    ws = [crossed, to(crossed, INNER_SWAP), sent_out, to(sent_out, END_SWAP)]
    last, _ = tie((last, total))
    ws += [last, to(last, END_SWAP)]
    grad_mix, scaled = mix_late(place, xs, ws, total, query)
    scaled = scatter(scaled, OUTWARD)
    *scaled, conv = tie((*scaled, conv))
    back, scaled_spec = convolve(index, scaled, spec, (firsts, fwd, inv, lasts), True, False)
    back = scatter(back, HOMEWARD)
    filter_grad = filter_gradient(scaled_spec, gated_spec, (None, fwd, inv, lasts[-1]), 1.0 / math.sqrt(seq))
    grad_query = finish_whole(conv, grad_mix)
    grad_key, grad_value = finish(place, back, value_in, key_in)
    return (grad_query, grad_key, grad_value, filter_grad)


def body(grad_out, proj_out, query, key_in, value_in, filters):
    rows, cols = key_in.shape
    lanes, seq = filters.shape
    fits = (
        lax.axis_size("ctx") == 2 * CHIPS
        and lax.axis_size("mp") == 4
        and lanes == LANES
        and rows % (16 * FAST) == 0
        and cols == 2 * CHIPS * LANES
        and seq == 2 * CHIPS * rows
        and seq == FAST * LANES
        and grad_out.shape[1] == 2 * proj_out.shape[1]
    )
    args = (grad_out, proj_out, query, key_in, value_in, filters)
    return lane_body(*args) if fits else general_body(*args)


def solution(mesh):
    return jax.shard_map(
        body,
        mesh=mesh,
        in_specs=(
            P("ctx", "mp"),
            P("mp", "ctx"),
            P("ctx", "mp"),
            P("ctx", "mp"),
            P("ctx", "mp"),
            P(("mp", "ctx"), None),
        ),
        out_specs=(P("ctx", "mp"), P("ctx", "mp"), P("ctx", "mp"), P(("mp", "ctx"), None)),
        check_vma=False,
    )
```
